256 devices in a mesh: row: 8 (over y, core), col: 32 (over x, z).
Axes of the slice: x: 4, y: 4, z: 8, core: 2. Of those that a mesh axis runs over, the one named last changes fastest.
Arguments:
- charges: float32 [262144], P(('row', 'col')), may hold values from -6 to 6
- anchors: int32 [3, 262144], P(None, ('row', 'col')), may hold values from 0 to 255, as said below
- stencil_weights: float32 [64, 262144], P(None, ('row', 'col')), may hold values from -0.75 to 0.75
- kernel_spectrum: float32 [256, 256, 256], P('row', 'col'), may hold values from 1 to 200, as said below
- near_count: int32 [256], P(('row', 'col')), may hold values from 1 to 32, 4096 in all
- near_target: int32 [8192], P(('row', 'col')), may hold values from 0 to 7
- near_source: int32 [8192], P(('row', 'col')), may hold values from 0 to 71
- near_tiles: float32 [8192, 128, 128], P(('row', 'col')), may hold values from -0.5 to 0.5
Outputs:
- potential: float32 [262144], P(('row', 'col'))
The draws below stay inside these ranges and needn't reach their ends.
Inputs may be any that keep to these rules, and one draw needn't show every extreme that they name: With p = t // 1024, r = p // 32, c = p % 32: anchors[0, t] = (r * 32 - 1 + i) mod 256 for some i in 0..30, anchors[1, t] = (c * 8 - 1 + j) mod 256 for some j in 0..6, anchors[2, t] any cell. kernel_spectrum[b, c, a] is unchanged when any one index n is replaced by (256 - n) mod 256, and positive.
All inputs are finite; a program needn't handle non-finite values. No bound on the sum of `near_count` on one device may be relied on, other than what follows from the above.
Results may differ from the reference program's by a relative error of at most 0.00005.
Values sent between devices are 32-bit elements; how exact they have to be, the bound alone decides.
No kernel may reach another device: no remote copies, remote signals or barrier semaphores. Data moves between devices by JAX's collectives and lax.ppermute only.
A program may use at most 64 MiB of HBM per device.

```python
import math
import jax
import jax.numpy as jnp
import numpy as np
from jax import lax

G = 256
PATCH_ROWS = 8
PATCH_COLS = 32
PATCHES = 256
CELLS_A = 32
CELLS_B = 8
TRI_DEV = 1024
TRI = 262144
BLK = 128
BLOCKS = 8
NP_DEV = 32
SLOTS = 8192


def draw_anchors(key, part):
    key = jax.random.fold_in(key, 11)
    first_key, second_key, third_key = jax.random.split(key, 3)
    triangle = jnp.arange(TRI, dtype=jnp.int32)
    patch = triangle // TRI_DEV
    patch_row = patch // PATCH_COLS
    patch_col = patch % PATCH_COLS
    first = (patch_row * CELLS_A - 1 + jax.random.randint(first_key, (TRI,), 0, CELLS_A - 1)) % G
    second = (patch_col * CELLS_B - 1 + jax.random.randint(second_key, (TRI,), 0, CELLS_B - 1)) % G
    third = jax.random.randint(third_key, (TRI,), 0, G)
    return jnp.stack([first, second, third]).astype(jnp.int32)


def draw_kernel_spectrum(key, part):
    key = jax.random.fold_in(key, 23)
    halves = G // 2 + 1
    rough = jax.random.uniform(key, (halves, halves, halves), jnp.float32)
    steps = jnp.arange(G, dtype=jnp.int32)
    folded = jnp.minimum(steps, G - steps)
    along_first = folded[None, None, :]
    along_second = folded[:, None, None]
    along_third = folded[None, :, None]
    picked = rough[along_first, along_second, along_third]
    radius = (along_first * along_first + along_second * along_second + along_third * along_third).astype(jnp.float32)
    return 8.0 * (0.3 + 0.7 * picked) + 40.0 / (1.0 + radius / 4.0)


def plant(result, own_key, low, largest):
    index_at = [jax.random.randint(jax.random.fold_in(own_key, axis), (), 0, length) for axis, length in enumerate(result.shape)]
    longest = result.shape.index(max(result.shape))
    beside = index_at[:longest] + [(index_at[longest] + 1) % result.shape[longest]] + index_at[longest + 1:]
    return result.at[tuple(index_at)].set(low).at[tuple(beside)].set(largest)


def level_of(rng, extent, pieces, smallest, top_value):
    gain, own = 1.0, jax.random.fold_in(rng, 6)
    for dim, blocks in pieces:
        steps = jnp.exp(jax.random.uniform(jax.random.fold_in(own, dim), (blocks,), jnp.float32, smallest / len(pieces), top_value / len(pieces)))
        gain = gain * jnp.repeat(steps, extent[dim] // blocks).reshape([-1 if axis == dim else 1 for axis in range(len(extent))])
    return gain


def profile(number_of, total, limit, skew):
    portions = [(1 << 20) // math.isqrt(rank ** skew) + 1 for rank in range(2, number_of + 1)]
    surplus, given = total - limit - (number_of - 1), [1] * (number_of - 1)
    while surplus > 0:
        movable = [i for i in range(number_of - 1) if given[i] < limit]
        whole, left = sum([portions[i] for i in movable]), surplus
        for i in movable:
            addition = min(limit - given[i], max(1, left * portions[i] // whole), surplus)
            given[i] = given[i] + addition
            surplus = surplus - addition
    return np.array([limit] + given)


def uneven_parts(own_key, number_of, total, most, skew):
    if number_of == 2:
        one = jax.random.randint(own_key, (), max(1, total - most), min(most, total - 1) + 1)
        return jnp.stack([one, total - one])
    lengths = jnp.asarray(profile(number_of, total, most, skew), jnp.int32)
    twos = (number_of - 1) // 2
    donor, receiver = lengths[1:1 + 2 * twos:2], lengths[2:2 + 2 * twos:2]
    slack = jnp.minimum(donor - 1, most - receiver)
    shifted = jax.random.randint(jax.random.fold_in(own_key, 1), (twos,), 0, 1 << 20) % (slack + 1)
    lengths = lengths.at[1:1 + 2 * twos:2].set(donor - shifted).at[2:2 + 2 * twos:2].set(receiver + shifted)
    return lengths[jax.random.permutation(jax.random.fold_in(own_key, 2), number_of)]


def normal_values(rng, dims, scale, bound, pieces=(), kind=jnp.bfloat16):
    array = scale * jax.random.normal(rng, dims, jnp.float32)
    if pieces:
        array = array * level_of(rng, dims, pieces, -0.22, 0.18)
    return jnp.clip(array, -bound, bound).astype(kind)


def setup_inputs(seed: int = 0) -> dict:
    keys = jax.random.split(jax.random.key(seed), 9)
    charges = normal_values(keys[0], (TRI,), 1.0, 6.0, ((0, 256),), jnp.float32)
    anchors = draw_anchors(jax.random.fold_in(keys[8], 71), 0)
    stencil_weights = normal_values(keys[2], (64, TRI), 0.125, 0.75, ((1, 256),), jnp.float32)
    kernel_spectrum = draw_kernel_spectrum(jax.random.fold_in(keys[8], 71), 0)
    near_count = uneven_parts(keys[4], PATCHES, PATCHES * NP_DEV // 2, NP_DEV, 2).astype(jnp.int32)
    near_target = plant(jax.random.randint(keys[5], (SLOTS,), 0, BLOCKS), jax.random.fold_in(keys[5], 1), 0, BLOCKS - 1).astype(jnp.int32)
    near_source = plant(jax.random.randint(keys[6], (SLOTS,), 0, 9 * BLOCKS), jax.random.fold_in(keys[6], 1), 0, (9 * BLOCKS) - 1).astype(jnp.int32)
    near_tiles = normal_values(keys[7], (SLOTS, BLK, BLK), BLK ** -0.5, 0.5, ((0, 256),), jnp.float32)
    return {"charges": charges, "anchors": anchors, "stencil_weights": stencil_weights, "kernel_spectrum": kernel_spectrum, "near_count": near_count, "near_target": near_target, "near_source": near_source, "near_tiles": near_tiles}


def stencil_cells(anchors):
    offsets = jnp.arange(64, dtype=jnp.int32)
    first = (anchors[0][None, :] + (offsets // 16)[:, None]) % G
    second = (anchors[1][None, :] + ((offsets // 4) % 4)[:, None]) % G
    third = (anchors[2][None, :] + (offsets % 4)[:, None]) % G
    return ((first * G + second) * G + third).astype(jnp.int32)


def reference(charges, anchors, stencil_weights, kernel_spectrum, near_count, near_target, near_source, near_tiles):
    cells = stencil_cells(anchors).reshape(-1)
    deposits = (stencil_weights * charges[None, :]).reshape(-1)
    grid_charge = jnp.zeros((G * G * G,), jnp.float32).at[cells].add(deposits).reshape(G, G, G)
    spectrum = jnp.transpose(kernel_spectrum, (2, 0, 1))
    grid_potential = jnp.real(jnp.fft.ifftn(spectrum * jnp.fft.fftn(grid_charge))).astype(jnp.float32)
    sampled = grid_potential.reshape(-1)[cells].reshape(64, TRI)
    far = jnp.sum(stencil_weights * sampled, axis=0)
    patch = jnp.arange(PATCHES, dtype=jnp.int32)[:, None]
    patch_row = patch // PATCH_COLS
    patch_col = patch % PATCH_COLS
    sources = near_source.reshape(PATCHES, NP_DEV)
    neighbour = sources // BLOCKS
    source_block = sources % BLOCKS
    root = ((patch_row + neighbour // 3 - 1) % PATCH_ROWS) * PATCH_COLS + (patch_col + neighbour % 3 - 1) % PATCH_COLS
    starts = root * TRI_DEV + source_block * BLK
    lanes = jnp.arange(BLK, dtype=jnp.int32)
    gathered = charges[(starts[:, :, None] + lanes[None, None, :]).astype(jnp.int32)]
    tiles = near_tiles.reshape(PATCHES, NP_DEV, BLK, BLK)
    terms = jnp.einsum("psij,psj->psi", tiles, gathered, precision=lax.Precision.HIGHEST)
    live = jnp.arange(NP_DEV, dtype=jnp.int32)[None, :] < near_count[:, None]
    terms = jnp.where(live[:, :, None], terms, jnp.zeros_like(terms))
    targets = patch * TRI_DEV + near_target.reshape(PATCHES, NP_DEV) * BLK
    places = (targets[:, :, None] + lanes[None, None, :]).astype(jnp.int32).reshape(-1)
    near = jnp.zeros((TRI,), jnp.float32).at[places].add(terms.reshape(-1))
    return far + near
```

```python
import jax
import jax.numpy as jnp
import ml_dtypes
import numpy as np
from jax import lax
from jax.experimental import pallas as pl
from jax.experimental.pallas import tpu as pltpu
from jax.sharding import PartitionSpec as P

G = 256
ROWS = 8
COLS = 32
CELLS_A = 32
CELLS_B = 8
TRI = 1024
LINES_B = 10
MAIN = LINES_B * CELLS_A
LINES = 384
SPREAD = MAIN + 8 * LINES_B
LANES = 128
TILES = TRI // LANES
F32 = jnp.float32
BF16 = jnp.bfloat16
BOTH = ("row", "col")
PARAMS = pltpu.CompilerParams(vmem_limit_bytes=48 * 1024 * 1024)


def split_table(table):
    high = table.astype(np.float32).astype(ml_dtypes.bfloat16)
    low = (table - high.astype(np.float64)).astype(np.float32).astype(ml_dtypes.bfloat16)
    return np.stack([high, low])


def cas(first, second):
    angle = (np.outer(first, second) % G) * (2.0 * np.pi / G)
    return np.cos(angle) + np.sin(angle)


def tables():
    steps = np.arange(G)
    device = np.arange(ROWS * COLS)
    plane = CELLS_B * (device % COLS) + device // COLS
    along_a = (np.arange(G) - 1) % G
    order = np.arange(LINES_B * COLS)
    along_b = (CELLS_B * (order % COLS) - 1 + order // COLS) % G
    lines = cas(plane, steps)
    first = cas(along_a, steps)
    second = cas(steps, along_b)
    return split_table(lines), split_table(first), split_table(second), split_table(second.T)


def halves(value):
    high = value.astype(BF16)
    low = (value - high.astype(F32)).astype(BF16)
    return high, low


def dot(left, right, dims=((1,), (0,))):
    return lax.dot_general(left, right, (dims, ((), ())), preferred_element_type=F32)


def dot_split(left, right, dims=((1,), (0,))):
    left_high, left_low = left
    right_high, right_low = right
    cross = dot(left_high, right_low, dims) + dot(left_low, right_high, dims)
    return dot(left_high, right_high, dims) + cross


def extra_row(line):
    return MAIN + 2 * (line // 2) + 32 * (line % 2)


def onehot(anchors_ref):
    cells = lax.broadcasted_iota(jnp.int32, (G, TRI), 0)
    matched = cells == anchors_ref[2:3, :]
    return jnp.where(matched, 1.0, 0.0).astype(BF16)


def local_place(anchors_ref, at):
    first = (anchors_ref[0:1, at] - (lax.axis_index("row") * CELLS_A - 1)) & (G - 1)
    second = (anchors_ref[1:2, at] - (lax.axis_index("col") * CELLS_B - 1)) & (G - 1)
    first = jnp.broadcast_to(first, (8, LANES))
    second = jnp.broadcast_to(second, (8, LANES))
    relative = lax.broadcasted_iota(jnp.int32, (8, LANES), 0) - (first & 7)
    near_masks = [relative == i for i in range(4)]
    next_masks = [relative == i - 8 for i in range(1, 4)]
    group = first >> 3
    groups = [group == g for g in range(4)]
    bits = [(second & bit) != 0 for bit in (1, 2, 4)]
    return near_masks, next_masks, groups, bits


def two_rows(rows, near_masks, next_masks):
    near = jnp.zeros((8, LANES), F32)
    after = jnp.zeros((8, LANES), F32)
    for i in range(4):
        near = jnp.where(near_masks[i], rows[i], near)
    for i in range(1, 4):
        after = jnp.where(next_masks[i - 1], rows[i], after)
    return near, after


def deposit_kernel(charges_ref, anchors_ref, weights_ref, table_ref, out_ref, scaled, spread, lines):
    scaled[...] = weights_ref[...] * charges_ref[...]
    zero = jnp.zeros((8, LANES), F32)

    def tile(step, carry):
        at = pl.ds(pl.multiple_of(step * LANES, LANES), LANES)
        near_masks, next_masks, groups, bits = local_place(anchors_ref, at)
        for k in range(4):
            blocks = []
            for j in range(4):
                rows = [
                    jnp.broadcast_to(scaled[16 * i + 4 * j + k, at][None, :], (8, LANES))
                    for i in range(4)
                ]
                blocks.append(two_rows(rows, near_masks, next_masks))
            for mask, shift, count in zip(bits, (1, 2, 4), (5, 7, 10)):
                wider = []
                for line in range(count):
                    low = blocks[line] if line < len(blocks) else (zero, zero)
                    high = blocks[line - shift] if line >= shift else (zero, zero)
                    wider.append(tuple(jnp.where(mask, h, l) for h, l in zip(high, low)))
                blocks = wider
            extras = []
            for line in range(LINES_B):
                near, after = blocks[line]
                pieces = []
                for v in range(5):
                    piece = jnp.where(groups[v], near, zero) if v < 4 else zero
                    if v > 0:
                        piece = jnp.where(groups[v - 1], after, piece)
                    pieces.append(piece)
                high, low = halves(jnp.concatenate(pieces[:4], axis=0))
                spread[0, k, pl.ds(line * 32, 32), at] = high
                spread[1, k, pl.ds(line * 32, 32), at] = low
                extras.append(pieces[4])
            high, low = halves(jnp.concatenate(extras, axis=0))
            spread[0, k, pl.ds(MAIN, 8 * LINES_B), at] = high
            spread[1, k, pl.ds(MAIN, 8 * LINES_B), at] = low
        return carry

    lax.fori_loop(0, TILES, tile, 0)
    hot = onehot(anchors_ref)
    total = None
    for k in range(4):
        placed = dot(spread[0, k], hot, ((1,), (1,))) + dot(spread[1, k], hot, ((1,), (1,)))
        placed = pltpu.roll(placed, k, 1) if k else placed
        total = placed if total is None else total + placed
    lines[pl.ds(0, MAIN), :] = total[:MAIN]
    lines[pl.ds(MAIN, LINES - MAIN), :] = jnp.zeros((LINES - MAIN, G), F32)
    for line in range(LINES_B):
        lines[pl.ds(extra_row(line), 2), :] = total[MAIN + 8 * line : MAIN + 8 * line + 2]
    out_ref[...] = dot_split((table_ref[0], table_ref[1]), halves(lines[...]), ((1,), (1,)))


def lane_roll(value, shift):
    shift = shift % LANES
    return pltpu.roll(value, shift, 1) if shift else value


def plane_kernel(tiles_ref, spectrum_ref, first_ref, second_ref, flipped_ref, out_ref, whole):
    lane = lax.broadcasted_iota(jnp.int32, (32, LANES), 1)
    slots = [(lane >> 5) == s for s in range(4)]
    rim = (lane & 31) < 2
    sides = [rim & (lane < 64), rim & (lane >= 64)]
    pieces = []
    for r in range(ROWS):
        main = [tiles_ref[pl.ds(32 * r, 32), pl.ds(LANES * v, LANES)] for v in range(3)]
        extra = tiles_ref[pl.ds(32 * ((r - 1) % ROWS), 32), pl.ds(2 * LANES, LANES)]
        for p in range(5):
            side = p % 2
            moved = lane_roll(extra, 64 * side - 64 - 2 * p)
            main[p // 2] = main[p // 2] + jnp.where(sides[side], moved, 0.0)
        pieces.append(main)
    for line in range(LINES_B):
        for w in range(2):
            joined = None
            for s in range(4):
                moved = lane_roll(pieces[4 * w + s][line // 4], 32 * (s - line % 4))
                joined = moved if joined is None else jnp.where(slots[s], moved, joined)
            whole[pl.ds(32 * line, 32), pl.ds(LANES * w, LANES)] = joined
    first = (first_ref[0], first_ref[1])
    half = dot_split(halves(whole[...]), first)
    image = dot_split((second_ref[0], second_ref[1]), halves(half))
    image = image * (spectrum_ref[...] * (1.0 / (G * G * G)))
    half = dot_split((flipped_ref[0], flipped_ref[1]), halves(image))
    whole[...] = dot_split(halves(half), first, ((1,), (1,)))
    results = []
    for r in range(ROWS):
        main = []
        for v in range(3):
            joined = None
            for s in range(4 if v < 2 else 2):
                line = 4 * v + s
                block = whole[pl.ds(32 * line, 32), pl.ds(LANES * (r // 4), LANES)]
                moved = lane_roll(block, 32 * (s - r % 4))
                joined = moved if joined is None else jnp.where(slots[s], moved, joined)
            main.append(joined)
        results.append(main)
    for r in range(ROWS):
        source = results[(r + 1) % ROWS]
        last = jnp.where(lane < 64, results[r][2], 0.0)
        for p in range(5):
            side = p % 2
            moved = lane_roll(source[p // 2], 64 + 2 * p - 64 * side)
            here = ((lane & 31) >> 1 == p) & (lane >= 64)
            last = jnp.where(here, moved, last)
        out_ref[pl.ds(32 * r, 32), pl.ds(0, LANES)] = results[r][0]
        out_ref[pl.ds(32 * r, 32), pl.ds(LANES, LANES)] = results[r][1]
        out_ref[pl.ds(32 * r, 32), pl.ds(2 * LANES, LANES)] = last


def gather_kernel(field_ref, anchors_ref, weights_ref, table_ref, near_ref, out_ref, lines, picked):
    turned = halves(field_ref[...].T)
    field = dot_split(turned, (table_ref[0], table_ref[1]))
    lines[pl.ds(0, MAIN), :] = field[:MAIN]
    lines[pl.ds(MAIN, 8 * LINES_B), :] = jnp.zeros((8 * LINES_B, G), F32)
    for line in range(LINES_B):
        row = extra_row(line)
        lines[pl.ds(MAIN + 8 * line, 2), :] = field[row : row + 2]
    hot = onehot(anchors_ref)
    for k in range(4):
        moved = lines[...]
        moved = pltpu.roll(moved, G - k, 1) if k else moved
        high, low = halves(moved)
        picked[k] = dot(high, hot) + dot(low, hot)

    def tile(step, carry):
        at = pl.ds(pl.multiple_of(step * LANES, LANES), LANES)
        near_masks, next_masks, groups, bits = local_place(anchors_ref, at)
        total = jnp.zeros((8, LANES), F32)
        for k in range(4):
            blocks = []
            for line in range(LINES_B):
                rows = [picked[k, pl.ds(32 * line + 8 * v, 8), at] for v in range(4)]
                rows.append(picked[k, pl.ds(MAIN + 8 * line, 8), at])
                pair = []
                for skip in range(2):
                    chosen = rows[skip]
                    for g in range(1, 4):
                        chosen = jnp.where(groups[g], rows[g + skip], chosen)
                    pair.append(chosen)
                blocks.append(pair)
            for mask, shift, count in zip(bits[::-1], (4, 2, 1), (7, 5, 4)):
                fewer = []
                for line in range(count):
                    low = blocks[line]
                    if line + shift < len(blocks):
                        high = blocks[line + shift]
                        fewer.append([jnp.where(mask, h, l) for h, l in zip(high, low)])
                    else:
                        fewer.append(low)
                blocks = fewer
            for j in range(4):
                rows = [
                    jnp.broadcast_to(weights_ref[16 * i + 4 * j + k, at][None, :], (8, LANES))
                    for i in range(4)
                ]
                near, after = two_rows(rows, near_masks, next_masks)
                total = total + (near * blocks[j][0] + after * blocks[j][1])
        out_ref[:, at] = jnp.sum(total, axis=0, keepdims=True) + near_ref[:, at]
        return carry

    lax.fori_loop(0, TILES, tile, 0)


def near_kernel(count_ref, target_ref, source_ref, charges_ref, tiles_ref, out_ref, beside, total, sem):
    step = pl.program_id(0)
    per_step, size = tiles_ref.shape[0], tiles_ref.shape[1]

    @pl.when(step == 0)
    def _():
        row, col = lax.axis_index("row"), lax.axis_index("col")
        copies = []
        for n in range(9):
            patch = ((row + n // 3 + ROWS - 1) % ROWS) * COLS + (col + n % 3 + COLS - 1) % COLS
            copies.append(
                pltpu.make_async_copy(
                    charges_ref.at[pl.ds(patch * 8, 8)], beside.at[pl.ds(8 * n, 8)], sem.at[n]
                )
            )
        for copy in copies:
            copy.start()
        total[...] = jnp.zeros_like(total)
        for copy in copies:
            copy.wait()

    def slot(u, carry):
        place = step * per_step + u
        rows = pl.ds(pl.multiple_of(target_ref[place] * size, size), size)
        source = beside[pl.ds(source_ref[place], 1), :]
        total[rows, :] = total[rows, :] + tiles_ref[u] * source
        return carry

    lax.fori_loop(0, jnp.clip(count_ref[0] - step * per_step, 0, per_step), slot, 0)

    @pl.when(step == pl.num_programs(0) - 1)
    def _():
        ones = jnp.ones((8, size), BF16)
        rest = total[...]
        result = jnp.zeros((8, TRI), F32)
        for _ in range(3):
            part = rest.astype(BF16)
            result = result + dot(ones, part, ((1,), (1,)))
            rest = rest - part.astype(F32)
        out_ref[...] = result[0:1]


def near_field(charges, near_count, near_target, near_source, near_tiles):
    slots, size, _ = near_tiles.shape
    everyone = lax.all_gather(charges.reshape(8, size), BOTH, axis=0, tiled=True)
    per_step = 8
    return pl.pallas_call(
        near_kernel,
        grid=(slots // per_step,),
        in_specs=[
            pl.BlockSpec(memory_space=pltpu.SMEM),
            pl.BlockSpec(memory_space=pltpu.SMEM),
            pl.BlockSpec(memory_space=pltpu.SMEM),
            pl.BlockSpec(memory_space=pl.ANY),
            pl.BlockSpec((per_step, size, size), lambda step: (step, 0, 0)),
        ],
        out_specs=pl.BlockSpec((1, TRI), lambda step: (0, 0)),
        out_shape=jax.ShapeDtypeStruct((1, TRI), F32),
        scratch_shapes=[
            pltpu.VMEM((72, size), F32),
            pltpu.VMEM((TRI, size), F32),
            pltpu.SemaphoreType.DMA((9,)),
        ],
        compiler_params=PARAMS,
        name="near",
    )(near_count, near_target, near_source, everyone, near_tiles)


def exchange(values):
    return lax.all_to_all(values, BOTH, split_axis=0, concat_axis=0, tiled=True)


def local(
    charges,
    anchors,
    stencil_weights,
    kernel_spectrum,
    near_count,
    near_target,
    near_source,
    near_tiles,
):
    lines_table, first, second, flipped = [jnp.asarray(table) for table in tables()]
    spectrum = lax.all_gather(kernel_spectrum, "row", axis=0, tiled=True)
    spectrum = lax.dynamic_index_in_dim(spectrum, lax.axis_index("row"), axis=1, keepdims=False)
    deposited = pl.pallas_call(
        deposit_kernel,
        out_shape=jax.ShapeDtypeStruct((G, LINES), F32),
        scratch_shapes=[
            pltpu.VMEM((64, TRI), F32),
            pltpu.VMEM((2, 4, SPREAD, TRI), BF16),
            pltpu.VMEM((LINES, G), F32),
        ],
        compiler_params=PARAMS,
        name="deposit",
    )(charges.reshape(1, TRI), anchors, stencil_weights, lines_table)
    received = exchange(deposited)
    near = near_field(charges, near_count, near_target, near_source, near_tiles)
    handed = pl.pallas_call(
        plane_kernel,
        out_shape=jax.ShapeDtypeStruct((G, LINES), F32),
        scratch_shapes=[pltpu.VMEM((MAIN, G), F32)],
        compiler_params=PARAMS,
        name="plane",
    )(received, spectrum, first, second, flipped)
    field = exchange(handed)
    result = pl.pallas_call(
        gather_kernel,
        out_shape=jax.ShapeDtypeStruct((1, TRI), F32),
        scratch_shapes=[
            pltpu.VMEM((SPREAD, G), F32),
            pltpu.VMEM((4, SPREAD, TRI), F32),
        ],
        compiler_params=PARAMS,
        name="gather",
    )(field, anchors, stencil_weights, lines_table, near)
    return result.reshape(TRI)


def solution(mesh):
    return jax.shard_map(
        local,
        mesh=mesh,
        in_specs=(
            P(("row", "col")),
            P(None, ("row", "col")),
            P(None, ("row", "col")),
            P("row", "col", None),
            P(("row", "col")),
            P(("row", "col")),
            P(("row", "col")),
            P(("row", "col"), None, None),
        ),
        out_specs=P(("row", "col")),
        check_vma=False,
    )
```

```python
import jax
import jax.numpy as jnp
import ml_dtypes
import numpy as np
from jax import lax
from jax.experimental import pallas as pl
from jax.experimental.pallas import tpu as pltpu
from jax.sharding import PartitionSpec as P

G = 256
ROWS = 8
COLS = 32
CELLS_A = 32
CELLS_B = 8
TRI = 1024
LINES_B = 10
MAIN = LINES_B * CELLS_A
LINES = 384
SPREAD = MAIN + 8 * LINES_B
LANES = 128
TILES = TRI // LANES
F32 = jnp.float32
BF16 = jnp.bfloat16
BOTH = ("row", "col")
KEPT = CELLS_A // 2 + 1
SENT = 2 * KEPT
PARAMS = pltpu.CompilerParams(vmem_limit_bytes=48 * 1024 * 1024)


def split_table(table):
    high = table.astype(np.float32).astype(ml_dtypes.bfloat16)
    low = (table - high.astype(np.float64)).astype(np.float32).astype(ml_dtypes.bfloat16)
    return np.stack([high, low])


def cas(first, second):
    angle = (np.outer(first, second) % G) * (2.0 * np.pi / G)
    return np.cos(angle) + np.sin(angle)


def tables():
    steps = np.arange(G)
    device = np.arange(ROWS * COLS)
    plane = CELLS_B * (device % COLS) + device // COLS
    along_a = (np.arange(G) - 1) % G
    order = np.arange(LINES_B * COLS)
    along_b = (CELLS_B * (order % COLS) - 1 + order // COLS) % G
    folded = np.minimum(steps, G - steps)
    block, inside = folded // CELLS_A, folded % CELLS_A
    mirrored = inside >= KEPT
    owner = np.where(mirrored, ROWS - 1 - block, block)
    inside = np.where(mirrored, CELLS_A - inside, inside)
    chosen = np.zeros((2, G, ROWS * SENT), ml_dtypes.bfloat16)
    for half in range(2):
        chosen[half, steps, owner * SENT + half * KEPT + inside] = 1.0
    lines = cas(plane, steps)
    first = cas(along_a, steps)
    second = cas(steps, along_b)
    return split_table(lines), split_table(first), split_table(second), split_table(second.T), chosen


def halves(value):
    high = value.astype(BF16)
    low = (value - high.astype(F32)).astype(BF16)
    return high, low


def thirds(value):
    parts = []
    for _ in range(3):
        parts.append(value.astype(BF16))
        value = value - parts[-1].astype(F32)
    return parts


def dot(left, right, dims=((1,), (0,))):
    return lax.dot_general(left, right, (dims, ((), ())), preferred_element_type=F32)


def dot_split(left, right, dims=((1,), (0,))):
    left_high, left_low = left
    right_high, right_low = right
    cross = dot(left_high, right_low, dims) + dot(left_low, right_high, dims)
    return dot(left_high, right_high, dims) + cross


def extra_row(line):
    return MAIN + 2 * (line // 2) + 32 * (line % 2)


def onehot(anchors_ref):
    cells = lax.broadcasted_iota(jnp.int32, (G, TRI), 0)
    matched = cells == anchors_ref[2:3, :]
    return jnp.where(matched, 1.0, 0.0).astype(BF16)


def local_place(anchors_ref, at):
    first = (anchors_ref[0:1, at] - (lax.axis_index("row") * CELLS_A - 1)) & (G - 1)
    second = (anchors_ref[1:2, at] - (lax.axis_index("col") * CELLS_B - 1)) & (G - 1)
    first = jnp.broadcast_to(first, (8, LANES))
    second = jnp.broadcast_to(second, (8, LANES))
    relative = lax.broadcasted_iota(jnp.int32, (8, LANES), 0) - (first & 7)
    near_masks = [relative == i for i in range(4)]
    next_masks = [relative == i - 8 for i in range(1, 4)]
    group = first >> 3
    groups = [group == g for g in range(4)]
    bits = [(second & bit) != 0 for bit in (1, 2, 4)]
    return near_masks, next_masks, groups, bits


def two_rows(rows, near_masks, next_masks):
    near = jnp.zeros((8, LANES), F32)
    after = jnp.zeros((8, LANES), F32)
    for i in range(4):
        near = jnp.where(near_masks[i], rows[i], near)
    for i in range(1, 4):
        after = jnp.where(next_masks[i - 1], rows[i], after)
    return near, after


def deposit_kernel(
    charges_hbm, anchors_hbm, weights_hbm, table_hbm, spectrum_hbm, out_ref, sent_ref,
    charges_ref, anchors_ref, weights_ref, table_ref, spectrum_ref, scaled, spread, lines, sem,
):
    pairs = (
        (weights_hbm, weights_ref),
        (anchors_hbm, anchors_ref),
        (charges_hbm, charges_ref),
        (spectrum_hbm.at[pl.ds(0, CELLS_B * KEPT), pl.ds(0, LANES)], spectrum_ref.at[0]),
        (spectrum_hbm.at[pl.ds(0, CELLS_B * KEPT), pl.ds(LANES, LANES)], spectrum_ref.at[1]),
        (table_hbm, table_ref),
    )
    copies = [pltpu.make_async_copy(a, b, sem.at[n]) for n, (a, b) in enumerate(pairs)]
    for copy in copies:
        copy.start()
    for copy in copies[:3]:
        copy.wait()
    scaled[...] = weights_ref[...] * charges_ref[...]
    zero = jnp.zeros((8, LANES), F32)

    def tile(step, carry):
        at = pl.ds(pl.multiple_of(step * LANES, LANES), LANES)
        near_masks, next_masks, groups, bits = local_place(anchors_ref, at)
        for k in range(4):
            blocks = []
            for j in range(4):
                rows = [
                    jnp.broadcast_to(scaled[16 * i + 4 * j + k, at][None, :], (8, LANES))
                    for i in range(4)
                ]
                blocks.append(two_rows(rows, near_masks, next_masks))
            for mask, shift, count in zip(bits, (1, 2, 4), (5, 7, 10)):
                wider = []
                for line in range(count):
                    low = blocks[line] if line < len(blocks) else (zero, zero)
                    high = blocks[line - shift] if line >= shift else (zero, zero)
                    wider.append(tuple(jnp.where(mask, h, l) for h, l in zip(high, low)))
                blocks = wider
            extras = []
            for line in range(LINES_B):
                near, after = blocks[line]
                pieces = []
                for v in range(5):
                    piece = jnp.where(groups[v], near, zero) if v < 4 else zero
                    if v > 0:
                        piece = jnp.where(groups[v - 1], after, piece)
                    pieces.append(piece)
                high, low = halves(jnp.concatenate(pieces[:4], axis=0))
                spread[0, k, pl.ds(line * 32, 32), at] = high
                spread[1, k, pl.ds(line * 32, 32), at] = low
                extras.append(pieces[4])
            high, low = halves(jnp.concatenate(extras, axis=0))
            spread[0, k, pl.ds(MAIN, 8 * LINES_B), at] = high
            spread[1, k, pl.ds(MAIN, 8 * LINES_B), at] = low
        return carry

    lax.fori_loop(0, TILES, tile, 0)
    for copy in copies[3:]:
        copy.wait()
    for c in range(CELLS_B):
        for half in range(2):
            rows = spectrum_ref[half, pl.ds(c, KEPT, stride=CELLS_B), :]
            sent_ref[pl.ds(c * SENT + half * KEPT, KEPT), :] = rows
    hot = onehot(anchors_ref)
    total = None
    for k in range(4):
        placed = dot(spread[0, k], hot, ((1,), (1,))) + dot(spread[1, k], hot, ((1,), (1,)))
        placed = pltpu.roll(placed, k, 1) if k else placed
        total = placed if total is None else total + placed
    lines[pl.ds(0, MAIN), :] = total[:MAIN]
    lines[pl.ds(MAIN, LINES - MAIN), :] = jnp.zeros((LINES - MAIN, G), F32)
    for line in range(LINES_B):
        lines[pl.ds(extra_row(line), 2), :] = total[MAIN + 8 * line : MAIN + 8 * line + 2]
    result = dot_split((table_ref[0], table_ref[1]), halves(lines[...]), ((1,), (1,)))
    for v in range(3):
        out_ref[pl.ds(v, G, stride=3), :] = result[:, LANES * v : LANES * (v + 1)]


def lane_roll(value, shift):
    shift = shift % LANES
    return pltpu.roll(value, shift, 1) if shift else value


def plane_kernel(tiles_ref, spectrum_ref, chosen_ref, first_ref, second_ref, flipped_ref, out_ref, whole):
    lane = lax.broadcasted_iota(jnp.int32, (32, LANES), 1)
    slots = [(lane >> 5) == s for s in range(4)]
    rim = (lane & 31) < 2
    sides = [rim & (lane < 64), rim & (lane >= 64)]
    pieces = []
    for r in range(ROWS):
        main = [tiles_ref[pl.ds(96 * r + v, 32, stride=3), :] for v in range(3)]
        extra = tiles_ref[pl.ds(96 * ((r - 1) % ROWS) + 2, 32, stride=3), :]
        for p in range(5):
            side = p % 2
            moved = lane_roll(extra, 64 * side - 64 - 2 * p)
            main[p // 2] = main[p // 2] + jnp.where(sides[side], moved, 0.0)
        pieces.append(main)
    for line in range(LINES_B):
        for w in range(2):
            joined = None
            for s in range(4):
                moved = lane_roll(pieces[4 * w + s][line // 4], 32 * (s - line % 4))
                joined = moved if joined is None else jnp.where(slots[s], moved, joined)
            whole[pl.ds(32 * line, 32), pl.ds(LANES * w, LANES)] = joined
    scale = 1.0 / (G * G * G)
    parts = thirds(spectrum_ref[...])
    spectrum = jnp.concatenate(
        [sum(dot(chosen_ref[half], part) for part in parts) * scale for half in range(2)], axis=1
    )
    first = (first_ref[0], first_ref[1])
    half = dot_split(halves(whole[...]), first)
    image = dot_split((second_ref[0], second_ref[1]), halves(half))
    image = image * spectrum
    half = dot_split((flipped_ref[0], flipped_ref[1]), halves(image))
    whole[...] = dot_split(halves(half), first, ((1,), (1,)))
    results = []
    for r in range(ROWS):
        main = []
        for v in range(3):
            joined = None
            for s in range(4 if v < 2 else 2):
                line = 4 * v + s
                block = whole[pl.ds(32 * line, 32), pl.ds(LANES * (r // 4), LANES)]
                moved = lane_roll(block, 32 * (s - r % 4))
                joined = moved if joined is None else jnp.where(slots[s], moved, joined)
            main.append(joined)
        results.append(main)
    for r in range(ROWS):
        source = results[(r + 1) % ROWS]
        last = jnp.where(lane < 64, results[r][2], 0.0)
        for p in range(5):
            side = p % 2
            moved = lane_roll(source[p // 2], 64 + 2 * p - 64 * side)
            here = ((lane & 31) >> 1 == p) & (lane >= 64)
            last = jnp.where(here, moved, last)
        for v, value in enumerate((results[r][0], results[r][1], last)):
            out_ref[pl.ds(96 * r + v, 32, stride=3), :] = value


def gather_kernel(field_ref, anchors_ref, weights_ref, table_ref, near_ref, out_ref, lines, picked):
    turned = [field_ref[pl.ds(v, G, stride=3), :].T for v in range(3)]
    turned = halves(jnp.concatenate(turned, axis=0))
    field = dot_split(turned, (table_ref[0], table_ref[1]))
    lines[pl.ds(0, MAIN), :] = field[:MAIN]
    lines[pl.ds(MAIN, 8 * LINES_B), :] = jnp.zeros((8 * LINES_B, G), F32)
    for line in range(LINES_B):
        row = extra_row(line)
        lines[pl.ds(MAIN + 8 * line, 2), :] = field[row : row + 2]
    hot = onehot(anchors_ref)
    for k in range(4):
        moved = lines[...]
        moved = pltpu.roll(moved, G - k, 1) if k else moved
        high, low = halves(moved)
        picked[k] = dot(high, hot) + dot(low, hot)

    def tile(step, carry):
        at = pl.ds(pl.multiple_of(step * LANES, LANES), LANES)
        near_masks, next_masks, groups, bits = local_place(anchors_ref, at)
        total = jnp.zeros((8, LANES), F32)
        for k in range(4):
            blocks = []
            for line in range(LINES_B):
                rows = [picked[k, pl.ds(32 * line + 8 * v, 8), at] for v in range(4)]
                rows.append(picked[k, pl.ds(MAIN + 8 * line, 8), at])
                pair = []
                for skip in range(2):
                    chosen = rows[skip]
                    for g in range(1, 4):
                        chosen = jnp.where(groups[g], rows[g + skip], chosen)
                    pair.append(chosen)
                blocks.append(pair)
            for mask, shift, count in zip(bits[::-1], (4, 2, 1), (7, 5, 4)):
                fewer = []
                for line in range(count):
                    low = blocks[line]
                    if line + shift < len(blocks):
                        high = blocks[line + shift]
                        fewer.append([jnp.where(mask, h, l) for h, l in zip(high, low)])
                    else:
                        fewer.append(low)
                blocks = fewer
            for j in range(4):
                rows = [
                    jnp.broadcast_to(weights_ref[16 * i + 4 * j + k, at][None, :], (8, LANES))
                    for i in range(4)
                ]
                near, after = two_rows(rows, near_masks, next_masks)
                total = total + (near * blocks[j][0] + after * blocks[j][1])
        out_ref[:, at] = jnp.sum(total, axis=0, keepdims=True) + near_ref[:, at]
        return carry

    lax.fori_loop(0, TILES, tile, 0)


def near_kernel(count_ref, target_ref, source_ref, charges_ref, tiles_ref, out_ref, total):
    step = pl.program_id(0)
    per_step, size = tiles_ref.shape[0], tiles_ref.shape[1]

    @pl.when(step == 0)
    def _():
        total[...] = jnp.zeros_like(total)

    def slot(u, carry):
        place = step * per_step + u
        rows = pl.ds(pl.multiple_of(target_ref[place] * size, size), size)
        source = charges_ref[pl.ds(source_ref[place], 1), :]
        total[rows, :] = total[rows, :] + tiles_ref[u] * source
        return carry

    lax.fori_loop(0, jnp.clip(count_ref[0] - step * per_step, 0, per_step), slot, 0)

    @pl.when(step == pl.num_programs(0) - 1)
    def _():
        ones = jnp.ones((8, size), BF16)
        result = sum(dot(ones, part, ((1,), (1,))) for part in thirds(total[...]))
        out_ref[...] = result[0:1]


def with_sides(value, axis):
    size = lax.axis_size(axis)
    up = [(i, (i + 1) % size) for i in range(size)]
    down = [(j, i) for i, j in up]
    before = lax.ppermute(value, axis, up)
    after = lax.ppermute(value, axis, down)
    return jnp.stack([before, value, after])


def near_field(charges, near_count, near_target, near_source, near_tiles):
    slots, size, _ = near_tiles.shape
    beside = with_sides(charges.reshape(8, size), "col")
    beside = with_sides(beside.reshape(24, size), "row").reshape(72, size)
    per_step = 8
    smem = pl.BlockSpec(memory_space=pltpu.SMEM)
    return pl.pallas_call(
        near_kernel,
        grid=(slots // per_step,),
        in_specs=[
            smem,
            smem,
            smem,
            pl.BlockSpec((72, size), lambda step: (0, 0)),
            pl.BlockSpec((per_step, size, size), lambda step: (step, 0, 0)),
        ],
        out_specs=pl.BlockSpec((1, TRI), lambda step: (0, 0)),
        out_shape=jax.ShapeDtypeStruct((1, TRI), F32),
        scratch_shapes=[pltpu.VMEM((TRI, size), F32)],
        compiler_params=PARAMS,
        name="near",
    )(near_count, near_target, near_source, beside, near_tiles)


def exchange(values, axes, pieces):
    shaped = values.reshape(pieces, 1, values.size // pieces)
    moved = lax.all_to_all(shaped, axes, split_axis=0, concat_axis=0, tiled=True)
    return moved.reshape(values.shape)


def local(
    charges,
    anchors,
    stencil_weights,
    kernel_spectrum,
    near_count,
    near_target,
    near_source,
    near_tiles,
):
    lines_table, first, second, flipped, chosen = [jnp.asarray(table) for table in tables()]
    devices = ROWS * COLS
    packed = jax.ShapeDtypeStruct((devices * LINES // LANES, LANES), F32)
    hbm = pl.BlockSpec(memory_space=pltpu.HBM)
    deposited, sent = pl.pallas_call(
        deposit_kernel,
        out_shape=(packed, jax.ShapeDtypeStruct((CELLS_B * SENT, LANES), F32)),
        in_specs=[hbm] * 5,
        scratch_shapes=[
            pltpu.VMEM((1, TRI), F32),
            pltpu.VMEM((3, TRI), jnp.int32),
            pltpu.VMEM((64, TRI), F32),
            pltpu.VMEM((2, G, G), BF16),
            pltpu.VMEM((2, CELLS_B * KEPT, LANES), F32),
            pltpu.VMEM((64, TRI), F32),
            pltpu.VMEM((2, 4, SPREAD, TRI), BF16),
            pltpu.VMEM((LINES, G), F32),
            pltpu.SemaphoreType.DMA((6,)),
        ],
        compiler_params=PARAMS,
        name="deposit",
    )(
        charges.reshape(1, TRI),
        anchors,
        stencil_weights,
        lines_table,
        kernel_spectrum.reshape(CELLS_A * CELLS_B, G),
    )
    received = exchange(deposited, BOTH, devices)
    spectrum = exchange(sent, "row", ROWS)
    handed = pl.pallas_call(
        plane_kernel,
        out_shape=packed,
        scratch_shapes=[pltpu.VMEM((MAIN, G), F32)],
        compiler_params=PARAMS,
        name="plane",
    )(received, spectrum, chosen, first, second, flipped)
    field = exchange(handed, BOTH, devices)
    charges, _ = lax.optimization_barrier((charges, handed))
    near = near_field(charges, near_count, near_target, near_source, near_tiles)
    result = pl.pallas_call(
        gather_kernel,
        out_shape=jax.ShapeDtypeStruct((1, TRI), F32),
        scratch_shapes=[
            pltpu.VMEM((SPREAD, G), F32),
            pltpu.VMEM((4, SPREAD, TRI), F32),
        ],
        compiler_params=PARAMS,
        name="gather",
    )(field, anchors, stencil_weights, lines_table, near)
    return result.reshape(TRI)


def solution(mesh):
    return jax.shard_map(
        local,
        mesh=mesh,
        in_specs=(
            P(("row", "col")),
            P(None, ("row", "col")),
            P(None, ("row", "col")),
            P("row", "col", None),
            P(("row", "col")),
            P(("row", "col")),
            P(("row", "col")),
            P(("row", "col"), None, None),
        ),
        out_specs=P(("row", "col")),
        check_vma=False,
    )
```

```python
import jax
import jax.numpy as jnp
import ml_dtypes
import numpy as np
from jax import lax
from jax.experimental import pallas as pl
from jax.experimental.pallas import tpu as pltpu
from jax.sharding import PartitionSpec as P

G = 256
ROWS = 8
COLS = 32
CELLS_A = 32
CELLS_B = 8
TRI = 1024
LINES_B = 10
MAIN = LINES_B * CELLS_A
LINES = 384
SPREAD = MAIN + 8 * LINES_B
LANES = 128
TILES = TRI // LANES
F32 = jnp.float32
BF16 = jnp.bfloat16
BOTH = ("row", "col")
KEPT = CELLS_A // 2 + 1
SENT = 40
PARAMS = pltpu.CompilerParams(vmem_limit_bytes=48 * 1024 * 1024)


def split_table(table):
    high = table.astype(np.float32).astype(ml_dtypes.bfloat16)
    low = (table - high.astype(np.float64)).astype(np.float32).astype(ml_dtypes.bfloat16)
    return np.stack([high, low])


def cas(first, second):
    angle = (np.outer(first, second) % G) * (2.0 * np.pi / G)
    return np.cos(angle) + np.sin(angle)


def tables():
    steps = np.arange(G)
    device = np.arange(ROWS * COLS)
    plane = CELLS_B * (device % COLS) + device // COLS
    along_a = (np.arange(G) - 1) % G
    order = np.arange(LINES_B * COLS)
    along_b = (CELLS_B * (order % COLS) - 1 + order // COLS) % G
    folded = np.minimum(steps, G - steps)
    block, inside = folded // CELLS_A, folded % CELLS_A
    mirrored = inside >= KEPT
    owner = np.where(mirrored, ROWS - 1 - block, block)
    inside = np.where(mirrored, CELLS_A - inside, inside)
    chosen = np.zeros((2, G, ROWS * SENT), ml_dtypes.bfloat16)
    for half in range(2):
        chosen[half, steps, owner * SENT + half * KEPT + inside] = 1.0
    lines = cas(plane, steps)
    first = cas(along_a, steps)
    second = cas(steps, along_b)
    return split_table(lines), split_table(first), split_table(second), split_table(second.T), chosen


def halves(value):
    high = value.astype(BF16)
    low = (value - high.astype(F32)).astype(BF16)
    return high, low


def thirds(value):
    parts = []
    for _ in range(3):
        parts.append(value.astype(BF16))
        value = value - parts[-1].astype(F32)
    return parts


def dot(left, right, dims=((1,), (0,))):
    return lax.dot_general(left, right, (dims, ((), ())), preferred_element_type=F32)


def dot_split(left, right, dims=((1,), (0,))):
    left_high, left_low = left
    right_high, right_low = right
    cross = dot(left_high, right_low, dims) + dot(left_low, right_high, dims)
    return dot(left_high, right_high, dims) + cross


def extra_row(line):
    return MAIN + 2 * (line // 2) + 32 * (line % 2)


def onehot(anchors_ref):
    cells = lax.broadcasted_iota(jnp.int32, (G, TRI), 0)
    matched = cells == anchors_ref[2:3, :]
    return jnp.where(matched, 1.0, 0.0).astype(BF16)


def local_place(anchors_ref, at):
    first = (anchors_ref[0:1, at] - (lax.axis_index("row") * CELLS_A - 1)) & (G - 1)
    second = (anchors_ref[1:2, at] - (lax.axis_index("col") * CELLS_B - 1)) & (G - 1)
    first = jnp.broadcast_to(first, (8, LANES))
    second = jnp.broadcast_to(second, (8, LANES))
    relative = lax.broadcasted_iota(jnp.int32, (8, LANES), 0) - (first & 7)
    near_masks = [relative == i for i in range(4)]
    next_masks = [relative == i - 8 for i in range(1, 4)]
    group = first >> 3
    groups = [group == g for g in range(4)]
    bits = [(second & bit) != 0 for bit in (1, 2, 4)]
    return near_masks, next_masks, groups, bits


def two_rows(rows, near_masks, next_masks):
    near = jnp.zeros((8, LANES), F32)
    after = jnp.zeros((8, LANES), F32)
    for i in range(4):
        near = jnp.where(near_masks[i], rows[i], near)
    for i in range(1, 4):
        after = jnp.where(next_masks[i - 1], rows[i], after)
    return near, after


def deposit_kernel(
    charges_hbm, anchors_hbm, weights_hbm, table_hbm, spectrum_hbm, out_ref, *rest
):
    sent_refs = rest[:ROWS]
    charges_ref, anchors_ref, weights_ref, table_ref, spectrum_ref = rest[ROWS : ROWS + 5]
    scaled, spread, lines, sem = rest[ROWS + 5 :]
    pairs = (
        (weights_hbm, weights_ref),
        (anchors_hbm, anchors_ref),
        (charges_hbm, charges_ref),
        (spectrum_hbm.at[pl.ds(0, CELLS_B * KEPT), pl.ds(0, LANES)], spectrum_ref.at[0]),
        (spectrum_hbm.at[pl.ds(0, CELLS_B * KEPT), pl.ds(LANES, LANES)], spectrum_ref.at[1]),
        (table_hbm, table_ref),
    )
    copies = [pltpu.make_async_copy(a, b, sem.at[n]) for n, (a, b) in enumerate(pairs)]
    for copy in copies:
        copy.start()
    for copy in copies[:3]:
        copy.wait()
    scaled[...] = weights_ref[...] * charges_ref[...]
    zero = jnp.zeros((8, LANES), F32)

    def tile(step, carry):
        at = pl.ds(pl.multiple_of(step * LANES, LANES), LANES)
        near_masks, next_masks, groups, bits = local_place(anchors_ref, at)
        for k in range(4):
            blocks = []
            for j in range(4):
                rows = [
                    jnp.broadcast_to(scaled[16 * i + 4 * j + k, at][None, :], (8, LANES))
                    for i in range(4)
                ]
                blocks.append(two_rows(rows, near_masks, next_masks))
            for mask, shift, count in zip(bits, (1, 2, 4), (5, 7, 10)):
                wider = []
                for line in range(count):
                    low = blocks[line] if line < len(blocks) else (zero, zero)
                    high = blocks[line - shift] if line >= shift else (zero, zero)
                    wider.append(tuple(jnp.where(mask, h, l) for h, l in zip(high, low)))
                blocks = wider
            extras = []
            for line in range(LINES_B):
                near, after = blocks[line]
                pieces = []
                for v in range(5):
                    piece = jnp.where(groups[v], near, zero) if v < 4 else zero
                    if v > 0:
                        piece = jnp.where(groups[v - 1], after, piece)
                    pieces.append(piece)
                high, low = halves(jnp.concatenate(pieces[:4], axis=0))
                spread[0, k, pl.ds(line * 32, 32), at] = high
                spread[1, k, pl.ds(line * 32, 32), at] = low
                extras.append(pieces[4])
            high, low = halves(jnp.concatenate(extras, axis=0))
            spread[0, k, pl.ds(MAIN, 8 * LINES_B), at] = high
            spread[1, k, pl.ds(MAIN, 8 * LINES_B), at] = low
        return carry

    lax.fori_loop(0, TILES, tile, 0)
    for copy in copies[3:]:
        copy.wait()
    for shift, sent in enumerate(sent_refs):
        c = (lax.axis_index("row") + shift) & (ROWS - 1)
        sent[pl.ds(SENT - 8, 8), :] = jnp.zeros((8, LANES), F32)
        for half in range(2):
            rows = spectrum_ref[half, pl.ds(c, KEPT, stride=CELLS_B), :]
            sent[pl.ds(half * KEPT, KEPT), :] = rows
    for shift in (1, ROWS - 1):
        for block in range(8):
            at = pl.ds(block * LANES, LANES)
            sent_refs[shift][pl.ds(SENT + block, 1), :] = charges_ref[:, at]
    hot = onehot(anchors_ref)
    total = None
    for k in range(4):
        placed = dot(spread[0, k], hot, ((1,), (1,))) + dot(spread[1, k], hot, ((1,), (1,)))
        placed = pltpu.roll(placed, k, 1) if k else placed
        total = placed if total is None else total + placed
    lines[pl.ds(0, MAIN), :] = total[:MAIN]
    lines[pl.ds(MAIN, LINES - MAIN), :] = jnp.zeros((LINES - MAIN, G), F32)
    for line in range(LINES_B):
        lines[pl.ds(extra_row(line), 2), :] = total[MAIN + 8 * line : MAIN + 8 * line + 2]
    result = dot_split((table_ref[0], table_ref[1]), halves(lines[...]), ((1,), (1,)))
    for v in range(3):
        out_ref[pl.ds(v, G, stride=3), :] = result[:, LANES * v : LANES * (v + 1)]


def lane_roll(value, shift):
    shift = shift % LANES
    return pltpu.roll(value, shift, 1) if shift else value


def plane_kernel(
    tiles_ref, charges_ref, chosen_ref, first_ref, second_ref, flipped_ref, *rest
):
    sent_refs, (out_ref, beside_ref, whole, spectrum_ref) = rest[:ROWS], rest[ROWS:]
    for shift, sent in enumerate(sent_refs):
        owner = (lax.axis_index("row") - shift) & (ROWS - 1)
        at = pl.ds(pl.multiple_of(owner * SENT, 8), SENT)
        spectrum_ref[at, :] = sent[pl.ds(0, SENT), :]
    beside_ref[pl.ds(0, 8), :] = sent_refs[1][pl.ds(SENT, 8), :]
    beside_ref[pl.ds(8, 8), :] = charges_ref[...]
    beside_ref[pl.ds(16, 8), :] = sent_refs[ROWS - 1][pl.ds(SENT, 8), :]
    lane = lax.broadcasted_iota(jnp.int32, (32, LANES), 1)
    slots = [(lane >> 5) == s for s in range(4)]
    rim = (lane & 31) < 2
    sides = [rim & (lane < 64), rim & (lane >= 64)]
    pieces = []
    for r in range(ROWS):
        main = [tiles_ref[pl.ds(96 * r + v, 32, stride=3), :] for v in range(3)]
        extra = tiles_ref[pl.ds(96 * ((r - 1) % ROWS) + 2, 32, stride=3), :]
        for p in range(5):
            side = p % 2
            moved = lane_roll(extra, 64 * side - 64 - 2 * p)
            main[p // 2] = main[p // 2] + jnp.where(sides[side], moved, 0.0)
        pieces.append(main)
    for line in range(LINES_B):
        for w in range(2):
            joined = None
            for s in range(4):
                moved = lane_roll(pieces[4 * w + s][line // 4], 32 * (s - line % 4))
                joined = moved if joined is None else jnp.where(slots[s], moved, joined)
            whole[pl.ds(32 * line, 32), pl.ds(LANES * w, LANES)] = joined
    scale = 1.0 / (G * G * G)
    parts = thirds(spectrum_ref[...])
    spectrum = jnp.concatenate(
        [sum(dot(chosen_ref[half], part) for part in parts) * scale for half in range(2)], axis=1
    )
    first = (first_ref[0], first_ref[1])
    half = dot_split(halves(whole[...]), first)
    image = dot_split((second_ref[0], second_ref[1]), halves(half))
    image = image * spectrum
    half = dot_split((flipped_ref[0], flipped_ref[1]), halves(image))
    whole[...] = dot_split(halves(half), first, ((1,), (1,)))
    results = []
    for r in range(ROWS):
        main = []
        for v in range(3):
            joined = None
            for s in range(4 if v < 2 else 2):
                line = 4 * v + s
                block = whole[pl.ds(32 * line, 32), pl.ds(LANES * (r // 4), LANES)]
                moved = lane_roll(block, 32 * (s - r % 4))
                joined = moved if joined is None else jnp.where(slots[s], moved, joined)
            main.append(joined)
        results.append(main)
    for r in range(ROWS):
        source = results[(r + 1) % ROWS]
        last = jnp.where(lane < 64, results[r][2], 0.0)
        for p in range(5):
            side = p % 2
            moved = lane_roll(source[p // 2], 64 + 2 * p - 64 * side)
            here = ((lane & 31) >> 1 == p) & (lane >= 64)
            last = jnp.where(here, moved, last)
        for v, value in enumerate((results[r][0], results[r][1], last)):
            out_ref[pl.ds(96 * r + v, 32, stride=3), :] = value


def gather_kernel(field_ref, anchors_ref, weights_ref, table_ref, near_ref, out_ref, lines, picked):
    turned = [field_ref[pl.ds(v, G, stride=3), :].T for v in range(3)]
    turned = halves(jnp.concatenate(turned, axis=0))
    field = dot_split(turned, (table_ref[0], table_ref[1]))
    lines[pl.ds(0, MAIN), :] = field[:MAIN]
    lines[pl.ds(MAIN, 8 * LINES_B), :] = jnp.zeros((8 * LINES_B, G), F32)
    for line in range(LINES_B):
        row = extra_row(line)
        lines[pl.ds(MAIN + 8 * line, 2), :] = field[row : row + 2]
    hot = onehot(anchors_ref)
    for k in range(4):
        moved = lines[...]
        moved = pltpu.roll(moved, G - k, 1) if k else moved
        high, low = halves(moved)
        picked[k] = dot(high, hot) + dot(low, hot)

    def tile(step, carry):
        at = pl.ds(pl.multiple_of(step * LANES, LANES), LANES)
        near_masks, next_masks, groups, bits = local_place(anchors_ref, at)
        total = jnp.zeros((8, LANES), F32)
        for k in range(4):
            blocks = []
            for line in range(LINES_B):
                rows = [picked[k, pl.ds(32 * line + 8 * v, 8), at] for v in range(4)]
                rows.append(picked[k, pl.ds(MAIN + 8 * line, 8), at])
                pair = []
                for skip in range(2):
                    chosen = rows[skip]
                    for g in range(1, 4):
                        chosen = jnp.where(groups[g], rows[g + skip], chosen)
                    pair.append(chosen)
                blocks.append(pair)
            for mask, shift, count in zip(bits[::-1], (4, 2, 1), (7, 5, 4)):
                fewer = []
                for line in range(count):
                    low = blocks[line]
                    if line + shift < len(blocks):
                        high = blocks[line + shift]
                        fewer.append([jnp.where(mask, h, l) for h, l in zip(high, low)])
                    else:
                        fewer.append(low)
                blocks = fewer
            for j in range(4):
                rows = [
                    jnp.broadcast_to(weights_ref[16 * i + 4 * j + k, at][None, :], (8, LANES))
                    for i in range(4)
                ]
                near, after = two_rows(rows, near_masks, next_masks)
                total = total + (near * blocks[j][0] + after * blocks[j][1])
        out_ref[:, at] = jnp.sum(total, axis=0, keepdims=True) + near_ref[:, at]
        return carry

    lax.fori_loop(0, TILES, tile, 0)


def near_kernel(
    count_ref, target_ref, source_ref, before_ref, own_ref, after_ref, tiles_ref, out_ref,
    charges_ref, total,
):
    step = pl.program_id(0)
    per_step, size = tiles_ref.shape[0], tiles_ref.shape[1]

    @pl.when(step == 0)
    def _():
        total[...] = jnp.zeros_like(total)
        for place, ref in enumerate((before_ref, own_ref, after_ref)):
            charges_ref[pl.ds(24 * place, 24), :] = ref[...]

    def slot(u, carry):
        place = step * per_step + u
        rows = pl.ds(pl.multiple_of(target_ref[place] * size, size), size)
        code = source_ref[place]
        neighbour = code >> 3
        row = neighbour // 3
        line = 24 * (neighbour - 3 * row) + 8 * row + (code & 7)
        source = charges_ref[pl.ds(line, 1), :]
        total[rows, :] = total[rows, :] + tiles_ref[u] * source
        return carry

    lax.fori_loop(0, jnp.clip(count_ref[0] - step * per_step, 0, per_step), slot, 0)

    @pl.when(step == pl.num_programs(0) - 1)
    def _():
        ones = jnp.ones((8, size), BF16)
        result = sum(dot(ones, part, ((1,), (1,))) for part in thirds(total[...]))
        out_ref[...] = result[0:1]


def shifted(value, axis, by):
    size = lax.axis_size(axis)
    return lax.ppermute(value, axis, [(i, (i + by) % size) for i in range(size)])


def near_field(beside, near_count, near_target, near_source, near_tiles):
    slots, size, _ = near_tiles.shape
    before, after = shifted(beside, "col", 1), shifted(beside, "col", -1)
    per_step = 8
    smem = pl.BlockSpec(memory_space=pltpu.SMEM)
    return pl.pallas_call(
        near_kernel,
        grid=(slots // per_step,),
        in_specs=[
            smem,
            smem,
            smem,
            *[pl.BlockSpec((24, size), lambda step: (0, 0))] * 3,
            pl.BlockSpec((per_step, size, size), lambda step: (step, 0, 0)),
        ],
        out_specs=pl.BlockSpec((1, TRI), lambda step: (0, 0)),
        out_shape=jax.ShapeDtypeStruct((1, TRI), F32),
        scratch_shapes=[pltpu.VMEM((72, size), F32), pltpu.VMEM((TRI, size), F32)],
        compiler_params=PARAMS,
        name="near",
    )(near_count, near_target, near_source, before, beside, after, near_tiles)


def exchange(values, axes, pieces):
    shaped = values.reshape(pieces, 1, values.size // pieces)
    moved = lax.all_to_all(shaped, axes, split_axis=0, concat_axis=0, tiled=True)
    return moved.reshape(values.shape)


def local(
    charges,
    anchors,
    stencil_weights,
    kernel_spectrum,
    near_count,
    near_target,
    near_source,
    near_tiles,
):
    lines_table, first, second, flipped, chosen = [jnp.asarray(table) for table in tables()]
    devices = ROWS * COLS
    packed = jax.ShapeDtypeStruct((devices * LINES // LANES, LANES), F32)
    hbm = pl.BlockSpec(memory_space=pltpu.HBM)
    sizes = [SENT + 8 if shift in (1, ROWS - 1) else SENT for shift in range(ROWS)]
    deposited, *sent = pl.pallas_call(
        deposit_kernel,
        out_shape=(packed, *[jax.ShapeDtypeStruct((size, LANES), F32) for size in sizes]),
        in_specs=[hbm] * 5,
        scratch_shapes=[
            pltpu.VMEM((1, TRI), F32),
            pltpu.VMEM((3, TRI), jnp.int32),
            pltpu.VMEM((64, TRI), F32),
            pltpu.VMEM((2, G, G), BF16),
            pltpu.VMEM((2, CELLS_B * KEPT, LANES), F32),
            pltpu.VMEM((64, TRI), F32),
            pltpu.VMEM((2, 4, SPREAD, TRI), BF16),
            pltpu.VMEM((LINES, G), F32),
            pltpu.SemaphoreType.DMA((6,)),
        ],
        compiler_params=PARAMS,
        name="deposit",
    )(
        *[
            pltpu.with_memory_space_constraint(value, pltpu.HBM)
            for value in (
                charges.reshape(1, TRI),
                anchors,
                stencil_weights,
                lines_table,
                kernel_spectrum.reshape(CELLS_A * CELLS_B, G),
            )
        ]
    )
    received = exchange(deposited, BOTH, devices)
    sent = [shifted(value, "row", shift) if shift else value for shift, value in enumerate(sent)]
    handed, beside = pl.pallas_call(
        plane_kernel,
        out_shape=(packed, jax.ShapeDtypeStruct((24, LANES), F32)),
        scratch_shapes=[pltpu.VMEM((MAIN, G), F32), pltpu.VMEM((ROWS * SENT, LANES), F32)],
        compiler_params=PARAMS,
        name="plane",
    )(received, charges.reshape(8, LANES), chosen, first, second, flipped, *sent)
    field = exchange(handed, BOTH, devices)
    near = near_field(beside, near_count, near_target, near_source, near_tiles)
    result = pl.pallas_call(
        gather_kernel,
        out_shape=jax.ShapeDtypeStruct((1, TRI), F32),
        scratch_shapes=[
            pltpu.VMEM((SPREAD, G), F32),
            pltpu.VMEM((4, SPREAD, TRI), F32),
        ],
        compiler_params=PARAMS,
        name="gather",
    )(field, anchors, stencil_weights, lines_table, near)
    return result.reshape(TRI)


def solution(mesh):
    return jax.shard_map(
        local,
        mesh=mesh,
        in_specs=(
            P(("row", "col")),
            P(None, ("row", "col")),
            P(None, ("row", "col")),
            P("row", "col", None),
            P(("row", "col")),
            P(("row", "col")),
            P(("row", "col")),
            P(("row", "col"), None, None),
        ),
        out_specs=P(("row", "col")),
        check_vma=False,
    )
```

```python
import jax
import jax.numpy as jnp
import ml_dtypes
import numpy as np
from jax import lax
from jax.experimental import pallas as pl
from jax.experimental.pallas import tpu as pltpu
from jax.sharding import PartitionSpec as P

G = 256
ROWS = 8
COLS = 32
CELLS_A = 32
CELLS_B = 8
TRI = 1024
LINES_B = 10
MAIN = LINES_B * CELLS_A
BLOCKS = 12
LINES = BLOCKS * CELLS_A
SPREAD = MAIN + CELLS_A
LANES = 128
TILES = TRI // LANES
KEPT = CELLS_A // 2 + 1
SENT = 40
CHUNK = 256
GROUPS = ((0, 4, 8), (1, 5, 9), (2, 6), (3, 7))
F32 = jnp.float32
BF16 = jnp.bfloat16
BOTH = ("row", "col")
PARAMS = pltpu.CompilerParams(vmem_limit_bytes=48 * 1024 * 1024)


def split_table(table):
    high = table.astype(np.float32).astype(ml_dtypes.bfloat16)
    low = (table - high.astype(np.float64)).astype(np.float32).astype(ml_dtypes.bfloat16)
    return np.stack([high, low])


def cas(first, second):
    angle = (np.outer(first, second) % G) * (2.0 * np.pi / G)
    return np.cos(angle) + np.sin(angle)


def row_at(slot, block):
    return 4 * (slot // 4) + (slot - block) % 4


def tables():
    steps = np.arange(G)
    device = np.arange(ROWS * COLS)
    plane = CELLS_B * (device % COLS) + device // COLS
    along_a = (np.arange(G) - 1) % G
    order = np.concatenate([
        (CELLS_B * np.arange(COLS) - 1 + line) % G for group in GROUPS for line in group
    ])
    outer = np.zeros((G, G))
    for slot in range(ROWS):
        row = row_at(slot, LINES_B)
        for extra in range(2):
            cell = (CELLS_A * (row + 1) - 1 + extra) % G
            for line in range(LINES_B):
                outer[CELLS_A * slot + 2 * line + extra] = cas(np.array([cell]), steps)[0]
    folded = np.minimum(steps, G - steps)
    block, inside = folded // CELLS_A, folded % CELLS_A
    mirrored = inside >= KEPT
    owner = np.where(mirrored, ROWS - 1 - block, block)
    inside = np.where(mirrored, CELLS_A - inside, inside)
    chosen = np.zeros((2, G, ROWS * SENT), ml_dtypes.bfloat16)
    for half in range(2):
        chosen[half, steps, owner * SENT + half * KEPT + inside] = 1.0
    second = cas(steps, order)
    return {
        "lines": split_table(cas(plane, steps)),
        "chosen": chosen,
        "first": split_table(cas(along_a, steps)),
        "outer": split_table(outer),
        "second": split_table(second),
        "flipped": split_table(second.T),
    }


def halves(value):
    high = value.astype(BF16)
    low = (value - high.astype(F32)).astype(BF16)
    return high, low


def thirds(value):
    parts = []
    for _ in range(3):
        parts.append(value.astype(BF16))
        value = value - parts[-1].astype(F32)
    return parts


def dot(left, right, dims=((1,), (0,))):
    return lax.dot_general(left, right, (dims, ((), ())), preferred_element_type=F32)


def dot_split(left, right, dims=((1,), (0,))):
    left_high, left_low = left
    right_high, right_low = right
    cross = dot(left_high, right_low, dims) + dot(left_low, right_high, dims)
    return dot(left_high, right_high, dims) + cross


def block_place(block):
    slot = (lax.axis_index("row") + block) & 3
    return pl.ds(pl.multiple_of(LANES * (block // 4) + CELLS_A * slot, CELLS_A), CELLS_A)


def onehot(anchors_ref):
    cells = lax.broadcasted_iota(jnp.int32, (G, TRI), 0)
    matched = cells == anchors_ref[2:3, :]
    return jnp.where(matched, 1.0, 0.0).astype(BF16)


def local_place(anchors_ref, at):
    first = (anchors_ref[0:1, at] - (lax.axis_index("row") * CELLS_A - 1)) & (G - 1)
    second = (anchors_ref[1:2, at] - (lax.axis_index("col") * CELLS_B - 1)) & (G - 1)
    first = jnp.broadcast_to(first, (8, LANES))
    second = jnp.broadcast_to(second, (8, LANES))
    return lax.broadcasted_iota(jnp.int32, (8, LANES), 0) - (first & 7), first >> 3, second


def masks_of(place):
    relative, group, second = place
    near_masks = [relative == i for i in range(4)]
    next_masks = [relative == i - 8 for i in range(1, 4)]
    groups = [group == g for g in range(4)]
    bits = [(second & bit) != 0 for bit in (1, 2, 4)]
    return near_masks, next_masks, groups, bits


def two_rows(rows, near_masks, next_masks):
    near = jnp.zeros((8, LANES), F32)
    after = jnp.zeros((8, LANES), F32)
    for i in range(4):
        near = jnp.where(near_masks[i], rows[i], near)
    for i in range(1, 4):
        after = jnp.where(next_masks[i - 1], rows[i], after)
    return near, after


def stencil_rows(ref, j, k, at):
    return [
        jnp.broadcast_to(ref[16 * i + 4 * j + k, at][None, :], (8, LANES)) for i in range(4)
    ]


def spread_tile(scaled, place, spread, k, tile):
    at = pl.ds(tile * LANES, LANES)
    low_at = pl.ds(TRI + tile * LANES, LANES)
    zero = jnp.zeros((8, LANES), F32)
    near_masks, next_masks, groups, bits = masks_of(place)
    blocks = [two_rows(stencil_rows(scaled, j, k, at), near_masks, next_masks) for j in range(4)]
    for mask, shift, count in zip(bits, (1, 2, 4), (5, 7, 10)):
        wider = []
        for line in range(count):
            if line < shift:
                wider.append([jnp.where(mask, zero, low) for low in blocks[line]])
            elif line >= len(blocks):
                wider.append([jnp.where(mask, high, zero) for high in blocks[line - shift]])
            else:
                pairs = zip(blocks[line - shift], blocks[line])
                wider.append([jnp.where(mask, high, low) for high, low in pairs])
        blocks = wider
    extras = [zero] * 4
    for line in range(LINES_B):
        near, after = blocks[line]
        pieces = []
        for v in range(4):
            piece = jnp.where(groups[v], near, zero)
            pieces.append(jnp.where(groups[v - 1], after, piece) if v else piece)
        high, low = halves(jnp.concatenate(pieces, axis=0))
        rows = pl.ds(CELLS_A * line, CELLS_A)
        spread[k, rows, at] = high
        spread[k, rows, low_at] = low
        last = jnp.where(groups[3], after, zero)
        if line % 4:
            last = extras[line // 4] + pltpu.roll(last, 2 * (line % 4), 0)
        extras[line // 4] = last
    high, low = halves(jnp.concatenate(extras, axis=0))
    spread[k, pl.ds(MAIN, CELLS_A), at] = high
    spread[k, pl.ds(MAIN, CELLS_A), low_at] = low


def deposit_kernel(
    charges_hbm, anchors_hbm, weights_hbm, table_hbm, spectrum_hbm, out_ref, *rest
):
    sent_refs = rest[:ROWS]
    charges_ref, anchors_ref, weights_ref, table_ref, spectrum_ref = rest[ROWS : ROWS + 5]
    scaled, spread, lines, sem = rest[ROWS + 5 :]
    pairs = (
        (weights_hbm, weights_ref),
        (anchors_hbm, anchors_ref),
        (charges_hbm, charges_ref),
        (spectrum_hbm.at[pl.ds(0, CELLS_B * KEPT), pl.ds(0, LANES)], spectrum_ref.at[0]),
        (spectrum_hbm.at[pl.ds(0, CELLS_B * KEPT), pl.ds(LANES, LANES)], spectrum_ref.at[1]),
        (table_hbm, table_ref),
    )
    copies = [pltpu.make_async_copy(a, b, sem.at[n]) for n, (a, b) in enumerate(pairs)]
    for copy in copies:
        copy.start()
    for copy in copies:
        copy.wait()
    scaled[...] = weights_ref[...] * charges_ref[...]
    places = [local_place(anchors_ref, pl.ds(tile * LANES, LANES)) for tile in range(TILES)]
    hot = onehot(anchors_ref)
    hot = jnp.concatenate([hot, hot], axis=1)
    total = None
    for k in (1, 2, 3, 0):
        for tile in range(TILES):
            spread_tile(scaled, places[tile], spread, k, tile)
        placed = dot(spread[k], hot, ((1,), (1,)))
        placed = pltpu.roll(placed, k, 1) if k else placed
        total = placed if total is None else total + placed
    for block in range(LINES_B + 1):
        lines[block_place(block), :] = total[CELLS_A * block : CELLS_A * (block + 1)]
    lines[block_place(LINES_B + 1), :] = jnp.zeros((CELLS_A, G), F32)
    result = dot_split((table_ref[0], table_ref[1]), halves(lines[...]), ((1,), (1,)))
    for v in range(3):
        out_ref[pl.ds(v, G, stride=3), :] = result[:, LANES * v : LANES * (v + 1)]
    for shift, sent in enumerate(sent_refs):
        c = (lax.axis_index("row") + shift) & (ROWS - 1)
        sent[pl.ds(SENT - 8, 8), :] = jnp.zeros((8, LANES), F32)
        for half in range(2):
            rows = spectrum_ref[half, pl.ds(c, KEPT, stride=CELLS_B), :]
            sent[pl.ds(half * KEPT, KEPT), :] = rows
    for shift in (1, ROWS - 1):
        for block in range(8):
            at = pl.ds(block * LANES, LANES)
            sent_refs[shift][pl.ds(SENT + block, 1), :] = charges_ref[:, at]


def spectrum_kernel(charges_ref, chosen_hbm, *rest):
    tables_hbm, sent_refs = rest[:4], rest[4 : 4 + ROWS]
    out_ref, beside_ref = rest[4 + ROWS : 6 + ROWS]
    staged, (chosen_ref, joined, sem) = rest[6 + ROWS : 10 + ROWS], rest[10 + ROWS :]
    pairs = [(chosen_hbm, chosen_ref), *zip(tables_hbm, staged)]
    copies = [pltpu.make_async_copy(a, b, sem.at[n]) for n, (a, b) in enumerate(pairs)]
    for copy in copies:
        copy.start()
    for shift, sent in enumerate(sent_refs):
        owner = (lax.axis_index("row") - shift) & (ROWS - 1)
        at = pl.ds(pl.multiple_of(owner * SENT, 8), SENT)
        joined[at, :] = sent[pl.ds(0, SENT), :]
    beside_ref[pl.ds(0, 8), :] = sent_refs[1][pl.ds(SENT, 8), :]
    beside_ref[pl.ds(8, 8), :] = charges_ref[...]
    beside_ref[pl.ds(16, 8), :] = sent_refs[ROWS - 1][pl.ds(SENT, 8), :]
    for copy in copies:
        copy.wait()
    parts = thirds(joined[...])
    for half in range(2):
        value = sum(dot(chosen_ref[half], part) for part in parts)
        out_ref[:, pl.ds(LANES * half, LANES)] = value * (1.0 / (G * G * G))


def plane_kernel(tiles_ref, spectrum_ref, first_ref, outer_ref, second_ref, flipped_ref, out_ref):
    lane = lax.broadcasted_iota(jnp.int32, (CELLS_A, LANES), 1)
    slots = [(lane >> 5) == s for s in range(4)]
    wide = lax.broadcasted_iota(jnp.int32, (CELLS_A, G), 1)
    pairs = [((wide & 31) >> 1) == line for line in range(LINES_B)]
    pieces = [
        [tiles_ref[pl.ds(96 * r + v, CELLS_A, stride=3), :] for v in range(3)] for r in range(ROWS)
    ]

    def joined(block):
        parts = []
        for w in range(2):
            value = None
            for s in range(4):
                piece = pieces[4 * w + s][block // 4]
                value = piece if value is None else jnp.where(slots[(block + s) & 3], piece, value)
            parts.append(value)
        return jnp.concatenate(parts, axis=1)

    def table(m):
        order = [row_at(slot, m) for slot in range(ROWS)]
        both = []
        for part in range(2):
            rows = [first_ref[part, pl.ds(CELLS_A * r, CELLS_A), :] for r in order]
            both.append(jnp.concatenate([*rows, outer_ref[part]], axis=0))
        return both

    rim = joined(LINES_B)
    half = []
    for m, group in enumerate(GROUPS):
        rows = [
            jnp.concatenate([joined(line), jnp.where(pairs[line], rim, 0.0)], axis=1)
            for line in group
        ]
        half.append(dot_split(halves(jnp.concatenate(rows, axis=0)), table(m)))
    half = jnp.concatenate(half, axis=0)
    image = dot_split((second_ref[0], second_ref[1]), halves(half)) * spectrum_ref[...]
    half = dot_split((flipped_ref[0], flipped_ref[1]), halves(image))
    blocks, at = {}, 0
    for m, group in enumerate(GROUPS):
        size = CELLS_A * len(group)
        value = dot_split(halves(half[at : at + size]), table(m), ((1,), (1,)))
        for place, line in enumerate(group):
            blocks[line] = value[CELLS_A * place : CELLS_A * (place + 1)]
        at += size
    zero = jnp.zeros((CELLS_A, G), F32)
    rim = zero
    for line in range(LINES_B):
        rim = jnp.where(pairs[line], blocks[line][:, G:], rim)
    blocks[LINES_B], blocks[LINES_B + 1] = rim, zero
    for r in range(ROWS):
        lanes = slice(LANES * (r // 4), LANES * (r // 4 + 1))
        for v in range(3):
            value = None
            for block in range(4 * v, 4 * v + 4):
                piece = blocks[block][:, lanes]
                value = piece if value is None else jnp.where(slots[(block + r) & 3], piece, value)
            out_ref[pl.ds(96 * r + v, CELLS_A, stride=3), :] = value


def gather_tile(weights_ref, place, picked, tile, base, at):
    near_masks, next_masks, groups, bits = masks_of(place)
    weights_at = pl.ds(tile * LANES, LANES)
    total = jnp.zeros((8, LANES), F32)
    for k in range(4):
        blocks = []
        for line in range(LINES_B):
            start = SPREAD * k + CELLS_A * line
            rows = [picked[base, pl.ds(start + 8 * v, 8), at] for v in range(4)]
            last = picked[base, pl.ds(SPREAD * k + MAIN + 8 * (line // 4), 8), at]
            rows.append(pltpu.roll(last, 8 - 2 * (line % 4), 0) if line % 4 else last)
            pair = []
            for skip in range(2):
                chosen = rows[skip]
                for g in range(1, 4):
                    chosen = jnp.where(groups[g], rows[g + skip], chosen)
                pair.append(chosen)
            blocks.append(pair)
        for mask, shift, count in zip(bits[::-1], (4, 2, 1), (7, 5, 4)):
            fewer = []
            for line in range(count):
                low = blocks[line]
                if line + shift < len(blocks):
                    high = blocks[line + shift]
                    low = [jnp.where(mask, h, l) for h, l in zip(high, low)]
                fewer.append(low)
            blocks = fewer
        for j in range(4):
            rows = stencil_rows(weights_ref, j, k, weights_at)
            near, after = two_rows(rows, near_masks, next_masks)
            total = total + (near * blocks[j][0] + after * blocks[j][1])
    return jnp.sum(total, axis=0, keepdims=True)


def gather_kernel(
    field_ref, anchors_ref, weights_ref, table_ref, near_ref, out_ref, lines, parts, picked
):
    turned = [field_ref[pl.ds(v, G, stride=3), :].T for v in range(3)]
    turned = halves(jnp.concatenate(turned, axis=0))
    lines[...] = dot_split(turned, (table_ref[0], table_ref[1]))
    field = jnp.concatenate([lines[block_place(b), :] for b in range(LINES_B + 1)], axis=0)
    for k in range(4):
        high, low = halves(pltpu.roll(field, G - k, 1) if k else field)
        parts[pl.ds(SPREAD * k, SPREAD), pl.ds(0, G)] = high
        parts[pl.ds(SPREAD * k, SPREAD), pl.ds(G, G)] = low
    hot = onehot(anchors_ref)
    hot = jnp.concatenate([hot, hot], axis=0)
    for chunk in range(TRI // CHUNK):
        picked[chunk] = dot(parts[...], hot[:, CHUNK * chunk : CHUNK * (chunk + 1)])
        for step in range(CHUNK // LANES):
            tile = chunk * (CHUNK // LANES) + step
            at = pl.ds(tile * LANES, LANES)
            place = local_place(anchors_ref, at)
            value = gather_tile(
                weights_ref, place, picked, tile, chunk, pl.ds(step * LANES, LANES)
            )
            out_ref[:, at] = value + near_ref[:, at]


def near_kernel(
    count_ref, target_ref, source_ref, before_ref, own_ref, after_ref, tiles_ref, out_ref,
    charges_ref, total,
):
    step = pl.program_id(0)
    per_step, size = tiles_ref.shape[0], tiles_ref.shape[1]

    @pl.when(step == 0)
    def _():
        total[...] = jnp.zeros_like(total)
        for place, ref in enumerate((before_ref, own_ref, after_ref)):
            charges_ref[pl.ds(24 * place, 24), :] = ref[...]

    def slot(u, carry):
        place = step * per_step + u
        rows = pl.ds(pl.multiple_of(target_ref[place] * size, size), size)
        code = source_ref[place]
        neighbour = code >> 3
        row = neighbour // 3
        line = 24 * (neighbour - 3 * row) + 8 * row + (code & 7)
        source = charges_ref[pl.ds(line, 1), :]
        total[rows, :] = total[rows, :] + tiles_ref[u] * source
        return carry

    lax.fori_loop(0, jnp.clip(count_ref[0] - step * per_step, 0, per_step), slot, 0)

    @pl.when(step == pl.num_programs(0) - 1)
    def _():
        ones = jnp.ones((8, size), BF16)
        result = sum(dot(ones, part, ((1,), (1,))) for part in thirds(total[...]))
        out_ref[...] = result[0:1]


def shifted(value, axis, by):
    size = lax.axis_size(axis)
    return lax.ppermute(value, axis, [(i, (i + by) % size) for i in range(size)])


def near_field(beside, near_count, near_target, near_source, near_tiles):
    slots, size, _ = near_tiles.shape
    before, after = shifted(beside, "col", 1), shifted(beside, "col", -1)
    per_step = 8
    smem = pl.BlockSpec(memory_space=pltpu.SMEM)
    return pl.pallas_call(
        near_kernel,
        grid=(slots // per_step,),
        in_specs=[
            smem,
            smem,
            smem,
            *[pl.BlockSpec((24, size), lambda step: (0, 0))] * 3,
            pl.BlockSpec((per_step, size, size), lambda step: (step, 0, 0)),
        ],
        out_specs=pl.BlockSpec((1, TRI), lambda step: (0, 0)),
        out_shape=jax.ShapeDtypeStruct((1, TRI), F32),
        scratch_shapes=[pltpu.VMEM((72, size), F32), pltpu.VMEM((TRI, size), F32)],
        compiler_params=PARAMS,
        name="near",
    )(near_count, near_target, near_source, before, beside, after, near_tiles)


def exchange(values, axes, pieces):
    shaped = values.reshape(pieces, 1, values.size // pieces)
    moved = lax.all_to_all(shaped, axes, split_axis=0, concat_axis=0, tiled=True)
    return moved.reshape(values.shape)


def local(
    charges,
    anchors,
    stencil_weights,
    kernel_spectrum,
    near_count,
    near_target,
    near_source,
    near_tiles,
):
    table = {name: jnp.asarray(value) for name, value in tables().items()}
    devices = ROWS * COLS
    packed = jax.ShapeDtypeStruct((devices * LINES // LANES, LANES), F32)
    hbm = pl.BlockSpec(memory_space=pltpu.HBM)
    sizes = [SENT + 8 if shift in (1, ROWS - 1) else SENT for shift in range(ROWS)]
    deposited, *sent = pl.pallas_call(
        deposit_kernel,
        out_shape=(packed, *[jax.ShapeDtypeStruct((size, LANES), F32) for size in sizes]),
        in_specs=[hbm] * 5,
        scratch_shapes=[
            pltpu.VMEM((1, TRI), F32),
            pltpu.VMEM((3, TRI), jnp.int32),
            pltpu.VMEM((64, TRI), F32),
            pltpu.VMEM((2, G, G), BF16),
            pltpu.VMEM((2, CELLS_B * KEPT, LANES), F32),
            pltpu.VMEM((64, TRI), F32),
            pltpu.VMEM((4, SPREAD, 2 * TRI), BF16),
            pltpu.VMEM((LINES, G), F32),
            pltpu.SemaphoreType.DMA((6,)),
        ],
        compiler_params=PARAMS,
        name="deposit",
    )(
        *[
            pltpu.with_memory_space_constraint(value, pltpu.HBM)
            for value in (
                charges.reshape(1, TRI),
                anchors,
                stencil_weights,
                table["lines"],
                kernel_spectrum.reshape(CELLS_A * CELLS_B, G),
            )
        ]
    )
    received = exchange(deposited, BOTH, devices)
    sent = [shifted(value, "row", shift) if shift else value for shift, value in enumerate(sent)]
    vmem = pl.BlockSpec(memory_space=pltpu.VMEM)
    names = ("first", "outer", "second", "flipped")
    spectrum, beside, *staged = pl.pallas_call(
        spectrum_kernel,
        out_shape=(
            jax.ShapeDtypeStruct((G, G), F32),
            jax.ShapeDtypeStruct((24, LANES), F32),
            *[jax.ShapeDtypeStruct(table[name].shape, BF16) for name in names],
        ),
        in_specs=[vmem, *[hbm] * 5, *[vmem] * ROWS],
        scratch_shapes=[
            pltpu.VMEM(table["chosen"].shape, BF16),
            pltpu.VMEM((ROWS * SENT, LANES), F32),
            pltpu.SemaphoreType.DMA((5,)),
        ],
        compiler_params=PARAMS,
        name="spectrum",
    )(
        charges.reshape(8, LANES),
        *[
            pltpu.with_memory_space_constraint(table[name], pltpu.HBM)
            for name in ("chosen", *names)
        ],
        *sent,
    )
    handed = pl.pallas_call(
        plane_kernel, out_shape=packed, compiler_params=PARAMS, name="plane"
    )(received, spectrum, *staged)
    field = exchange(handed, BOTH, devices)
    beside, _ = lax.optimization_barrier((beside, handed))
    near = near_field(beside, near_count, near_target, near_source, near_tiles)
    result = pl.pallas_call(
        gather_kernel,
        out_shape=jax.ShapeDtypeStruct((1, TRI), F32),
        scratch_shapes=[
            pltpu.VMEM((LINES, G), F32),
            pltpu.VMEM((4 * SPREAD, 2 * G), BF16),
            pltpu.VMEM((TRI // CHUNK, 4 * SPREAD, CHUNK), F32),
        ],
        compiler_params=PARAMS,
        name="gather",
    )(field, anchors, stencil_weights, table["lines"], near)
    return result.reshape(TRI)


def solution(mesh):
    return jax.shard_map(
        local,
        mesh=mesh,
        in_specs=(
            P(("row", "col")),
            P(None, ("row", "col")),
            P(None, ("row", "col")),
            P("row", "col", None),
            P(("row", "col")),
            P(("row", "col")),
            P(("row", "col")),
            P(("row", "col"), None, None),
        ),
        out_specs=P(("row", "col")),
        check_vma=False,
    )
```

```python
import jax
import jax.numpy as jnp
import ml_dtypes
import numpy as np
from jax import lax
from jax.experimental import pallas as pl
from jax.experimental.pallas import tpu as pltpu
from jax.sharding import PartitionSpec as P

G = 256
ROWS = 8
COLS = 32
CELLS_A = 32
CELLS_B = 8
TRI = 1024
LINES_B = 10
MAIN = LINES_B * CELLS_A
BLOCKS = 12
LINES = BLOCKS * CELLS_A
SPREAD = MAIN + CELLS_A
LANES = 128
TILES = TRI // LANES
KEPT = CELLS_A // 2 + 1
SENT = 40
CHUNK = 256
GROUPS = ((0, 4, 8), (1, 5, 9), (2, 6), (3, 7))
F32 = jnp.float32
BF16 = jnp.bfloat16
BOTH = ("row", "col")


def params(mebibytes):
    return pltpu.CompilerParams(vmem_limit_bytes=mebibytes * 1024 * 1024)


def split_table(table):
    high = table.astype(np.float32).astype(ml_dtypes.bfloat16)
    low = (table - high.astype(np.float64)).astype(np.float32).astype(ml_dtypes.bfloat16)
    return np.stack([high, low])


def cas(first, second):
    angle = (np.outer(first, second) % G) * (2.0 * np.pi / G)
    return np.cos(angle) + np.sin(angle)


def row_at(slot, block):
    return 4 * (slot // 4) + (slot - block) % 4


def tables():
    steps = np.arange(G)
    device = np.arange(ROWS * COLS)
    plane = CELLS_B * (device % COLS) + device // COLS
    along_a = (np.arange(G) - 1) % G
    order = np.concatenate([
        (CELLS_B * np.arange(COLS) - 1 + line) % G for group in GROUPS for line in group
    ])
    outer = np.zeros((G, G))
    for slot in range(ROWS):
        row = row_at(slot, LINES_B)
        for extra in range(2):
            cell = (CELLS_A * (row + 1) - 1 + extra) % G
            for line in range(LINES_B):
                outer[CELLS_A * slot + 2 * line + extra] = cas(np.array([cell]), steps)[0]
    second = cas(steps, order)
    return {
        "lines": split_table(cas(plane, steps)),
        "first": split_table(cas(along_a, steps)),
        "outer": split_table(outer),
        "second": split_table(second),
        "flipped": split_table(second.T),
    }


def halves(value):
    high = value.astype(BF16)
    low = (value - high.astype(F32)).astype(BF16)
    return high, low


def thirds(value):
    parts = []
    for _ in range(3):
        parts.append(value.astype(BF16))
        value = value - parts[-1].astype(F32)
    return parts


def dot(left, right, dims=((1,), (0,))):
    return lax.dot_general(left, right, (dims, ((), ())), preferred_element_type=F32)


def dot_split(left, right, dims=((1,), (0,))):
    left_high, left_low = left
    right_high, right_low = right
    cross = dot(left_high, right_low, dims) + dot(left_low, right_high, dims)
    return dot(left_high, right_high, dims) + cross


def block_place(block):
    slot = (lax.axis_index("row") + block) & 3
    return pl.ds(pl.multiple_of(LANES * (block // 4) + CELLS_A * slot, CELLS_A), CELLS_A)


def onehot(anchors_ref):
    cells = lax.broadcasted_iota(jnp.int32, (G, TRI), 0)
    matched = cells == anchors_ref[2:3, :]
    return jnp.where(matched, 1.0, 0.0).astype(BF16)


def local_place(anchors_ref, at):
    first = (anchors_ref[0:1, at] - (lax.axis_index("row") * CELLS_A - 1)) & (G - 1)
    second = (anchors_ref[1:2, at] - (lax.axis_index("col") * CELLS_B - 1)) & (G - 1)
    first = jnp.broadcast_to(first, (8, LANES))
    second = jnp.broadcast_to(second, (8, LANES))
    return lax.broadcasted_iota(jnp.int32, (8, LANES), 0) - (first & 7), first >> 3, second


def masks_of(place):
    relative, group, second = place
    near_masks = [relative == i for i in range(4)]
    next_masks = [relative == i - 8 for i in range(1, 4)]
    groups = [group == g for g in range(4)]
    bits = [(second & bit) != 0 for bit in (1, 2, 4)]
    return near_masks, next_masks, groups, bits


def two_rows(rows, near_masks, next_masks):
    near = jnp.zeros((8, LANES), F32)
    after = jnp.zeros((8, LANES), F32)
    for i in range(4):
        near = jnp.where(near_masks[i], rows[i], near)
    for i in range(1, 4):
        after = jnp.where(next_masks[i - 1], rows[i], after)
    return near, after


def stencil_rows(ref, j, k, at):
    return [
        jnp.broadcast_to(ref[16 * i + 4 * j + k, at][None, :], (8, LANES)) for i in range(4)
    ]


def spread_tile(scaled, place, spread, k, tile):
    at = pl.ds(tile * LANES, LANES)
    low_at = pl.ds(TRI + tile * LANES, LANES)
    zero = jnp.zeros((8, LANES), F32)
    near_masks, next_masks, groups, bits = masks_of(place)
    blocks = [two_rows(stencil_rows(scaled, j, k, at), near_masks, next_masks) for j in range(4)]
    for mask, shift, count in zip(bits, (1, 2, 4), (5, 7, 10)):
        wider = []
        for line in range(count):
            if line < shift:
                wider.append([jnp.where(mask, zero, low) for low in blocks[line]])
            elif line >= len(blocks):
                wider.append([jnp.where(mask, high, zero) for high in blocks[line - shift]])
            else:
                pairs = zip(blocks[line - shift], blocks[line])
                wider.append([jnp.where(mask, high, low) for high, low in pairs])
        blocks = wider
    extras = [zero] * 4
    for line in range(LINES_B):
        near, after = blocks[line]
        pieces = []
        for v in range(4):
            piece = jnp.where(groups[v], near, zero)
            pieces.append(jnp.where(groups[v - 1], after, piece) if v else piece)
        high, low = halves(jnp.concatenate(pieces, axis=0))
        rows = pl.ds(CELLS_A * line, CELLS_A)
        spread[k, rows, at] = high
        spread[k, rows, low_at] = low
        last = jnp.where(groups[3], after, zero)
        if line % 4:
            last = extras[line // 4] + pltpu.roll(last, 2 * (line % 4), 0)
        extras[line // 4] = last
    high, low = halves(jnp.concatenate(extras, axis=0))
    spread[k, pl.ds(MAIN, CELLS_A), at] = high
    spread[k, pl.ds(MAIN, CELLS_A), low_at] = low


def deposit_kernel(
    charges_hbm, anchors_hbm, weights_hbm, table_hbm, spectrum_hbm, out_ref, *rest
):
    sent_refs = rest[:ROWS]
    charges_ref, anchors_ref, weights_ref, table_ref, spectrum_ref = rest[ROWS : ROWS + 5]
    scaled, spread, lines, sem = rest[ROWS + 5 :]
    pairs = (
        (weights_hbm, weights_ref),
        (anchors_hbm, anchors_ref),
        (charges_hbm, charges_ref),
        (spectrum_hbm.at[pl.ds(0, CELLS_B * KEPT), pl.ds(0, LANES)], spectrum_ref.at[0]),
        (spectrum_hbm.at[pl.ds(0, CELLS_B * KEPT), pl.ds(LANES, LANES)], spectrum_ref.at[1]),
        (table_hbm, table_ref),
    )
    copies = [pltpu.make_async_copy(a, b, sem.at[n]) for n, (a, b) in enumerate(pairs)]
    for copy in copies:
        copy.start()
    for copy in copies:
        copy.wait()
    scaled[...] = weights_ref[...] * charges_ref[...]
    places = [local_place(anchors_ref, pl.ds(tile * LANES, LANES)) for tile in range(TILES)]
    hot = onehot(anchors_ref)
    hot = jnp.concatenate([hot, hot], axis=1)
    total = None
    for k in (1, 2, 3, 0):
        for tile in range(TILES):
            spread_tile(scaled, places[tile], spread, k, tile)
        placed = dot(spread[k], hot, ((1,), (1,)))
        placed = pltpu.roll(placed, k, 1) if k else placed
        total = placed if total is None else total + placed
    for block in range(LINES_B + 1):
        lines[block_place(block), :] = total[CELLS_A * block : CELLS_A * (block + 1)]
    lines[block_place(LINES_B + 1), :] = jnp.zeros((CELLS_A, G), F32)
    result = dot_split((table_ref[0], table_ref[1]), halves(lines[...]), ((1,), (1,)))
    for v in range(3):
        out_ref[pl.ds(v, G, stride=3), :] = result[:, LANES * v : LANES * (v + 1)]
    for shift, sent in enumerate(sent_refs):
        c = (lax.axis_index("row") + shift) & (ROWS - 1)
        sent[pl.ds(SENT - 8, 8), :] = jnp.zeros((8, LANES), F32)
        for half in range(2):
            rows = spectrum_ref[half, pl.ds(c, KEPT, stride=CELLS_B), :]
            sent[pl.ds(half * KEPT, KEPT), :] = rows
    for shift in (0, 1, ROWS - 1):
        for block in range(8):
            at = pl.ds(block * LANES, LANES)
            sent_refs[shift][pl.ds(SENT + block, 1), :] = charges_ref[:, at]


def spectrum_kernel(*refs):
    sent_refs, (out_ref, beside_ref, joined) = refs[:ROWS], refs[ROWS:]
    for shift, sent in enumerate(sent_refs):
        owner = (lax.axis_index("row") - shift) & (ROWS - 1)
        at = pl.ds(pl.multiple_of(owner * SENT, 8), SENT)
        joined[at, :] = sent[pl.ds(0, SENT), :]
    for place, shift in enumerate((1, 0, ROWS - 1)):
        beside_ref[pl.ds(8 * place, 8), :] = sent_refs[shift][pl.ds(SENT, 8), :]
    line = lax.broadcasted_iota(jnp.int32, (G, ROWS * SENT), 0)
    folded = jnp.minimum(line, G - line)
    block, inside = folded >> 5, folded & (CELLS_A - 1)
    mirrored = inside >= KEPT
    owner = jnp.where(mirrored, ROWS - 1 - block, block)
    inside = jnp.where(mirrored, CELLS_A - inside, inside)
    place = lax.broadcasted_iota(jnp.int32, (G, ROWS * SENT), 1) - (owner * SENT + inside)
    parts = thirds(joined[...])
    for half in range(2):
        chosen = jnp.where(place == half * KEPT, 1.0, 0.0).astype(BF16)
        value = sum(dot(chosen, part) for part in parts)
        out_ref[:, pl.ds(LANES * half, LANES)] = value * (1.0 / (G * G * G))


def plane_kernel(tiles_ref, spectrum_ref, *rest):
    tables_hbm, out_ref, tables_ref, sem = rest[:4], rest[4], rest[5:9], rest[9]
    first_ref, outer_ref, second_ref, flipped_ref = tables_ref
    copies = [
        pltpu.make_async_copy(a, b, sem.at[n]) for n, (a, b) in enumerate(zip(tables_hbm, tables_ref))
    ]
    for copy in copies:
        copy.start()
    lane = lax.broadcasted_iota(jnp.int32, (CELLS_A, LANES), 1)
    slots = [(lane >> 5) == s for s in range(4)]
    wide = lax.broadcasted_iota(jnp.int32, (CELLS_A, G), 1)
    pairs = [((wide & 31) >> 1) == line for line in range(LINES_B)]
    pieces = [
        [tiles_ref[pl.ds(96 * r + v, CELLS_A, stride=3), :] for v in range(3)] for r in range(ROWS)
    ]

    def joined(block):
        parts = []
        for w in range(2):
            value = None
            for s in range(4):
                piece = pieces[4 * w + s][block // 4]
                value = piece if value is None else jnp.where(slots[(block + s) & 3], piece, value)
            parts.append(value)
        return jnp.concatenate(parts, axis=1)

    def table(m):
        order = [row_at(slot, m) for slot in range(ROWS)]
        both = []
        for part in range(2):
            rows = [first_ref[part, pl.ds(CELLS_A * r, CELLS_A), :] for r in order]
            both.append(jnp.concatenate([*rows, outer_ref[part]], axis=0))
        return both

    rim = joined(LINES_B)
    half = []
    for group in GROUPS:
        rows = [
            jnp.concatenate([joined(line), jnp.where(pairs[line], rim, 0.0)], axis=1)
            for line in group
        ]
        half.append(halves(jnp.concatenate(rows, axis=0)))
    copies[0].wait()
    copies[1].wait()
    half = [dot_split(rows, table(m)) for m, rows in enumerate(half)]
    half = halves(jnp.concatenate(half, axis=0))
    copies[2].wait()
    image = dot_split((second_ref[0], second_ref[1]), half) * spectrum_ref[...]
    copies[3].wait()
    half = dot_split((flipped_ref[0], flipped_ref[1]), halves(image))
    blocks, at = {}, 0
    for m, group in enumerate(GROUPS):
        size = CELLS_A * len(group)
        value = dot_split(halves(half[at : at + size]), table(m), ((1,), (1,)))
        for place, line in enumerate(group):
            blocks[line] = value[CELLS_A * place : CELLS_A * (place + 1)]
        at += size
    zero = jnp.zeros((CELLS_A, G), F32)
    rim = zero
    for line in range(LINES_B):
        rim = jnp.where(pairs[line], blocks[line][:, G:], rim)
    blocks[LINES_B], blocks[LINES_B + 1] = rim, zero
    for r in range(ROWS):
        lanes = slice(LANES * (r // 4), LANES * (r // 4 + 1))
        for v in range(3):
            value = None
            for block in range(4 * v, 4 * v + 4):
                piece = blocks[block][:, lanes]
                value = piece if value is None else jnp.where(slots[(block + r) & 3], piece, value)
            out_ref[pl.ds(96 * r + v, CELLS_A, stride=3), :] = value


def gather_tile(weights_ref, place, picked, tile, base, at):
    near_masks, next_masks, groups, bits = masks_of(place)
    weights_at = pl.ds(tile * LANES, LANES)
    total = jnp.zeros((8, LANES), F32)
    for k in range(4):
        blocks = []
        for line in range(LINES_B):
            start = SPREAD * k + CELLS_A * line
            rows = [picked[base, pl.ds(start + 8 * v, 8), at] for v in range(4)]
            last = picked[base, pl.ds(SPREAD * k + MAIN + 8 * (line // 4), 8), at]
            rows.append(pltpu.roll(last, 8 - 2 * (line % 4), 0) if line % 4 else last)
            pair = []
            for skip in range(2):
                chosen = rows[skip]
                for g in range(1, 4):
                    chosen = jnp.where(groups[g], rows[g + skip], chosen)
                pair.append(chosen)
            blocks.append(pair)
        for mask, shift, count in zip(bits[::-1], (4, 2, 1), (7, 5, 4)):
            fewer = []
            for line in range(count):
                low = blocks[line]
                if line + shift < len(blocks):
                    high = blocks[line + shift]
                    low = [jnp.where(mask, h, l) for h, l in zip(high, low)]
                fewer.append(low)
            blocks = fewer
        for j in range(4):
            rows = stencil_rows(weights_ref, j, k, weights_at)
            near, after = two_rows(rows, near_masks, next_masks)
            total = total + (near * blocks[j][0] + after * blocks[j][1])
    return jnp.sum(total, axis=0, keepdims=True)


def gather_kernel(
    field_ref, anchors_ref, weights_ref, table_ref, near_ref, out_ref, lines, parts, picked
):
    turned = [field_ref[pl.ds(v, G, stride=3), :].T for v in range(3)]
    turned = halves(jnp.concatenate(turned, axis=0))
    lines[...] = dot_split(turned, (table_ref[0], table_ref[1]))
    field = jnp.concatenate([lines[block_place(b), :] for b in range(LINES_B + 1)], axis=0)
    for k in range(4):
        high, low = halves(pltpu.roll(field, G - k, 1) if k else field)
        parts[pl.ds(SPREAD * k, SPREAD), pl.ds(0, G)] = high
        parts[pl.ds(SPREAD * k, SPREAD), pl.ds(G, G)] = low
    hot = onehot(anchors_ref)
    hot = jnp.concatenate([hot, hot], axis=0)
    for chunk in range(TRI // CHUNK):
        picked[chunk] = dot(parts[...], hot[:, CHUNK * chunk : CHUNK * (chunk + 1)])
        for step in range(CHUNK // LANES):
            tile = chunk * (CHUNK // LANES) + step
            at = pl.ds(tile * LANES, LANES)
            place = local_place(anchors_ref, at)
            value = gather_tile(
                weights_ref, place, picked, tile, chunk, pl.ds(step * LANES, LANES)
            )
            out_ref[:, at] = value + near_ref[:, at]


def near_kernel(
    count_ref, target_ref, source_ref, before_ref, own_ref, after_ref, tiles_ref, out_ref,
    charges_ref, total,
):
    step = pl.program_id(0)
    per_step, size = tiles_ref.shape[0], tiles_ref.shape[1]

    @pl.when(step == 0)
    def _():
        total[...] = jnp.zeros_like(total)
        for place, ref in enumerate((before_ref, own_ref, after_ref)):
            charges_ref[pl.ds(24 * place, 24), :] = ref[...]

    def slot(u, carry):
        place = step * per_step + u
        rows = pl.ds(pl.multiple_of(target_ref[place] * size, size), size)
        code = source_ref[place]
        neighbour = code >> 3
        row = neighbour // 3
        line = 24 * (neighbour - 3 * row) + 8 * row + (code & 7)
        source = charges_ref[pl.ds(line, 1), :]
        total[rows, :] = total[rows, :] + tiles_ref[u] * source
        return carry

    lax.fori_loop(0, jnp.clip(count_ref[0] - step * per_step, 0, per_step), slot, 0)

    @pl.when(step == pl.num_programs(0) - 1)
    def _():
        ones = jnp.ones((8, size), BF16)
        result = sum(dot(ones, part, ((1,), (1,))) for part in thirds(total[...]))
        out_ref[...] = result[0:1]


def shifted(value, axis, by):
    size = lax.axis_size(axis)
    return lax.ppermute(value, axis, [(i, (i + by) % size) for i in range(size)])


def near_field(beside, near_count, near_target, near_source, near_tiles):
    slots, size, _ = near_tiles.shape
    before, after = shifted(beside, "col", 1), shifted(beside, "col", -1)
    per_step = 8
    smem = pl.BlockSpec(memory_space=pltpu.SMEM)
    return pl.pallas_call(
        near_kernel,
        grid=(slots // per_step,),
        in_specs=[
            smem,
            smem,
            smem,
            *[pl.BlockSpec((24, size), lambda step: (0, 0))] * 3,
            pl.BlockSpec((per_step, size, size), lambda step: (step, 0, 0)),
        ],
        out_specs=pl.BlockSpec((1, TRI), lambda step: (0, 0)),
        out_shape=jax.ShapeDtypeStruct((1, TRI), F32),
        scratch_shapes=[pltpu.VMEM((72, size), F32), pltpu.VMEM((TRI, size), F32)],
        compiler_params=params(8),
        name="near",
    )(near_count, near_target, near_source, before, beside, after, near_tiles)


def exchange(values, axes, pieces):
    shaped = values.reshape(pieces, 1, values.size // pieces)
    moved = lax.all_to_all(shaped, axes, split_axis=0, concat_axis=0, tiled=True)
    return moved.reshape(values.shape)


def local(
    charges,
    anchors,
    stencil_weights,
    kernel_spectrum,
    near_count,
    near_target,
    near_source,
    near_tiles,
):
    table = {name: jnp.asarray(value) for name, value in tables().items()}
    devices = ROWS * COLS
    packed = jax.ShapeDtypeStruct((devices * LINES // LANES, LANES), F32)
    hbm = pl.BlockSpec(memory_space=pltpu.HBM)
    sizes = [SENT + 8 if shift in (0, 1, ROWS - 1) else SENT for shift in range(ROWS)]
    deposited, *sent = pl.pallas_call(
        deposit_kernel,
        out_shape=(packed, *[jax.ShapeDtypeStruct((size, LANES), F32) for size in sizes]),
        in_specs=[hbm] * 5,
        scratch_shapes=[
            pltpu.VMEM((1, TRI), F32),
            pltpu.VMEM((3, TRI), jnp.int32),
            pltpu.VMEM((64, TRI), F32),
            pltpu.VMEM((2, G, G), BF16),
            pltpu.VMEM((2, CELLS_B * KEPT, LANES), F32),
            pltpu.VMEM((64, TRI), F32),
            pltpu.VMEM((4, SPREAD, 2 * TRI), BF16),
            pltpu.VMEM((LINES, G), F32),
            pltpu.SemaphoreType.DMA((6,)),
        ],
        compiler_params=params(20),
        name="deposit",
    )(
        *[
            pltpu.with_memory_space_constraint(value, pltpu.HBM)
            for value in (
                charges.reshape(1, TRI),
                anchors,
                stencil_weights,
                table["lines"],
                kernel_spectrum.reshape(CELLS_A * CELLS_B, G),
            )
        ]
    )
    received = exchange(deposited, BOTH, devices)
    sent = [shifted(value, "row", shift) if shift else value for shift, value in enumerate(sent)]
    spectrum, beside = pl.pallas_call(
        spectrum_kernel,
        out_shape=(
            jax.ShapeDtypeStruct((G, G), F32),
            jax.ShapeDtypeStruct((24, LANES), F32),
        ),
        scratch_shapes=[pltpu.VMEM((ROWS * SENT, LANES), F32)],
        compiler_params=params(8),
        name="spectrum",
    )(*sent)
    names = ("first", "outer", "second", "flipped")
    vmem = pl.BlockSpec(memory_space=pltpu.VMEM)
    handed = pl.pallas_call(
        plane_kernel,
        out_shape=packed,
        in_specs=[vmem, vmem, *[hbm] * 4],
        scratch_shapes=[
            *[pltpu.VMEM(table[name].shape, BF16) for name in names],
            pltpu.SemaphoreType.DMA((4,)),
        ],
        compiler_params=params(12),
        name="plane",
    )(
        received,
        spectrum,
        *[pltpu.with_memory_space_constraint(table[name], pltpu.HBM) for name in names],
    )
    field = exchange(handed, BOTH, devices)
    beside, _ = lax.optimization_barrier((beside, handed))
    near = near_field(beside, near_count, near_target, near_source, near_tiles)
    result = pl.pallas_call(
        gather_kernel,
        out_shape=jax.ShapeDtypeStruct((1, TRI), F32),
        scratch_shapes=[
            pltpu.VMEM((LINES, G), F32),
            pltpu.VMEM((4 * SPREAD, 2 * G), BF16),
            pltpu.VMEM((TRI // CHUNK, 4 * SPREAD, CHUNK), F32),
        ],
        compiler_params=params(20),
        name="gather",
    )(field, anchors, stencil_weights, table["lines"], near)
    return result.reshape(TRI)


def solution(mesh):
    return jax.shard_map(
        local,
        mesh=mesh,
        in_specs=(
            P(("row", "col")),
            P(None, ("row", "col")),
            P(None, ("row", "col")),
            P("row", "col", None),
            P(("row", "col")),
            P(("row", "col")),
            P(("row", "col")),
            P(("row", "col"), None, None),
        ),
        out_specs=P(("row", "col")),
        check_vma=False,
    )
```

```python
import math

import jax
import jax.numpy as jnp
import ml_dtypes
import numpy as np
from jax import lax
from jax.experimental import pallas as pl
from jax.experimental.pallas import tpu as pltpu
from jax.sharding import PartitionSpec as P

G = 256
ROWS = 8
COLS = 32
CELLS_A = 32
CELLS_B = 8
TRI = 1024
LINES_B = 10
MAIN = LINES_B * CELLS_A
BLOCKS = 12
LINES = BLOCKS * CELLS_A
SPREAD = MAIN + CELLS_A
LANES = 128
TILES = TRI // LANES
KEPT = CELLS_A // 2 + 1
SENT = 40
CHUNK = 256
PART = 8
GROUPS = ((0, 4, 8), (1, 5, 9), (2, 6), (3, 7))
F32 = jnp.float32
BF16 = jnp.bfloat16
BOTH = ("row", "col")


def params(mebibytes):
    return pltpu.CompilerParams(vmem_limit_bytes=mebibytes * 1024 * 1024)


def split_table(table):
    high = table.astype(np.float32).astype(ml_dtypes.bfloat16)
    low = (table - high.astype(np.float64)).astype(np.float32).astype(ml_dtypes.bfloat16)
    return np.stack([high, low])


def cas(first, second):
    angle = (np.outer(first, second) % G) * (2.0 * np.pi / G)
    return np.cos(angle) + np.sin(angle)


def row_at(slot, block):
    return 4 * (slot // 4) + (slot - block) % 4


def line_table():
    steps = np.arange(G)
    device = np.arange(ROWS * COLS)
    plane = CELLS_B * (device % COLS) + device // COLS
    return split_table(cas(plane, steps))


def halves(value):
    high = value.astype(BF16)
    low = (value - high.astype(F32)).astype(BF16)
    return high, low


def thirds(value):
    parts = []
    for _ in range(3):
        parts.append(value.astype(BF16))
        value = value - parts[-1].astype(F32)
    return parts


def dot(left, right, dims=((1,), (0,))):
    return lax.dot_general(left, right, (dims, ((), ())), preferred_element_type=F32)


def dot_table(rows, table, dims=((1,), (0,))):
    high, low = rows
    size = high.shape[0]
    both = dot(jnp.concatenate([high, low], axis=0), table[0], dims)
    return both[:size] + (both[size:] + dot(high, table[1], dims))


def table_dot(table, value, dims=((1,), (0,))):
    high, low = value
    size = table[0].shape[0]
    both = dot(jnp.concatenate([table[0], table[1]], axis=0), high, dims)
    return both[:size] + (both[size:] + dot(table[0], low, dims))


def block_place(block):
    slot = (lax.axis_index("row") + block) & 3
    return pl.ds(pl.multiple_of(LANES * (block // 4) + CELLS_A * slot, CELLS_A), CELLS_A)


def onehot(anchors_ref):
    cells = lax.broadcasted_iota(jnp.int32, (G, TRI), 0)
    matched = cells == anchors_ref[2:3, :]
    return jnp.where(matched, 1.0, 0.0).astype(BF16)


def local_place(anchors_ref, at):
    first = (anchors_ref[0:1, at] - (lax.axis_index("row") * CELLS_A - 1)) & (G - 1)
    second = (anchors_ref[1:2, at] - (lax.axis_index("col") * CELLS_B - 1)) & (G - 1)
    first = jnp.broadcast_to(first, (8, LANES))
    second = jnp.broadcast_to(second, (8, LANES))
    return lax.broadcasted_iota(jnp.int32, (8, LANES), 0) - (first & 7), first >> 3, second


def masks_of(place):
    relative, group, second = place
    near_masks = [relative == i for i in range(4)]
    next_masks = [relative == i - 8 for i in range(1, 4)]
    groups = [group == g for g in range(4)]
    bits = [(second & bit) != 0 for bit in (1, 2, 4)]
    return near_masks, next_masks, groups, bits


def two_rows(rows, near_masks, next_masks):
    near = jnp.zeros((8, LANES), F32)
    after = jnp.zeros((8, LANES), F32)
    for i in range(4):
        near = jnp.where(near_masks[i], rows[i], near)
    for i in range(1, 4):
        after = jnp.where(next_masks[i - 1], rows[i], after)
    return near, after


def stencil_rows(ref, j, k, at):
    return [
        jnp.broadcast_to(ref[16 * i + 4 * j + k, at][None, :], (8, LANES)) for i in range(4)
    ]


def spread_tile(scaled, place, spread, k, tile):
    at = pl.ds(tile * LANES, LANES)
    low_at = pl.ds(TRI + tile * LANES, LANES)
    zero = jnp.zeros((8, LANES), F32)
    near_masks, next_masks, groups, bits = masks_of(place)
    blocks = [two_rows(stencil_rows(scaled, j, k, at), near_masks, next_masks) for j in range(4)]
    for mask, shift, count in zip(bits, (1, 2, 4), (5, 7, 10)):
        wider = []
        for line in range(count):
            if line < shift:
                wider.append([jnp.where(mask, zero, low) for low in blocks[line]])
            elif line >= len(blocks):
                wider.append([jnp.where(mask, high, zero) for high in blocks[line - shift]])
            else:
                pairs = zip(blocks[line - shift], blocks[line])
                wider.append([jnp.where(mask, high, low) for high, low in pairs])
        blocks = wider
    extras = [zero] * 4
    for line in range(LINES_B):
        near, after = blocks[line]
        pieces = []
        for v in range(4):
            piece = jnp.where(groups[v], near, zero)
            pieces.append(jnp.where(groups[v - 1], after, piece) if v else piece)
        high, low = halves(jnp.concatenate(pieces, axis=0))
        rows = pl.ds(CELLS_A * line, CELLS_A)
        spread[k, rows, at] = high
        spread[k, rows, low_at] = low
        last = jnp.where(groups[3], after, zero)
        if line % 4:
            last = extras[line // 4] + pltpu.roll(last, 2 * (line % 4), 0)
        extras[line // 4] = last
    high, low = halves(jnp.concatenate(extras, axis=0))
    spread[k, pl.ds(MAIN, CELLS_A), at] = high
    spread[k, pl.ds(MAIN, CELLS_A), low_at] = low


def deposit_kernel(
    charges_hbm, anchors_hbm, weights_hbm, table_hbm, spectrum_hbm, out_ref, *rest
):
    sent_refs = rest[:ROWS]
    charges_ref, anchors_ref, weights_ref, table_ref, spectrum_ref = rest[ROWS : ROWS + 5]
    scaled, spread, lines, sem = rest[ROWS + 5 :]
    pairs = (
        (weights_hbm, weights_ref),
        (anchors_hbm, anchors_ref),
        (charges_hbm, charges_ref),
        (spectrum_hbm.at[pl.ds(0, CELLS_B * KEPT), pl.ds(0, LANES)], spectrum_ref.at[0]),
        (spectrum_hbm.at[pl.ds(0, CELLS_B * KEPT), pl.ds(LANES, LANES)], spectrum_ref.at[1]),
        (table_hbm, table_ref),
    )
    copies = [pltpu.make_async_copy(a, b, sem.at[n]) for n, (a, b) in enumerate(pairs)]
    for copy in copies:
        copy.start()
    for copy in copies[:3]:
        copy.wait()
    scaled[...] = weights_ref[...] * charges_ref[...]
    places = [local_place(anchors_ref, pl.ds(tile * LANES, LANES)) for tile in range(TILES)]
    cells = lax.broadcasted_iota(jnp.int32, (LANES, G), 1)
    hot = []
    for tile in range(TILES):
        row = anchors_ref[2:3, pl.ds(tile * LANES, LANES)]
        column = jnp.broadcast_to(row, (LANES, LANES)).T
        column = jnp.concatenate([column, column], axis=1)
        hot.append(jnp.where(cells == column, 1.0, 0.0).astype(BF16))
    hot = jnp.concatenate(hot + hot, axis=0)
    total = None
    for k in (1, 2, 3, 0):
        for tile in range(TILES):
            spread_tile(scaled, places[tile], spread, k, tile)
        placed = dot(spread[k], hot)
        placed = pltpu.roll(placed, k, 1) if k else placed
        total = placed if total is None else total + placed
    for block in range(LINES_B + 1):
        lines[block_place(block), :] = total[CELLS_A * block : CELLS_A * (block + 1)]
    lines[block_place(LINES_B + 1), :] = jnp.zeros((CELLS_A, G), F32)
    for copy in copies[3:]:
        copy.wait()
    result = table_dot((table_ref[0], table_ref[1]), halves(lines[...]), ((1,), (1,)))
    for v in range(3):
        out_ref[pl.ds(v, G, stride=3), :] = result[:, LANES * v : LANES * (v + 1)]
    for shift, sent in enumerate(sent_refs):
        c = (lax.axis_index("row") + shift) & (ROWS - 1)
        sent[pl.ds(SENT - 8, 8), :] = jnp.zeros((8, LANES), F32)
        for half in range(2):
            rows = spectrum_ref[half, pl.ds(c, KEPT, stride=CELLS_B), :]
            sent[pl.ds(half * KEPT, KEPT), :] = rows
    for shift in (0, 1, ROWS - 1):
        for block in range(8):
            at = pl.ds(block * LANES, LANES)
            sent_refs[shift][pl.ds(SENT + block, 1), :] = charges_ref[:, at]


def cas_of(turns):
    centred = ((turns + 3 * G // 8) & (G - 1)) - G // 2
    angle = (G // 4 - jnp.abs(centred)).astype(F32) * (2.0 * math.pi / G)
    square = angle * angle
    value = jnp.full_like(square, math.sqrt(2.0) / math.factorial(13))
    for power in (11, 9, 7, 5, 3, 1):
        sign = 1.0 if power % 4 == 1 else -1.0
        value = value * square + sign * math.sqrt(2.0) / math.factorial(power)
    return value * angle


def spectrum_kernel(*refs):
    sent_refs, (out_ref, beside_ref, waves_ref, joined) = refs[:ROWS], refs[ROWS:]
    for shift, sent in enumerate(sent_refs):
        owner = (lax.axis_index("row") - shift) & (ROWS - 1)
        at = pl.ds(pl.multiple_of(owner * SENT, 8), SENT)
        joined[at, :] = sent[pl.ds(0, SENT), :]
    for place, shift in enumerate((1, 0, ROWS - 1)):
        beside_ref[pl.ds(8 * place, 8), :] = sent_refs[shift][pl.ds(SENT, 8), :]
    line = lax.broadcasted_iota(jnp.int32, (G, ROWS * SENT), 0)
    folded = jnp.minimum(line, G - line)
    block, inside = folded >> 5, folded & (CELLS_A - 1)
    mirrored = inside >= KEPT
    owner = jnp.where(mirrored, ROWS - 1 - block, block)
    inside = jnp.where(mirrored, CELLS_A - inside, inside)
    place = lax.broadcasted_iota(jnp.int32, (G, ROWS * SENT), 1) - (owner * SENT + inside)
    parts = thirds(joined[...])
    for half in range(2):
        chosen = jnp.where(place == half * KEPT, 1.0, 0.0).astype(BF16)
        value = sum(dot(chosen, part) for part in parts)
        out_ref[:, pl.ds(LANES * half, LANES)] = value * (1.0 / (G * G * G))
        cell = lax.broadcasted_iota(jnp.int32, (G, LANES), 0) - 1
        wave = lax.broadcasted_iota(jnp.int32, (G, LANES), 1) + LANES * half
        waves_ref[half] = cas_of(cell * wave)


def plane_kernel(tiles_ref, spectrum_ref, waves_ref, out_ref):
    lane = lax.broadcasted_iota(jnp.int32, (CELLS_A, LANES), 1)
    slots = [(lane >> 5) == s for s in range(4)]
    wide = lax.broadcasted_iota(jnp.int32, (CELLS_A, G), 1)
    pairs = [((wide & 31) >> 1) == line for line in range(LINES_B)]
    pieces = [
        [tiles_ref[pl.ds(96 * r + v, CELLS_A, stride=3), :] for v in range(3)] for r in range(ROWS)
    ]

    def joined(block):
        parts = []
        for w in range(2):
            value = None
            for s in range(4):
                piece = pieces[4 * w + s][block // 4]
                value = piece if value is None else jnp.where(slots[(block + s) & 3], piece, value)
            parts.append(value)
        return jnp.concatenate(parts, axis=1)

    def waves(start, count, stride=1):
        rows = [waves_ref[half, pl.ds(start, count, stride=stride), :] for half in range(2)]
        return jnp.concatenate(rows, axis=1)

    first = halves(waves(0, G))
    even = (lax.broadcasted_iota(jnp.int32, (CELLS_A, G), 0) & 1) == 0
    outer = []
    for slot in range(ROWS):
        start = CELLS_A * ((row_at(slot, LINES_B) + 1) % ROWS)
        outer.append(jnp.where(even, waves(start, 1), waves(start + 1, 1)))
    outer = halves(jnp.concatenate(outer, axis=0))
    lines = [line for group in GROUPS for line in group]
    flipped = []
    for line in lines:
        rows = waves(line % CELLS_B, COLS, CELLS_B)
        flipped.append(pltpu.roll(rows, COLS - 1, 0) if line >= CELLS_B else rows)
    flipped = jnp.concatenate([*flipped, jnp.zeros((LINES - MAIN, G), F32)], axis=0)
    second = halves(flipped.T[:, :MAIN])
    flipped = halves(flipped[:MAIN])

    def table(m):
        order = [row_at(slot, m) for slot in range(ROWS)]
        return [
            jnp.concatenate([part[CELLS_A * r : CELLS_A * (r + 1)] for r in order], axis=0)
            for part in first
        ]

    rim = joined(LINES_B)
    main = [
        halves(jnp.concatenate([joined(line) for line in group], axis=0)) for group in GROUPS
    ]
    rims = halves(jnp.concatenate([jnp.where(pairs[line], rim, 0.0) for line in lines], axis=0))
    half = jnp.concatenate([dot_table(rows, table(m)) for m, rows in enumerate(main)], axis=0)
    half = halves(half + dot_table(rims, outer))
    image = table_dot(second, half) * spectrum_ref[...]
    half = halves(table_dot(flipped, halves(image)))
    rims = dot_table(half, outer, ((1,), (1,)))
    blocks, at = {}, 0
    for m, group in enumerate(GROUPS):
        size = CELLS_A * len(group)
        rows = [part[at : at + size] for part in half]
        value = dot_table(rows, table(m), ((1,), (1,)))
        for place, line in enumerate(group):
            blocks[line] = value[CELLS_A * place : CELLS_A * (place + 1)]
        at += size
    zero = jnp.zeros((CELLS_A, G), F32)
    rim = zero
    for place, line in enumerate(lines):
        rim = jnp.where(pairs[line], rims[CELLS_A * place : CELLS_A * (place + 1)], rim)
    blocks[LINES_B], blocks[LINES_B + 1] = rim, zero
    for r in range(ROWS):
        lanes = slice(LANES * (r // 4), LANES * (r // 4 + 1))
        for v in range(3):
            value = None
            for block in range(4 * v, 4 * v + 4):
                piece = blocks[block][:, lanes]
                value = piece if value is None else jnp.where(slots[(block + r) & 3], piece, value)
            out_ref[pl.ds(96 * r + v, CELLS_A, stride=3), :] = value


def gather_tile(weights_ref, place, picked, tile, base, at):
    near_masks, next_masks, groups, bits = masks_of(place)
    weights_at = pl.ds(tile * LANES, LANES)
    total = jnp.zeros((8, LANES), F32)
    for k in range(4):
        blocks = []
        for line in range(LINES_B):
            start = SPREAD * k + CELLS_A * line
            rows = [picked[base, pl.ds(start + 8 * v, 8), at] for v in range(4)]
            last = picked[base, pl.ds(SPREAD * k + MAIN + 8 * (line // 4), 8), at]
            rows.append(pltpu.roll(last, 8 - 2 * (line % 4), 0) if line % 4 else last)
            pair = []
            for skip in range(2):
                chosen = rows[skip]
                for g in range(1, 4):
                    chosen = jnp.where(groups[g], rows[g + skip], chosen)
                pair.append(chosen)
            blocks.append(pair)
        for mask, shift, count in zip(bits[::-1], (4, 2, 1), (7, 5, 4)):
            fewer = []
            for line in range(count):
                low = blocks[line]
                if line + shift < len(blocks):
                    high = blocks[line + shift]
                    low = [jnp.where(mask, h, l) for h, l in zip(high, low)]
                fewer.append(low)
            blocks = fewer
        for j in range(4):
            rows = stencil_rows(weights_ref, j, k, weights_at)
            near, after = two_rows(rows, near_masks, next_masks)
            total = total + (near * blocks[j][0] + after * blocks[j][1])
    return jnp.sum(total, axis=0, keepdims=True)


def gather_kernel(
    field_ref, anchors_ref, weights_ref, table_ref, near_ref, out_ref, lines, parts, picked
):
    turned = [field_ref[pl.ds(v, G, stride=3), :].T for v in range(3)]
    turned = halves(jnp.concatenate(turned, axis=0))
    lines[...] = dot_table(turned, (table_ref[0], table_ref[1]))
    field = jnp.concatenate([lines[block_place(b), :] for b in range(LINES_B + 1)], axis=0)
    for k in range(4):
        high, low = halves(pltpu.roll(field, G - k, 1) if k else field)
        parts[pl.ds(SPREAD * k, SPREAD), pl.ds(0, G)] = high
        parts[pl.ds(SPREAD * k, SPREAD), pl.ds(G, G)] = low
    hot = onehot(anchors_ref)
    hot = jnp.concatenate([hot, hot], axis=0)
    for chunk in range(TRI // CHUNK):
        picked[chunk] = dot(parts[...], hot[:, CHUNK * chunk : CHUNK * (chunk + 1)])
        for step in range(CHUNK // LANES):
            tile = chunk * (CHUNK // LANES) + step
            at = pl.ds(tile * LANES, LANES)
            place = local_place(anchors_ref, at)
            value = gather_tile(
                weights_ref, place, picked, tile, chunk, pl.ds(step * LANES, LANES)
            )
            out_ref[:, at] = value + near_ref[:, at]


def near_kernel(
    count_ref, target_ref, source_ref, before_ref, own_ref, after_ref, tiles_hbm, out_ref,
    charges_ref, total, tiles_ref, sem,
):
    size = LANES
    parts = tiles_hbm.shape[0] // PART
    copies = []
    for part in range(parts):
        at = pl.ds(PART * part, PART)
        copies.append(pltpu.make_async_copy(tiles_hbm.at[at], tiles_ref.at[at], sem.at[part]))
    for copy in copies:
        copy.start()
    total[...] = jnp.zeros_like(total)
    for place, ref in enumerate((before_ref, own_ref, after_ref)):
        charges_ref[pl.ds(24 * place, 24), :] = ref[...]

    def slot(place, carry):
        rows = pl.ds(pl.multiple_of(target_ref[place] * size, size), size)
        code = source_ref[place]
        neighbour = code >> 3
        row = neighbour // 3
        line = 24 * (neighbour - 3 * row) + 8 * row + (code & 7)
        source = charges_ref[pl.ds(line, 1), :]
        total[rows, :] = total[rows, :] + tiles_ref[place] * source
        return carry

    for part, copy in enumerate(copies):
        copy.wait()
        start = PART * part
        lax.fori_loop(start, jnp.clip(count_ref[0], start, start + PART), slot, 0)
    ones = jnp.ones((8, size), BF16)
    result = sum(dot(ones, part, ((1,), (1,))) for part in thirds(total[...]))
    out_ref[...] = result[0:1]


def shifted(value, axis, by):
    size = lax.axis_size(axis)
    return lax.ppermute(value, axis, [(i, (i + by) % size) for i in range(size)])


def near_field(beside, near_count, near_target, near_source, near_tiles):
    slots, size, _ = near_tiles.shape
    before, after = shifted(beside, "col", 1), shifted(beside, "col", -1)
    smem = pl.BlockSpec(memory_space=pltpu.SMEM)
    vmem = pl.BlockSpec(memory_space=pltpu.VMEM)
    return pl.pallas_call(
        near_kernel,
        in_specs=[smem, smem, smem, vmem, vmem, vmem, pl.BlockSpec(memory_space=pltpu.HBM)],
        out_shape=jax.ShapeDtypeStruct((1, TRI), F32),
        scratch_shapes=[
            pltpu.VMEM((72, size), F32),
            pltpu.VMEM((TRI, size), F32),
            pltpu.VMEM((slots, size, size), F32),
            pltpu.SemaphoreType.DMA((slots // PART,)),
        ],
        compiler_params=params(8),
        name="near",
    )(
        near_count,
        near_target,
        near_source,
        before,
        beside,
        after,
        pltpu.with_memory_space_constraint(near_tiles, pltpu.HBM),
    )


def exchange(values, axes, pieces):
    shaped = values.reshape(pieces, 1, values.size // pieces)
    moved = lax.all_to_all(shaped, axes, split_axis=0, concat_axis=0, tiled=True)
    return moved.reshape(values.shape)


def local(
    charges,
    anchors,
    stencil_weights,
    kernel_spectrum,
    near_count,
    near_target,
    near_source,
    near_tiles,
):
    table = jnp.asarray(line_table())
    devices = ROWS * COLS
    packed = jax.ShapeDtypeStruct((devices * LINES // LANES, LANES), F32)
    hbm = pl.BlockSpec(memory_space=pltpu.HBM)
    sizes = [SENT + 8 if shift in (0, 1, ROWS - 1) else SENT for shift in range(ROWS)]
    deposited, *sent = pl.pallas_call(
        deposit_kernel,
        out_shape=(packed, *[jax.ShapeDtypeStruct((size, LANES), F32) for size in sizes]),
        in_specs=[hbm] * 5,
        scratch_shapes=[
            pltpu.VMEM((1, TRI), F32),
            pltpu.VMEM((3, TRI), jnp.int32),
            pltpu.VMEM((64, TRI), F32),
            pltpu.VMEM((2, G, G), BF16),
            pltpu.VMEM((2, CELLS_B * KEPT, LANES), F32),
            pltpu.VMEM((64, TRI), F32),
            pltpu.VMEM((4, SPREAD, 2 * TRI), BF16),
            pltpu.VMEM((LINES, G), F32),
            pltpu.SemaphoreType.DMA((6,)),
        ],
        compiler_params=params(20),
        name="deposit",
    )(
        *[
            pltpu.with_memory_space_constraint(value, pltpu.HBM)
            for value in (
                charges.reshape(1, TRI),
                anchors,
                stencil_weights,
                table,
                kernel_spectrum.reshape(CELLS_A * CELLS_B, G),
            )
        ]
    )
    received = exchange(deposited, BOTH, devices)
    sent = [shifted(value, "row", shift) if shift else value for shift, value in enumerate(sent)]
    spectrum, beside, waves = pl.pallas_call(
        spectrum_kernel,
        out_shape=(
            jax.ShapeDtypeStruct((G, G), F32),
            jax.ShapeDtypeStruct((24, LANES), F32),
            jax.ShapeDtypeStruct((2, G, LANES), F32),
        ),
        scratch_shapes=[pltpu.VMEM((ROWS * SENT, LANES), F32)],
        compiler_params=params(8),
        name="spectrum",
    )(*sent)
    handed = pl.pallas_call(
        plane_kernel, out_shape=packed, compiler_params=params(12), name="plane"
    )(received, spectrum, waves)
    field = exchange(handed, BOTH, devices)
    beside, _ = lax.optimization_barrier((beside, handed))
    near = near_field(beside, near_count, near_target, near_source, near_tiles)
    result = pl.pallas_call(
        gather_kernel,
        out_shape=jax.ShapeDtypeStruct((1, TRI), F32),
        scratch_shapes=[
            pltpu.VMEM((LINES, G), F32),
            pltpu.VMEM((4 * SPREAD, 2 * G), BF16),
            pltpu.VMEM((TRI // CHUNK, 4 * SPREAD, CHUNK), F32),
        ],
        compiler_params=params(20),
        name="gather",
    )(field, anchors, stencil_weights, table, near)
    return result.reshape(TRI)


def solution(mesh):
    return jax.shard_map(
        local,
        mesh=mesh,
        in_specs=(
            P(("row", "col")),
            P(None, ("row", "col")),
            P(None, ("row", "col")),
            P("row", "col", None),
            P(("row", "col")),
            P(("row", "col")),
            P(("row", "col")),
            P(("row", "col"), None, None),
        ),
        out_specs=P(("row", "col")),
        check_vma=False,
    )
```

```python
import math

import jax
import jax.numpy as jnp
import ml_dtypes
import numpy as np
from jax import lax
from jax.experimental import pallas as pl
from jax.experimental.pallas import tpu as pltpu
from jax.sharding import PartitionSpec as P

G = 256
ROWS = 8
COLS = 32
CELLS_A = 32
CELLS_B = 8
TRI = 1024
LINES_B = 10
MAIN = LINES_B * CELLS_A
BLOCKS = 12
LINES = BLOCKS * CELLS_A
SPREAD = MAIN + CELLS_A
LANES = 128
TILES = TRI // LANES
KEPT = CELLS_A // 2 + 1
SENT = 40
CHUNK = 256
PART = 8
GROUPS = ((0, 4, 8), (1, 5, 9), (2, 6), (3, 7))
F32 = jnp.float32
BF16 = jnp.bfloat16
BOTH = ("row", "col")


def params(mebibytes):
    return pltpu.CompilerParams(vmem_limit_bytes=mebibytes * 1024 * 1024)


def split_table(table):
    high = table.astype(np.float32).astype(ml_dtypes.bfloat16)
    low = (table - high.astype(np.float64)).astype(np.float32).astype(ml_dtypes.bfloat16)
    return np.stack([high, low])


def cas(first, second):
    angle = (np.outer(first, second) % G) * (2.0 * np.pi / G)
    return np.cos(angle) + np.sin(angle)


def row_at(slot, block):
    return 4 * (slot // 4) + (slot - block) % 4


def line_table():
    steps = np.arange(G)
    device = np.arange(ROWS * COLS)
    plane = CELLS_B * (device % COLS) + device // COLS
    return split_table(cas(plane, steps))


def halves(value):
    high = value.astype(BF16)
    low = (value - high.astype(F32)).astype(BF16)
    return high, low


def paired(value):
    high = value.astype(BF16).astype(F32)
    return jnp.concatenate([high, value - high], axis=0).astype(BF16)


def thirds(value):
    parts = []
    for _ in range(3):
        parts.append(value.astype(BF16))
        value = value - parts[-1].astype(F32)
    return parts


def dot(left, right, dims=((1,), (0,))):
    return lax.dot_general(left, right, (dims, ((), ())), preferred_element_type=F32)


def dot_table(rows, table, dims=((1,), (0,))):
    high, low = rows
    size = high.shape[0]
    both = dot(jnp.concatenate([high, low], axis=0), table[0], dims)
    return both[:size] + (both[size:] + dot(high, table[1], dims))


def table_dot(table, value, dims=((1,), (0,))):
    high, low = value
    size = table[0].shape[0]
    both = dot(jnp.concatenate([table[0], table[1]], axis=0), high, dims)
    return both[:size] + (both[size:] + dot(table[0], low, dims))


def block_place(block):
    slot = (lax.axis_index("row") + block) & 3
    return pl.ds(pl.multiple_of(LANES * (block // 4) + CELLS_A * slot, CELLS_A), CELLS_A)


def onehot(anchors_ref):
    cells = lax.broadcasted_iota(jnp.int32, (G, TRI), 0)
    matched = cells == anchors_ref[2:3, :]
    return jnp.where(matched, 1.0, 0.0).astype(BF16)


def local_place(anchors_ref, at):
    first = (anchors_ref[0:1, at] - (lax.axis_index("row") * CELLS_A - 1)) & (G - 1)
    second = (anchors_ref[1:2, at] - (lax.axis_index("col") * CELLS_B - 1)) & (G - 1)
    first = jnp.broadcast_to(first, (8, LANES))
    second = jnp.broadcast_to(second, (8, LANES))
    return lax.broadcasted_iota(jnp.int32, (8, LANES), 0) - (first & 7), first >> 3, second


def masks_of(place):
    relative, group, second = place
    near_masks = [relative == i for i in range(4)]
    next_masks = [relative == i - 8 for i in range(1, 4)]
    groups = [group == g for g in range(4)]
    bits = [(second & bit) != 0 for bit in (1, 2, 4)]
    return near_masks, next_masks, groups, bits


def two_rows(rows, near_masks, next_masks):
    near = jnp.zeros((8, LANES), F32)
    after = jnp.zeros((8, LANES), F32)
    for i in range(4):
        near = jnp.where(near_masks[i], rows[i], near)
    for i in range(1, 4):
        after = jnp.where(next_masks[i - 1], rows[i], after)
    return near, after


def stencil_rows(ref, j, k, at):
    return [
        jnp.broadcast_to(ref[16 * i + 4 * j + k, at][None, :], (8, LANES)) for i in range(4)
    ]


def spread_tile(scaled, place, spread, k, tile):
    at = pl.ds(tile * LANES, LANES)
    zero = jnp.zeros((8, LANES), F32)
    none = jnp.zeros((16, LANES), BF16)
    near_masks, next_masks, groups, bits = masks_of(place)
    _, group, second = place
    group, second = [jnp.concatenate([part, part], axis=0) for part in (group, second)]
    wide_groups = [group == g for g in range(4)]
    wide_bits = [(second & bit) != 0 for bit in (1, 2, 4)]
    blocks, rims = [], []
    for j in range(4):
        rows = two_rows(stencil_rows(scaled, j, k, at), near_masks, next_masks)
        blocks.append([paired(row) for row in rows])
        rim = jnp.where(groups[3], rows[1], zero)
        rim = rim + pltpu.roll(rim, 2, 0)
        rims.append(rim + pltpu.roll(rim, 4, 0))
    for mask, shift, count in zip(wide_bits, (1, 2, 4), (5, 7, 10)):
        wider = []
        for line in range(count):
            if line < shift:
                wider.append([jnp.where(mask, none, low) for low in blocks[line]])
            elif line >= len(blocks):
                wider.append([jnp.where(mask, high, none) for high in blocks[line - shift]])
            else:
                pairs = zip(blocks[line - shift], blocks[line])
                wider.append([jnp.where(mask, high, low) for high, low in pairs])
        blocks = wider
    for line in range(LINES_B):
        near, after = blocks[line]
        for v in range(4):
            piece = jnp.where(wide_groups[v], near, none)
            piece = jnp.where(wide_groups[v - 1], after, piece) if v else piece
            spread[k, pl.ds(2 * (CELLS_A * line + 8 * v), 16), at] = piece
    beyond = (lax.broadcasted_iota(jnp.int32, (8, LANES), 0) >> 1) - place[2]
    for v in range(3):
        piece = zero
        for j in range(4):
            piece = jnp.where(beyond == j - 4 * v, rims[j], piece)
        spread[k, pl.ds(2 * (MAIN + 8 * v), 16), at] = paired(piece)
    spread[k, pl.ds(2 * (MAIN + 24), 16), at] = none


def deposit_kernel(
    charges_hbm, anchors_hbm, weights_hbm, table_hbm, spectrum_hbm, out_ref, *rest
):
    sent_refs = rest[:ROWS]
    charges_ref, anchors_ref, weights_ref, table_ref, spectrum_ref = rest[ROWS : ROWS + 5]
    scaled, spread, lines, sem = rest[ROWS + 5 :]
    pairs = (
        (weights_hbm, weights_ref),
        (anchors_hbm, anchors_ref),
        (charges_hbm, charges_ref),
        (spectrum_hbm.at[pl.ds(0, CELLS_B * KEPT), pl.ds(0, LANES)], spectrum_ref.at[0]),
        (spectrum_hbm.at[pl.ds(0, CELLS_B * KEPT), pl.ds(LANES, LANES)], spectrum_ref.at[1]),
        (table_hbm, table_ref),
    )
    copies = [pltpu.make_async_copy(a, b, sem.at[n]) for n, (a, b) in enumerate(pairs)]
    for copy in copies:
        copy.start()
    for copy in copies[:3]:
        copy.wait()
    scaled[...] = weights_ref[...] * charges_ref[...]
    places = [local_place(anchors_ref, pl.ds(tile * LANES, LANES)) for tile in range(TILES)]
    cells = lax.broadcasted_iota(jnp.int32, (LANES, G), 1)
    hot = []
    for tile in range(TILES):
        row = anchors_ref[2:3, pl.ds(tile * LANES, LANES)]
        column = jnp.broadcast_to(row, (LANES, LANES)).T
        column = jnp.concatenate([column, column], axis=1)
        hot.append(jnp.where(cells == column, 1.0, 0.0).astype(BF16))
    hot = jnp.concatenate(hot, axis=0)
    total = None
    for k in (1, 2, 3, 0):
        for tile in range(TILES):
            spread_tile(scaled, places[tile], spread, k, tile)
        placed = dot(spread[k], hot).reshape(SPREAD // 8, 2, 8, G)
        placed = (placed[:, 0] + placed[:, 1]).reshape(SPREAD, G)
        placed = pltpu.roll(placed, k, 1) if k else placed
        total = placed if total is None else total + placed
    for block in range(LINES_B + 1):
        lines[block_place(block), :] = total[CELLS_A * block : CELLS_A * (block + 1)]
    lines[block_place(LINES_B + 1), :] = jnp.zeros((CELLS_A, G), F32)
    for copy in copies[3:]:
        copy.wait()
    result = table_dot((table_ref[0], table_ref[1]), halves(lines[...]), ((1,), (1,)))
    for v in range(3):
        out_ref[pl.ds(v, G, stride=3), :] = result[:, LANES * v : LANES * (v + 1)]
    for shift, sent in enumerate(sent_refs):
        c = (lax.axis_index("row") + shift) & (ROWS - 1)
        sent[pl.ds(SENT - 8, 8), :] = jnp.zeros((8, LANES), F32)
        for half in range(2):
            rows = spectrum_ref[half, pl.ds(c, KEPT, stride=CELLS_B), :]
            sent[pl.ds(half * KEPT, KEPT), :] = rows
    for shift in (0, 1, ROWS - 1):
        for block in range(8):
            at = pl.ds(block * LANES, LANES)
            sent_refs[shift][pl.ds(SENT + block, 1), :] = charges_ref[:, at]


def cas_of(turns):
    centred = ((turns + 3 * G // 8) & (G - 1)) - G // 2
    angle = (G // 4 - jnp.abs(centred)).astype(F32) * (2.0 * math.pi / G)
    square = angle * angle
    value = jnp.full_like(square, math.sqrt(2.0) / math.factorial(13))
    for power in (11, 9, 7, 5, 3, 1):
        sign = 1.0 if power % 4 == 1 else -1.0
        value = value * square + sign * math.sqrt(2.0) / math.factorial(power)
    return value * angle


def spectrum_kernel(*refs):
    sent_refs, (out_ref, beside_ref, waves_ref, joined) = refs[:ROWS], refs[ROWS:]
    for shift, sent in enumerate(sent_refs):
        owner = (lax.axis_index("row") - shift) & (ROWS - 1)
        at = pl.ds(pl.multiple_of(owner * SENT, 8), SENT)
        joined[at, :] = sent[pl.ds(0, SENT), :]
    for place, shift in enumerate((1, 0, ROWS - 1)):
        beside_ref[pl.ds(8 * place, 8), :] = sent_refs[shift][pl.ds(SENT, 8), :]
    line = lax.broadcasted_iota(jnp.int32, (G, ROWS * SENT), 0)
    folded = jnp.minimum(line, G - line)
    block, inside = folded >> 5, folded & (CELLS_A - 1)
    mirrored = inside >= KEPT
    owner = jnp.where(mirrored, ROWS - 1 - block, block)
    inside = jnp.where(mirrored, CELLS_A - inside, inside)
    place = lax.broadcasted_iota(jnp.int32, (G, ROWS * SENT), 1) - (owner * SENT + inside)
    parts = thirds(joined[...])
    for half in range(2):
        chosen = jnp.where(place == half * KEPT, 1.0, 0.0).astype(BF16)
        value = sum(dot(chosen, part) for part in parts)
        out_ref[:, pl.ds(LANES * half, LANES)] = value * (1.0 / (G * G * G))
        cell = lax.broadcasted_iota(jnp.int32, (G, LANES), 0) - 1
        wave = lax.broadcasted_iota(jnp.int32, (G, LANES), 1) + LANES * half
        waves_ref[half] = cas_of(cell * wave)


def plane_kernel(tiles_ref, spectrum_ref, waves_ref, out_ref):
    lane = lax.broadcasted_iota(jnp.int32, (CELLS_A, LANES), 1)
    slots = [(lane >> 5) == s for s in range(4)]
    wide = lax.broadcasted_iota(jnp.int32, (CELLS_A, G), 1)
    pairs = [((wide & 31) >> 1) == line for line in range(LINES_B)]
    pieces = [
        [tiles_ref[pl.ds(96 * r + v, CELLS_A, stride=3), :] for v in range(3)] for r in range(ROWS)
    ]

    def joined(block):
        parts = []
        for w in range(2):
            value = None
            for s in range(4):
                piece = pieces[4 * w + s][block // 4]
                value = piece if value is None else jnp.where(slots[(block + s) & 3], piece, value)
            parts.append(value)
        return jnp.concatenate(parts, axis=1)

    def waves(start, count, stride=1):
        rows = [waves_ref[half, pl.ds(start, count, stride=stride), :] for half in range(2)]
        return jnp.concatenate(rows, axis=1)

    first = halves(waves(0, G))
    even = (lax.broadcasted_iota(jnp.int32, (CELLS_A, G), 0) & 1) == 0
    outer = []
    for slot in range(ROWS):
        start = CELLS_A * ((row_at(slot, LINES_B) + 1) % ROWS)
        outer.append(jnp.where(even, waves(start, 1), waves(start + 1, 1)))
    outer = halves(jnp.concatenate(outer, axis=0))
    lines = [line for group in GROUPS for line in group]
    flipped = []
    for line in lines:
        rows = waves(line % CELLS_B, COLS, CELLS_B)
        flipped.append(pltpu.roll(rows, COLS - 1, 0) if line >= CELLS_B else rows)
    flipped = jnp.concatenate([*flipped, jnp.zeros((LINES - MAIN, G), F32)], axis=0)
    second = halves(flipped.T[:, :MAIN])
    flipped = halves(flipped[:MAIN])

    def table(m):
        order = [row_at(slot, m) for slot in range(ROWS)]
        return [
            jnp.concatenate([part[CELLS_A * r : CELLS_A * (r + 1)] for r in order], axis=0)
            for part in first
        ]

    rim = joined(LINES_B)
    main = [
        halves(jnp.concatenate([joined(line) for line in group], axis=0)) for group in GROUPS
    ]
    rims = halves(jnp.concatenate([jnp.where(pairs[line], rim, 0.0) for line in lines], axis=0))
    half = jnp.concatenate([dot_table(rows, table(m)) for m, rows in enumerate(main)], axis=0)
    half = halves(half + dot_table(rims, outer))
    image = table_dot(second, half) * spectrum_ref[...]
    half = halves(table_dot(flipped, halves(image)))
    rims = dot_table(half, outer, ((1,), (1,)))
    blocks, at = {}, 0
    for m, group in enumerate(GROUPS):
        size = CELLS_A * len(group)
        rows = [part[at : at + size] for part in half]
        value = dot_table(rows, table(m), ((1,), (1,)))
        for place, line in enumerate(group):
            blocks[line] = value[CELLS_A * place : CELLS_A * (place + 1)]
        at += size
    zero = jnp.zeros((CELLS_A, G), F32)
    rim = zero
    for place, line in enumerate(lines):
        rim = jnp.where(pairs[line], rims[CELLS_A * place : CELLS_A * (place + 1)], rim)
    blocks[LINES_B], blocks[LINES_B + 1] = rim, zero
    for r in range(ROWS):
        lanes = slice(LANES * (r // 4), LANES * (r // 4 + 1))
        for v in range(3):
            value = None
            for block in range(4 * v, 4 * v + 4):
                piece = blocks[block][:, lanes]
                value = piece if value is None else jnp.where(slots[(block + r) & 3], piece, value)
            out_ref[pl.ds(96 * r + v, CELLS_A, stride=3), :] = value


def gather_tile(weights_ref, place, picked, tile, base, at):
    near_masks, next_masks, groups, bits = masks_of(place)
    weights_at = pl.ds(tile * LANES, LANES)
    total = jnp.zeros((8, LANES), F32)
    for k in range(4):
        blocks = []
        for line in range(LINES_B):
            start = SPREAD * k + CELLS_A * line
            rows = [picked[base, pl.ds(start + 8 * v, 8), at] for v in range(4)]
            last = picked[base, pl.ds(SPREAD * k + MAIN + 8 * (line // 4), 8), at]
            rows.append(pltpu.roll(last, 8 - 2 * (line % 4), 0) if line % 4 else last)
            pair = []
            for skip in range(2):
                chosen = rows[skip]
                for g in range(1, 4):
                    chosen = jnp.where(groups[g], rows[g + skip], chosen)
                pair.append(chosen)
            blocks.append(pair)
        for mask, shift, count in zip(bits[::-1], (4, 2, 1), (7, 5, 4)):
            fewer = []
            for line in range(count):
                low = blocks[line]
                if line + shift < len(blocks):
                    high = blocks[line + shift]
                    low = [jnp.where(mask, h, l) for h, l in zip(high, low)]
                fewer.append(low)
            blocks = fewer
        for j in range(4):
            rows = stencil_rows(weights_ref, j, k, weights_at)
            near, after = two_rows(rows, near_masks, next_masks)
            total = total + (near * blocks[j][0] + after * blocks[j][1])
    return jnp.sum(total, axis=0, keepdims=True)


def gather_kernel(
    field_ref, anchors_ref, weights_ref, table_ref, near_ref, out_ref, lines, parts, picked
):
    turned = [field_ref[pl.ds(v, G, stride=3), :].T for v in range(3)]
    turned = halves(jnp.concatenate(turned, axis=0))
    lines[...] = dot_table(turned, (table_ref[0], table_ref[1]))
    field = jnp.concatenate([lines[block_place(b), :] for b in range(LINES_B + 1)], axis=0)
    for k in range(4):
        high, low = halves(pltpu.roll(field, G - k, 1) if k else field)
        parts[pl.ds(SPREAD * k, SPREAD), pl.ds(0, G)] = high
        parts[pl.ds(SPREAD * k, SPREAD), pl.ds(G, G)] = low
    hot = onehot(anchors_ref)
    hot = jnp.concatenate([hot, hot], axis=0)
    for chunk in range(TRI // CHUNK):
        picked[chunk] = dot(parts[...], hot[:, CHUNK * chunk : CHUNK * (chunk + 1)])
        for step in range(CHUNK // LANES):
            tile = chunk * (CHUNK // LANES) + step
            at = pl.ds(tile * LANES, LANES)
            place = local_place(anchors_ref, at)
            value = gather_tile(
                weights_ref, place, picked, tile, chunk, pl.ds(step * LANES, LANES)
            )
            out_ref[:, at] = value + near_ref[:, at]


def near_kernel(
    count_ref, target_ref, source_ref, before_ref, own_ref, after_ref, tiles_hbm, out_ref,
    charges_ref, total, tiles_ref, sem,
):
    size = LANES
    parts = tiles_hbm.shape[0] // PART
    copies = []
    for part in range(parts):
        at = pl.ds(PART * part, PART)
        copies.append(pltpu.make_async_copy(tiles_hbm.at[at], tiles_ref.at[at], sem.at[part]))
    for copy in copies:
        copy.start()
    total[...] = jnp.zeros_like(total)
    for place, ref in enumerate((before_ref, own_ref, after_ref)):
        charges_ref[pl.ds(24 * place, 24), :] = ref[...]

    def slot(place, carry):
        rows = pl.ds(pl.multiple_of(target_ref[place] * size, size), size)
        code = source_ref[place]
        neighbour = code >> 3
        row = neighbour // 3
        line = 24 * (neighbour - 3 * row) + 8 * row + (code & 7)
        source = charges_ref[pl.ds(line, 1), :]
        total[rows, :] = total[rows, :] + tiles_ref[place] * source
        return carry

    for part, copy in enumerate(copies):
        copy.wait()
        start = PART * part
        lax.fori_loop(start, jnp.clip(count_ref[0], start, start + PART), slot, 0)
    ones = jnp.ones((8, size), BF16)
    result = sum(dot(ones, part, ((1,), (1,))) for part in thirds(total[...]))
    out_ref[...] = result[0:1]


def shifted(value, axis, by):
    size = lax.axis_size(axis)
    return lax.ppermute(value, axis, [(i, (i + by) % size) for i in range(size)])


def near_field(beside, near_count, near_target, near_source, near_tiles):
    slots, size, _ = near_tiles.shape
    before, after = shifted(beside, "col", 1), shifted(beside, "col", -1)
    smem = pl.BlockSpec(memory_space=pltpu.SMEM)
    vmem = pl.BlockSpec(memory_space=pltpu.VMEM)
    return pl.pallas_call(
        near_kernel,
        in_specs=[smem, smem, smem, vmem, vmem, vmem, pl.BlockSpec(memory_space=pltpu.HBM)],
        out_shape=jax.ShapeDtypeStruct((1, TRI), F32),
        scratch_shapes=[
            pltpu.VMEM((72, size), F32),
            pltpu.VMEM((TRI, size), F32),
            pltpu.VMEM((slots, size, size), F32),
            pltpu.SemaphoreType.DMA((slots // PART,)),
        ],
        compiler_params=params(8),
        name="near",
    )(
        near_count,
        near_target,
        near_source,
        before,
        beside,
        after,
        pltpu.with_memory_space_constraint(near_tiles, pltpu.HBM),
    )


def exchange(values, axes, pieces):
    shaped = values.reshape(pieces, 1, values.size // pieces)
    moved = lax.all_to_all(shaped, axes, split_axis=0, concat_axis=0, tiled=True)
    return moved.reshape(values.shape)


def local(
    charges,
    anchors,
    stencil_weights,
    kernel_spectrum,
    near_count,
    near_target,
    near_source,
    near_tiles,
):
    table = jnp.asarray(line_table())
    devices = ROWS * COLS
    packed = jax.ShapeDtypeStruct((devices * LINES // LANES, LANES), F32)
    hbm = pl.BlockSpec(memory_space=pltpu.HBM)
    sizes = [SENT + 8 if shift in (0, 1, ROWS - 1) else SENT for shift in range(ROWS)]
    deposited, *sent = pl.pallas_call(
        deposit_kernel,
        out_shape=(packed, *[jax.ShapeDtypeStruct((size, LANES), F32) for size in sizes]),
        in_specs=[hbm] * 5,
        scratch_shapes=[
            pltpu.VMEM((1, TRI), F32),
            pltpu.VMEM((3, TRI), jnp.int32),
            pltpu.VMEM((64, TRI), F32),
            pltpu.VMEM((2, G, G), BF16),
            pltpu.VMEM((2, CELLS_B * KEPT, LANES), F32),
            pltpu.VMEM((64, TRI), F32),
            pltpu.VMEM((4, 2 * SPREAD, TRI), BF16),
            pltpu.VMEM((LINES, G), F32),
            pltpu.SemaphoreType.DMA((6,)),
        ],
        compiler_params=params(20),
        name="deposit",
    )(
        *[
            pltpu.with_memory_space_constraint(value, pltpu.HBM)
            for value in (
                charges.reshape(1, TRI),
                anchors,
                stencil_weights,
                table,
                kernel_spectrum.reshape(CELLS_A * CELLS_B, G),
            )
        ]
    )
    received = exchange(deposited, BOTH, devices)
    sent = [shifted(value, "row", shift) if shift else value for shift, value in enumerate(sent)]
    spectrum, beside, waves = pl.pallas_call(
        spectrum_kernel,
        out_shape=(
            jax.ShapeDtypeStruct((G, G), F32),
            jax.ShapeDtypeStruct((24, LANES), F32),
            jax.ShapeDtypeStruct((2, G, LANES), F32),
        ),
        scratch_shapes=[pltpu.VMEM((ROWS * SENT, LANES), F32)],
        compiler_params=params(8),
        name="spectrum",
    )(*sent)
    handed = pl.pallas_call(
        plane_kernel, out_shape=packed, compiler_params=params(12), name="plane"
    )(received, spectrum, waves)
    field = exchange(handed, BOTH, devices)
    beside, _ = lax.optimization_barrier((beside, handed))
    near = near_field(beside, near_count, near_target, near_source, near_tiles)
    result = pl.pallas_call(
        gather_kernel,
        out_shape=jax.ShapeDtypeStruct((1, TRI), F32),
        scratch_shapes=[
            pltpu.VMEM((LINES, G), F32),
            pltpu.VMEM((4 * SPREAD, 2 * G), BF16),
            pltpu.VMEM((TRI // CHUNK, 4 * SPREAD, CHUNK), F32),
        ],
        compiler_params=params(20),
        name="gather",
    )(field, anchors, stencil_weights, table, near)
    return result.reshape(TRI)


def solution(mesh):
    return jax.shard_map(
        local,
        mesh=mesh,
        in_specs=(
            P(("row", "col")),
            P(None, ("row", "col")),
            P(None, ("row", "col")),
            P("row", "col", None),
            P(("row", "col")),
            P(("row", "col")),
            P(("row", "col")),
            P(("row", "col"), None, None),
        ),
        out_specs=P(("row", "col")),
        check_vma=False,
    )
```

```python
import math

import jax
import jax.numpy as jnp
import ml_dtypes
import numpy as np
from jax import lax
from jax.experimental import pallas as pl
from jax.experimental.pallas import tpu as pltpu
from jax.sharding import PartitionSpec as P

G = 256
ROWS = 8
COLS = 32
CELLS_A = 32
CELLS_B = 8
TRI = 1024
LINES_B = 10
MAIN = LINES_B * CELLS_A
BLOCKS = 12
LINES = BLOCKS * CELLS_A
SPREAD = MAIN + CELLS_A
LANES = 128
TILES = TRI // LANES
HALF = ROWS // 2
SENT = 2 * CELLS_A + 8
CHUNK = 256
PART = 8
GROUPS = ((0, 4, 8), (1, 5, 9), (2, 6), (3, 7))
F32 = jnp.float32
BF16 = jnp.bfloat16
BOTH = ("row", "col")


def params(mebibytes):
    return pltpu.CompilerParams(vmem_limit_bytes=mebibytes * 1024 * 1024)


def split_table(table):
    high = table.astype(np.float32).astype(ml_dtypes.bfloat16)
    low = (table - high.astype(np.float64)).astype(np.float32).astype(ml_dtypes.bfloat16)
    return np.stack([high, low])


def cas(first, second):
    angle = (np.outer(first, second) % G) * (2.0 * np.pi / G)
    return np.cos(angle) + np.sin(angle)


def row_at(slot, block):
    return 4 * (slot // 4) + (slot - block) % 4


def line_table():
    steps = np.arange(G)
    device = np.arange(ROWS * COLS)
    plane = CELLS_B * (device % COLS) + device // COLS
    return split_table(cas(plane, steps))


def halves(value):
    high = value.astype(BF16)
    low = (value - high.astype(F32)).astype(BF16)
    return high, low


def paired(value):
    high = value.astype(BF16).astype(F32)
    return jnp.concatenate([high, value - high], axis=0).astype(BF16)


def thirds(value):
    parts = []
    for _ in range(3):
        parts.append(value.astype(BF16))
        value = value - parts[-1].astype(F32)
    return parts


def dot(left, right, dims=((1,), (0,))):
    return lax.dot_general(left, right, (dims, ((), ())), preferred_element_type=F32)


def dot_table(rows, table, dims=((1,), (0,))):
    high, low = rows
    size = high.shape[0]
    both = dot(jnp.concatenate([high, low], axis=0), table[0], dims)
    return both[:size] + (both[size:] + dot(high, table[1], dims))


def table_dot(table, value, dims=((1,), (0,))):
    high, low = value
    size = table[0].shape[0]
    both = dot(jnp.concatenate([table[0], table[1]], axis=0), high, dims)
    return both[:size] + (both[size:] + dot(table[0], low, dims))


def block_place(block):
    slot = (lax.axis_index("row") + block) & 3
    return pl.ds(pl.multiple_of(LANES * (block // 4) + CELLS_A * slot, CELLS_A), CELLS_A)


def onehot(anchors_ref):
    cells = lax.broadcasted_iota(jnp.int32, (G, TRI), 0)
    matched = cells == anchors_ref[2:3, :]
    return jnp.where(matched, 1.0, 0.0).astype(BF16)


def local_place(anchors_ref, at):
    first = (anchors_ref[0:1, at] - (lax.axis_index("row") * CELLS_A - 1)) & (G - 1)
    second = (anchors_ref[1:2, at] - (lax.axis_index("col") * CELLS_B - 1)) & (G - 1)
    first = jnp.broadcast_to(first, (8, LANES))
    second = jnp.broadcast_to(second, (8, LANES))
    return lax.broadcasted_iota(jnp.int32, (8, LANES), 0) - (first & 7), first >> 3, second


def masks_of(place):
    relative, group, second = place
    near_masks = [relative == i for i in range(4)]
    next_masks = [relative == i - 8 for i in range(1, 4)]
    groups = [group == g for g in range(4)]
    bits = [(second & bit) != 0 for bit in (1, 2, 4)]
    return near_masks, next_masks, groups, bits


def two_rows(rows, near_masks, next_masks):
    near = jnp.zeros((8, LANES), F32)
    after = jnp.zeros((8, LANES), F32)
    for i in range(4):
        near = jnp.where(near_masks[i], rows[i], near)
    for i in range(1, 4):
        after = jnp.where(next_masks[i - 1], rows[i], after)
    return near, after


def stencil_rows(ref, j, k, at):
    return [
        jnp.broadcast_to(ref[16 * i + 4 * j + k, at][None, :], (8, LANES)) for i in range(4)
    ]


def spread_tile(scaled, place, spread, k, tile):
    at = pl.ds(tile * LANES, LANES)
    zero = jnp.zeros((8, LANES), F32)
    none = jnp.zeros((16, LANES), BF16)
    near_masks, next_masks, groups, bits = masks_of(place)
    _, group, second = place
    group, second = [jnp.concatenate([part, part], axis=0) for part in (group, second)]
    wide_groups = [group == g for g in range(4)]
    wide_bits = [(second & bit) != 0 for bit in (1, 2, 4)]
    blocks, rims = [], []
    for j in range(4):
        rows = two_rows(stencil_rows(scaled, j, k, at), near_masks, next_masks)
        blocks.append([paired(row) for row in rows])
        rim = jnp.where(groups[3], rows[1], zero)
        rim = rim + pltpu.roll(rim, 2, 0)
        rims.append(rim + pltpu.roll(rim, 4, 0))
    for mask, shift, count in zip(wide_bits, (1, 2, 4), (5, 7, 10)):
        wider = []
        for line in range(count):
            if line < shift:
                wider.append([jnp.where(mask, none, low) for low in blocks[line]])
            elif line >= len(blocks):
                wider.append([jnp.where(mask, high, none) for high in blocks[line - shift]])
            else:
                pairs = zip(blocks[line - shift], blocks[line])
                wider.append([jnp.where(mask, high, low) for high, low in pairs])
        blocks = wider
    for line in range(LINES_B):
        near, after = blocks[line]
        for v in range(4):
            piece = jnp.where(wide_groups[v], near, none)
            piece = jnp.where(wide_groups[v - 1], after, piece) if v else piece
            spread[k, pl.ds(2 * (CELLS_A * line + 8 * v), 16), at] = piece
    beyond = (lax.broadcasted_iota(jnp.int32, (8, LANES), 0) >> 1) - place[2]
    for v in range(3):
        piece = zero
        for j in range(4):
            piece = jnp.where(beyond == j - 4 * v, rims[j], piece)
        spread[k, pl.ds(2 * (MAIN + 8 * v), 16), at] = paired(piece)
    spread[k, pl.ds(2 * (MAIN + 24), 16), at] = none


def deposit_kernel(
    charges_hbm, anchors_hbm, weights_hbm, table_hbm, spectrum_hbm, out_ref, *rest
):
    first_ref, sent_refs = rest[0], rest[1 : 1 + HALF]
    charges_ref, anchors_ref, weights_ref, table_ref, spectrum_ref = rest[1 + HALF : 6 + HALF]
    scaled, spread, lines, sem = rest[6 + HALF :]
    pairs = (
        (weights_hbm, weights_ref),
        (anchors_hbm, anchors_ref),
        (charges_hbm, charges_ref),
        (spectrum_hbm.at[:, pl.ds(0, LANES)], spectrum_ref.at[0]),
        (spectrum_hbm.at[:, pl.ds(LANES, LANES)], spectrum_ref.at[1]),
        (table_hbm, table_ref),
    )
    copies = [pltpu.make_async_copy(a, b, sem.at[n]) for n, (a, b) in enumerate(pairs)]
    for copy in copies:
        copy.start()
    for copy in copies[:3]:
        copy.wait()
    scaled[...] = weights_ref[...] * charges_ref[...]
    places = [local_place(anchors_ref, pl.ds(tile * LANES, LANES)) for tile in range(TILES)]
    cells = lax.broadcasted_iota(jnp.int32, (LANES, G), 1)
    hot = []
    for tile in range(TILES):
        row = anchors_ref[2:3, pl.ds(tile * LANES, LANES)]
        column = jnp.broadcast_to(row, (LANES, LANES)).T
        column = jnp.concatenate([column, column], axis=1)
        hot.append(jnp.where(cells == column, 1.0, 0.0).astype(BF16))
    hot = jnp.concatenate(hot, axis=0)
    total = None
    for k in (1, 2, 3, 0):
        for tile in range(TILES):
            spread_tile(scaled, places[tile], spread, k, tile)
        placed = dot(spread[k], hot).reshape(SPREAD // 8, 2, 8, G)
        placed = (placed[:, 0] + placed[:, 1]).reshape(SPREAD, G)
        placed = pltpu.roll(placed, k, 1) if k else placed
        total = placed if total is None else total + placed
    for block in range(LINES_B + 1):
        lines[block_place(block), :] = total[CELLS_A * block : CELLS_A * (block + 1)]
    lines[block_place(LINES_B + 1), :] = jnp.zeros((CELLS_A, G), F32)
    for copy in copies[3:]:
        copy.wait()
    result = table_dot((table_ref[0], table_ref[1]), halves(lines[...]), ((1,), (1,)))
    for v in range(3):
        out_ref[pl.ds(v, G, stride=3), :] = result[:, LANES * v : LANES * (v + 1)]
    for half in range(2):
        first_ref[pl.ds(CELLS_B * half, CELLS_B), :] = spectrum_ref[half, pl.ds(0, CELLS_B), :]
    for step, sent in enumerate(sent_refs):
        c = lax.axis_index("row") ^ step
        for half in range(2):
            rows = spectrum_ref[half, pl.ds(c, CELLS_A, stride=CELLS_B), :]
            sent[pl.ds(CELLS_A * half, CELLS_A), :] = rows
    for block in range(8):
        charges = charges_ref[:, pl.ds(block * LANES, LANES)]
        first_ref[pl.ds(16 + block, 1), :] = charges
        for sent in sent_refs:
            sent[pl.ds(2 * CELLS_A + block, 1), :] = charges


def join_kernel(first_ref, *refs):
    row = lax.axis_index("row")
    for step in range(1, HALF):
        sent, out = refs[step - 1], refs[step + HALF - 2]
        out[pl.ds(0, SENT), :] = sent[...]
        out[pl.ds(SENT, 8), :] = line_of(first_ref, row ^ step)


def line_of(first_ref, c):
    halves_of = [first_ref[pl.ds(c + CELLS_B * half, 1), :] for half in range(2)]
    return jnp.concatenate([*halves_of, jnp.zeros((6, LANES), F32)], axis=0)


def waves_kernel(_, waves_ref):
    for half in range(2):
        cell = lax.broadcasted_iota(jnp.int32, (G, LANES), 0) - 1
        wave = lax.broadcasted_iota(jnp.int32, (G, LANES), 1) + LANES * half
        waves_ref[half] = cas_of(cell * wave)


def cas_of(turns):
    centred = ((turns + 3 * G // 8) & (G - 1)) - G // 2
    angle = (G // 4 - jnp.abs(centred)).astype(F32) * (2.0 * math.pi / G)
    square = angle * angle
    value = jnp.full_like(square, math.sqrt(2.0) / math.factorial(13))
    for power in (11, 9, 7, 5, 3, 1):
        sign = 1.0 if power % 4 == 1 else -1.0
        value = value * square + sign * math.sqrt(2.0) / math.factorial(power)
    return value * angle


def spectrum_kernel(first_ref, own_ref, *refs):
    received, (out_ref, beside_ref, joined) = refs[: HALF - 1], refs[HALF - 1 :]
    row = lax.axis_index("row")
    place = row & (HALF - 1)
    missing = line_of(first_ref, row)
    for step, ref in enumerate((own_ref, *received)):
        at = pl.ds(pl.multiple_of(2 * CELLS_A * (place ^ step), 2 * CELLS_A), 2 * CELLS_A)
        joined[at, :] = ref[pl.ds(0, 2 * CELLS_A), :]
        if step:
            missing = jnp.where(place ^ step == HALF - 1, ref[pl.ds(SENT, 8), :], missing)
    joined[pl.ds(2 * CELLS_A * HALF, 8), :] = missing
    charges = pl.ds(2 * CELLS_A, 8)
    nearest = received[0][charges, :]
    outside = (place == 0) | (place == HALF - 1)
    other = jnp.where(outside, first_ref[pl.ds(16, 8), :], received[2][charges, :])
    odd = (row & 1) == 1
    beside_ref[pl.ds(0, 8), :] = jnp.where(odd, nearest, other)
    beside_ref[pl.ds(8, 8), :] = own_ref[charges, :]
    beside_ref[pl.ds(16, 8), :] = jnp.where(odd, other, nearest)
    shape = (G, joined.shape[0])
    line = lax.broadcasted_iota(jnp.int32, shape, 0)
    line = jnp.minimum(line, G - line)
    line = jnp.where(row >= HALF, G // 2 - line, line)
    source = 2 * CELLS_A * (line >> 5) + (line & (CELLS_A - 1))
    pitch = jnp.where(line == G // 2, 1, CELLS_A)
    source = lax.broadcasted_iota(jnp.int32, shape, 1) - source
    parts = thirds(joined[...])
    for half in range(2):
        chosen = jnp.where(source == half * pitch, 1.0, 0.0).astype(BF16)
        value = sum(dot(chosen, part) for part in parts)
        out_ref[:, pl.ds(LANES * half, LANES)] = value * (1.0 / (G * G * G))


def plane_kernel(tiles_ref, spectrum_ref, waves_ref, out_ref):
    lane = lax.broadcasted_iota(jnp.int32, (CELLS_A, LANES), 1)
    slots = [(lane >> 5) == s for s in range(4)]
    wide = lax.broadcasted_iota(jnp.int32, (CELLS_A, G), 1)
    pairs = [((wide & 31) >> 1) == line for line in range(LINES_B)]
    pieces = [
        [tiles_ref[pl.ds(96 * r + v, CELLS_A, stride=3), :] for v in range(3)] for r in range(ROWS)
    ]

    def joined(block):
        parts = []
        for w in range(2):
            value = None
            for s in range(4):
                piece = pieces[4 * w + s][block // 4]
                value = piece if value is None else jnp.where(slots[(block + s) & 3], piece, value)
            parts.append(value)
        return jnp.concatenate(parts, axis=1)

    def waves(start, count, stride=1):
        rows = [waves_ref[half, pl.ds(start, count, stride=stride), :] for half in range(2)]
        return jnp.concatenate(rows, axis=1)

    first = halves(waves(0, G))
    even = (lax.broadcasted_iota(jnp.int32, (CELLS_A, G), 0) & 1) == 0
    outer = []
    for slot in range(ROWS):
        start = CELLS_A * ((row_at(slot, LINES_B) + 1) % ROWS)
        outer.append(jnp.where(even, waves(start, 1), waves(start + 1, 1)))
    outer = halves(jnp.concatenate(outer, axis=0))
    lines = [line for group in GROUPS for line in group]
    flipped = []
    for line in lines:
        rows = waves(line % CELLS_B, COLS, CELLS_B)
        flipped.append(pltpu.roll(rows, COLS - 1, 0) if line >= CELLS_B else rows)
    flipped = jnp.concatenate([*flipped, jnp.zeros((LINES - MAIN, G), F32)], axis=0)
    second = halves(flipped.T[:, :MAIN])
    flipped = halves(flipped[:MAIN])

    def table(m):
        order = [row_at(slot, m) for slot in range(ROWS)]
        return [
            jnp.concatenate([part[CELLS_A * r : CELLS_A * (r + 1)] for r in order], axis=0)
            for part in first
        ]

    rim = joined(LINES_B)
    main = [
        halves(jnp.concatenate([joined(line) for line in group], axis=0)) for group in GROUPS
    ]
    rims = halves(jnp.concatenate([jnp.where(pairs[line], rim, 0.0) for line in lines], axis=0))
    half = jnp.concatenate([dot_table(rows, table(m)) for m, rows in enumerate(main)], axis=0)
    half = halves(half + dot_table(rims, outer))
    image = table_dot(second, half) * spectrum_ref[...]
    half = halves(table_dot(flipped, halves(image)))
    rims = dot_table(half, outer, ((1,), (1,)))
    blocks, at = {}, 0
    for m, group in enumerate(GROUPS):
        size = CELLS_A * len(group)
        rows = [part[at : at + size] for part in half]
        value = dot_table(rows, table(m), ((1,), (1,)))
        for place, line in enumerate(group):
            blocks[line] = value[CELLS_A * place : CELLS_A * (place + 1)]
        at += size
    zero = jnp.zeros((CELLS_A, G), F32)
    rim = zero
    for place, line in enumerate(lines):
        rim = jnp.where(pairs[line], rims[CELLS_A * place : CELLS_A * (place + 1)], rim)
    blocks[LINES_B], blocks[LINES_B + 1] = rim, zero
    for r in range(ROWS):
        lanes = slice(LANES * (r // 4), LANES * (r // 4 + 1))
        for v in range(3):
            value = None
            for block in range(4 * v, 4 * v + 4):
                piece = blocks[block][:, lanes]
                value = piece if value is None else jnp.where(slots[(block + r) & 3], piece, value)
            out_ref[pl.ds(96 * r + v, CELLS_A, stride=3), :] = value


def gather_tile(weights_ref, place, picked, tile, base, at):
    near_masks, next_masks, groups, bits = masks_of(place)
    weights_at = pl.ds(tile * LANES, LANES)
    total = jnp.zeros((8, LANES), F32)
    for k in range(4):
        blocks = []
        for line in range(LINES_B):
            start = SPREAD * k + CELLS_A * line
            rows = [picked[base, pl.ds(start + 8 * v, 8), at] for v in range(4)]
            last = picked[base, pl.ds(SPREAD * k + MAIN + 8 * (line // 4), 8), at]
            rows.append(pltpu.roll(last, 8 - 2 * (line % 4), 0) if line % 4 else last)
            pair = []
            for skip in range(2):
                chosen = rows[skip]
                for g in range(1, 4):
                    chosen = jnp.where(groups[g], rows[g + skip], chosen)
                pair.append(chosen)
            blocks.append(pair)
        for mask, shift, count in zip(bits[::-1], (4, 2, 1), (7, 5, 4)):
            fewer = []
            for line in range(count):
                low = blocks[line]
                if line + shift < len(blocks):
                    high = blocks[line + shift]
                    low = [jnp.where(mask, h, l) for h, l in zip(high, low)]
                fewer.append(low)
            blocks = fewer
        for j in range(4):
            rows = stencil_rows(weights_ref, j, k, weights_at)
            near, after = two_rows(rows, near_masks, next_masks)
            total = total + (near * blocks[j][0] + after * blocks[j][1])
    return jnp.sum(total, axis=0, keepdims=True)


def gather_kernel(
    field_ref, anchors_ref, weights_ref, table_ref, near_ref, out_ref, lines, parts, picked
):
    turned = [field_ref[pl.ds(v, G, stride=3), :].T for v in range(3)]
    turned = halves(jnp.concatenate(turned, axis=0))
    lines[...] = dot_table(turned, (table_ref[0], table_ref[1]))
    field = jnp.concatenate([lines[block_place(b), :] for b in range(LINES_B + 1)], axis=0)
    for k in range(4):
        high, low = halves(pltpu.roll(field, G - k, 1) if k else field)
        parts[pl.ds(SPREAD * k, SPREAD), pl.ds(0, G)] = high
        parts[pl.ds(SPREAD * k, SPREAD), pl.ds(G, G)] = low
    hot = onehot(anchors_ref)
    hot = jnp.concatenate([hot, hot], axis=0)
    for chunk in range(TRI // CHUNK):
        picked[chunk] = dot(parts[...], hot[:, CHUNK * chunk : CHUNK * (chunk + 1)])
        for step in range(CHUNK // LANES):
            tile = chunk * (CHUNK // LANES) + step
            at = pl.ds(tile * LANES, LANES)
            place = local_place(anchors_ref, at)
            value = gather_tile(
                weights_ref, place, picked, tile, chunk, pl.ds(step * LANES, LANES)
            )
            out_ref[:, at] = value + near_ref[:, at]


def near_kernel(
    count_ref, target_ref, source_ref, before_ref, own_ref, after_ref, tiles_hbm, out_ref,
    charges_ref, total, tiles_ref, sem,
):
    size = LANES
    parts = tiles_hbm.shape[0] // PART
    copies = []
    for part in range(parts):
        at = pl.ds(PART * part, PART)
        copies.append(pltpu.make_async_copy(tiles_hbm.at[at], tiles_ref.at[at], sem.at[part]))
    for copy in copies:
        copy.start()
    total[...] = jnp.zeros_like(total)
    for place, ref in enumerate((before_ref, own_ref, after_ref)):
        charges_ref[pl.ds(24 * place, 24), :] = ref[...]

    def slot(place, carry):
        rows = pl.ds(pl.multiple_of(target_ref[place] * size, size), size)
        code = source_ref[place]
        neighbour = code >> 3
        row = neighbour // 3
        line = 24 * (neighbour - 3 * row) + 8 * row + (code & 7)
        source = charges_ref[pl.ds(line, 1), :]
        total[rows, :] = total[rows, :] + tiles_ref[place] * source
        return carry

    for part, copy in enumerate(copies):
        copy.wait()
        start = PART * part
        lax.fori_loop(start, jnp.clip(count_ref[0], start, start + PART), slot, 0)
    ones = jnp.ones((8, size), BF16)
    result = sum(dot(ones, part, ((1,), (1,))) for part in thirds(total[...]))
    out_ref[...] = result[0:1]


def shifted(value, axis, by):
    size = lax.axis_size(axis)
    return lax.ppermute(value, axis, [(i, (i + by) % size) for i in range(size)])


def near_field(beside, near_count, near_target, near_source, near_tiles):
    slots, size, _ = near_tiles.shape
    before, after = shifted(beside, "col", 1), shifted(beside, "col", -1)
    smem = pl.BlockSpec(memory_space=pltpu.SMEM)
    vmem = pl.BlockSpec(memory_space=pltpu.VMEM)
    return pl.pallas_call(
        near_kernel,
        in_specs=[smem, smem, smem, vmem, vmem, vmem, pl.BlockSpec(memory_space=pltpu.HBM)],
        out_shape=jax.ShapeDtypeStruct((1, TRI), F32),
        scratch_shapes=[
            pltpu.VMEM((72, size), F32),
            pltpu.VMEM((TRI, size), F32),
            pltpu.VMEM((slots, size, size), F32),
            pltpu.SemaphoreType.DMA((slots // PART,)),
        ],
        compiler_params=params(8),
        name="near",
    )(
        near_count,
        near_target,
        near_source,
        before,
        beside,
        after,
        pltpu.with_memory_space_constraint(near_tiles, pltpu.HBM),
    )


def swapped(value, mask):
    return lax.ppermute(value, "row", [(i, i ^ mask) for i in range(ROWS)])


def exchange(values, axes, pieces):
    shaped = values.reshape(pieces, 1, values.size // pieces)
    moved = lax.all_to_all(shaped, axes, split_axis=0, concat_axis=0, tiled=True)
    return moved.reshape(values.shape)


def local(
    charges,
    anchors,
    stencil_weights,
    kernel_spectrum,
    near_count,
    near_target,
    near_source,
    near_tiles,
):
    table = jnp.asarray(line_table())
    devices = ROWS * COLS
    packed = jax.ShapeDtypeStruct((devices * LINES // LANES, LANES), F32)
    hbm = pl.BlockSpec(memory_space=pltpu.HBM)
    deposited, first, *sent = pl.pallas_call(
        deposit_kernel,
        out_shape=(packed, *[jax.ShapeDtypeStruct((size, LANES), F32) for size in (24, *[SENT] * HALF)]),
        in_specs=[hbm] * 5,
        scratch_shapes=[
            pltpu.VMEM((1, TRI), F32),
            pltpu.VMEM((3, TRI), jnp.int32),
            pltpu.VMEM((64, TRI), F32),
            pltpu.VMEM((2, G, G), BF16),
            pltpu.VMEM((2, CELLS_A * CELLS_B, LANES), F32),
            pltpu.VMEM((64, TRI), F32),
            pltpu.VMEM((4, 2 * SPREAD, TRI), BF16),
            pltpu.VMEM((LINES, G), F32),
            pltpu.SemaphoreType.DMA((6,)),
        ],
        compiler_params=params(20),
        name="deposit",
    )(
        *[
            pltpu.with_memory_space_constraint(value, pltpu.HBM)
            for value in (
                charges.reshape(1, TRI),
                anchors,
                stencil_weights,
                table,
                kernel_spectrum.reshape(CELLS_A * CELLS_B, G),
            )
        ]
    )
    received = exchange(deposited, BOTH, devices)
    first = swapped(first, ROWS - 1)
    joined = pl.pallas_call(
        join_kernel,
        out_shape=[jax.ShapeDtypeStruct((SENT + 8, LANES), F32)] * (HALF - 1),
        compiler_params=params(8),
        name="join",
    )(first, *sent[1:])
    joined = [swapped(value, step + 1) for step, value in enumerate(joined)]
    waves = pl.pallas_call(
        waves_kernel,
        out_shape=jax.ShapeDtypeStruct((2, G, LANES), F32),
        compiler_params=params(8),
        name="waves",
    )(first)
    spectrum, beside = pl.pallas_call(
        spectrum_kernel,
        out_shape=(
            jax.ShapeDtypeStruct((G, G), F32),
            jax.ShapeDtypeStruct((24, LANES), F32),
        ),
        scratch_shapes=[pltpu.VMEM((2 * CELLS_A * HALF + 8, LANES), F32)],
        compiler_params=params(8),
        name="spectrum",
    )(first, sent[0], *joined)
    handed = pl.pallas_call(
        plane_kernel, out_shape=packed, compiler_params=params(12), name="plane"
    )(received, spectrum, waves)
    field = exchange(handed, BOTH, devices)
    beside, _ = lax.optimization_barrier((beside, handed))
    near = near_field(beside, near_count, near_target, near_source, near_tiles)
    result = pl.pallas_call(
        gather_kernel,
        out_shape=jax.ShapeDtypeStruct((1, TRI), F32),
        scratch_shapes=[
            pltpu.VMEM((LINES, G), F32),
            pltpu.VMEM((4 * SPREAD, 2 * G), BF16),
            pltpu.VMEM((TRI // CHUNK, 4 * SPREAD, CHUNK), F32),
        ],
        compiler_params=params(20),
        name="gather",
    )(field, anchors, stencil_weights, table, near)
    return result.reshape(TRI)


def solution(mesh):
    return jax.shard_map(
        local,
        mesh=mesh,
        in_specs=(
            P(("row", "col")),
            P(None, ("row", "col")),
            P(None, ("row", "col")),
            P("row", "col", None),
            P(("row", "col")),
            P(("row", "col")),
            P(("row", "col")),
            P(("row", "col"), None, None),
        ),
        out_specs=P(("row", "col")),
        check_vma=False,
    )
```

```python
import math

import jax
import jax.numpy as jnp
import ml_dtypes
import numpy as np
from jax import lax
from jax.experimental import pallas as pl
from jax.experimental.pallas import tpu as pltpu
from jax.sharding import PartitionSpec as P

G = 256
ROWS = 8
COLS = 32
CELLS_A = 32
CELLS_B = 8
TRI = 1024
LINES_B = 10
MAIN = LINES_B * CELLS_A
BLOCKS = 12
LINES = BLOCKS * CELLS_A
SPREAD = MAIN + CELLS_A
LANES = 128
TILES = TRI // LANES
HALF = ROWS // 2
SENT = 2 * CELLS_A + 8
CHUNK = 256
PART = 8
SHIFTS = 5
GROUPS = ((0, 4, 8), (1, 5, 9), (2, 6), (3, 7))
F32 = jnp.float32
BF16 = jnp.bfloat16
BOTH = ("row", "col")


def params(mebibytes):
    return pltpu.CompilerParams(vmem_limit_bytes=mebibytes * 1024 * 1024)


def split_table(table):
    high = table.astype(np.float32).astype(ml_dtypes.bfloat16)
    low = (table - high.astype(np.float64)).astype(np.float32).astype(ml_dtypes.bfloat16)
    return np.stack([high, low])


def cas(first, second):
    angle = (np.outer(first, second) % G) * (2.0 * np.pi / G)
    return np.cos(angle) + np.sin(angle)


def row_at(slot, block):
    return 4 * (slot // 4) + (slot - block) % 4


def line_table():
    steps = np.arange(G)
    device = np.arange(ROWS * COLS)
    plane = CELLS_B * (device % COLS) + device // COLS
    return split_table(cas(plane, steps))


def halves(value):
    high = value.astype(BF16)
    low = (value - high.astype(F32)).astype(BF16)
    return high, low


def paired(value):
    high = value.astype(BF16).astype(F32)
    return jnp.concatenate([high, value - high], axis=0).astype(BF16)


def thirds(value):
    parts = []
    for _ in range(3):
        parts.append(value.astype(BF16))
        value = value - parts[-1].astype(F32)
    return parts


def dot(left, right, dims=((1,), (0,))):
    return lax.dot_general(left, right, (dims, ((), ())), preferred_element_type=F32)


def dot_table(rows, table, dims=((1,), (0,))):
    high, low = rows
    size = high.shape[0]
    both = dot(jnp.concatenate([high, low], axis=0), table[0], dims)
    return both[:size] + (both[size:] + dot(high, table[1], dims))


def table_dot(table, value, dims=((1,), (0,))):
    high, low = value
    size = table[0].shape[0]
    both = dot(jnp.concatenate([table[0], table[1]], axis=0), high, dims)
    return both[:size] + (both[size:] + dot(table[0], low, dims))


def block_place(block):
    slot = (lax.axis_index("row") + block) & 3
    return pl.ds(pl.multiple_of(LANES * (block // 4) + CELLS_A * slot, CELLS_A), CELLS_A)


def onehot(anchors_ref):
    cells = lax.broadcasted_iota(jnp.int32, (LANES, TRI), 0)
    matched = cells == anchors_ref[2:3, :] >> 1
    return jnp.where(matched, 1.0, 0.0).astype(BF16)


def local_place(anchors_ref, at):
    first = (anchors_ref[0:1, at] - (lax.axis_index("row") * CELLS_A - 1)) & (G - 1)
    second = (anchors_ref[1:2, at] - (lax.axis_index("col") * CELLS_B - 1)) & (G - 1)
    first = jnp.broadcast_to(first, (8, LANES))
    second = jnp.broadcast_to(second, (8, LANES))
    return lax.broadcasted_iota(jnp.int32, (8, LANES), 0) - (first & 7), first >> 3, second


def masks_of(place):
    relative, group, second = place
    near_masks = [relative == i for i in range(4)]
    next_masks = [relative == i - 8 for i in range(1, 4)]
    groups = [group == g for g in range(4)]
    bits = [(second & bit) != 0 for bit in (1, 2, 4)]
    return near_masks, next_masks, groups, bits


def two_rows(rows, near_masks, next_masks):
    near = jnp.zeros((8, LANES), F32)
    after = jnp.zeros((8, LANES), F32)
    for i in range(4):
        near = jnp.where(near_masks[i], rows[i], near)
    for i in range(1, 4):
        after = jnp.where(next_masks[i - 1], rows[i], after)
    return near, after


def stencil_rows(ref, j, k, at):
    return [
        jnp.broadcast_to(ref[16 * i + 4 * j + k, at][None, :], (8, LANES)) for i in range(4)
    ]


def spread_tile(scaled, place, spread, k, tile):
    at = pl.ds(tile * LANES, LANES)
    zero = jnp.zeros((8, LANES), F32)
    none = jnp.zeros((16, LANES), BF16)
    near_masks, next_masks, groups, bits = masks_of(place)
    _, group, second = place
    group, second = [jnp.concatenate([part, part], axis=0) for part in (group, second)]
    wide_groups = [group == g for g in range(4)]
    wide_bits = [(second & bit) != 0 for bit in (1, 2, 4)]
    blocks, rims = [], []
    for j in range(4):
        rows = two_rows(stencil_rows(scaled, j, k, at), near_masks, next_masks)
        blocks.append([paired(row) for row in rows])
        rim = jnp.where(groups[3], rows[1], zero)
        rim = rim + pltpu.roll(rim, 2, 0)
        rims.append(rim + pltpu.roll(rim, 4, 0))
    for mask, shift, count in zip(wide_bits, (1, 2, 4), (5, 7, 10)):
        wider = []
        for line in range(count):
            if line < shift:
                wider.append([jnp.where(mask, none, low) for low in blocks[line]])
            elif line >= len(blocks):
                wider.append([jnp.where(mask, high, none) for high in blocks[line - shift]])
            else:
                pairs = zip(blocks[line - shift], blocks[line])
                wider.append([jnp.where(mask, high, low) for high, low in pairs])
        blocks = wider
    for line in range(LINES_B):
        near, after = blocks[line]
        for v in range(4):
            piece = jnp.where(wide_groups[v], near, none)
            piece = jnp.where(wide_groups[v - 1], after, piece) if v else piece
            spread[k, pl.ds(2 * (CELLS_A * line + 8 * v), 16), at] = piece
    beyond = (lax.broadcasted_iota(jnp.int32, (8, LANES), 0) >> 1) - place[2]
    for v in range(3):
        piece = zero
        for j in range(4):
            piece = jnp.where(beyond == j - 4 * v, rims[j], piece)
        spread[k, pl.ds(2 * (MAIN + 8 * v), 16), at] = paired(piece)
    spread[k, pl.ds(2 * (MAIN + 24), 16), at] = none


def deposit_kernel(
    charges_hbm, anchors_hbm, weights_hbm, table_hbm, spectrum_hbm, out_ref, *rest
):
    first_ref, sent_refs = rest[0], rest[1 : 1 + HALF]
    charges_ref, anchors_ref, weights_ref, table_ref, spectrum_ref = rest[1 + HALF : 6 + HALF]
    scaled, spread, lines, sem = rest[6 + HALF :]
    pairs = (
        (weights_hbm, weights_ref),
        (anchors_hbm, anchors_ref),
        (charges_hbm, charges_ref),
        (spectrum_hbm.at[:, pl.ds(0, LANES)], spectrum_ref.at[0]),
        (spectrum_hbm.at[:, pl.ds(LANES, LANES)], spectrum_ref.at[1]),
        (table_hbm, table_ref),
    )
    copies = [pltpu.make_async_copy(a, b, sem.at[n]) for n, (a, b) in enumerate(pairs)]
    for copy in copies:
        copy.start()
    for copy in copies[:3]:
        copy.wait()
    scaled[...] = weights_ref[...] * charges_ref[...]
    places = [local_place(anchors_ref, pl.ds(tile * LANES, LANES)) for tile in range(TILES)]
    cells = lax.broadcasted_iota(jnp.int32, (LANES, G), 1)
    hot = []
    for tile in range(TILES):
        row = anchors_ref[2:3, pl.ds(tile * LANES, LANES)]
        column = jnp.broadcast_to(row, (LANES, LANES)).T
        column = jnp.concatenate([column, column], axis=1)
        hot.append(jnp.where(cells == column, 1.0, 0.0).astype(BF16))
    hot = jnp.concatenate(hot, axis=0)
    total = None
    for k in (1, 2, 3, 0):
        for tile in range(TILES):
            spread_tile(scaled, places[tile], spread, k, tile)
        placed = dot(spread[k], hot).reshape(SPREAD // 8, 2, 8, G)
        placed = (placed[:, 0] + placed[:, 1]).reshape(SPREAD, G)
        placed = pltpu.roll(placed, k, 1) if k else placed
        total = placed if total is None else total + placed
    for block in range(LINES_B + 1):
        lines[block_place(block), :] = total[CELLS_A * block : CELLS_A * (block + 1)]
    lines[block_place(LINES_B + 1), :] = jnp.zeros((CELLS_A, G), F32)
    for copy in copies[3:]:
        copy.wait()
    result = table_dot((table_ref[0], table_ref[1]), halves(lines[...]), ((1,), (1,)))
    for v in range(3):
        out_ref[pl.ds(v, G, stride=3), :] = result[:, LANES * v : LANES * (v + 1)]
    for half in range(2):
        first_ref[pl.ds(CELLS_B * half, CELLS_B), :] = spectrum_ref[half, pl.ds(0, CELLS_B), :]
    for step, sent in enumerate(sent_refs):
        c = lax.axis_index("row") ^ step
        for half in range(2):
            rows = spectrum_ref[half, pl.ds(c, CELLS_A, stride=CELLS_B), :]
            sent[pl.ds(CELLS_A * half, CELLS_A), :] = rows
    for block in range(8):
        charges = charges_ref[:, pl.ds(block * LANES, LANES)]
        first_ref[pl.ds(16 + block, 1), :] = charges
        for sent in sent_refs:
            sent[pl.ds(2 * CELLS_A + block, 1), :] = charges


def join_kernel(first_ref, *refs):
    row = lax.axis_index("row")
    for step in range(1, HALF):
        sent, out = refs[step - 1], refs[step + HALF - 2]
        out[pl.ds(0, SENT), :] = sent[...]
        out[pl.ds(SENT, 8), :] = line_of(first_ref, row ^ step)


def line_of(first_ref, c):
    halves_of = [first_ref[pl.ds(c + CELLS_B * half, 1), :] for half in range(2)]
    return jnp.concatenate([*halves_of, jnp.zeros((6, LANES), F32)], axis=0)


def waves_kernel(_, waves_ref):
    for half in range(2):
        cell = lax.broadcasted_iota(jnp.int32, (G, LANES), 0) - 1
        wave = lax.broadcasted_iota(jnp.int32, (G, LANES), 1) + LANES * half
        waves_ref[half] = cas_of(cell * wave)


def cas_of(turns):
    centred = ((turns + 3 * G // 8) & (G - 1)) - G // 2
    angle = (G // 4 - jnp.abs(centred)).astype(F32) * (2.0 * math.pi / G)
    square = angle * angle
    value = jnp.full_like(square, math.sqrt(2.0) / math.factorial(13))
    for power in (11, 9, 7, 5, 3, 1):
        sign = 1.0 if power % 4 == 1 else -1.0
        value = value * square + sign * math.sqrt(2.0) / math.factorial(power)
    return value * angle


def spectrum_kernel(first_ref, own_ref, *refs):
    received, (out_ref, beside_ref, joined) = refs[: HALF - 1], refs[HALF - 1 :]
    row = lax.axis_index("row")
    place = row & (HALF - 1)
    missing = line_of(first_ref, row)
    for step, ref in enumerate((own_ref, *received)):
        at = pl.ds(pl.multiple_of(2 * CELLS_A * (place ^ step), 2 * CELLS_A), 2 * CELLS_A)
        joined[at, :] = ref[pl.ds(0, 2 * CELLS_A), :]
        if step:
            missing = jnp.where(place ^ step == HALF - 1, ref[pl.ds(SENT, 8), :], missing)
    joined[pl.ds(2 * CELLS_A * HALF, 8), :] = missing
    charges = pl.ds(2 * CELLS_A, 8)
    nearest = received[0][charges, :]
    outside = (place == 0) | (place == HALF - 1)
    other = jnp.where(outside, first_ref[pl.ds(16, 8), :], received[2][charges, :])
    odd = (row & 1) == 1
    beside_ref[pl.ds(0, 8), :] = jnp.where(odd, nearest, other)
    beside_ref[pl.ds(8, 8), :] = own_ref[charges, :]
    beside_ref[pl.ds(16, 8), :] = jnp.where(odd, other, nearest)
    shape = (G, joined.shape[0])
    line = lax.broadcasted_iota(jnp.int32, shape, 0)
    line = jnp.minimum(line, G - line)
    line = jnp.where(row >= HALF, G // 2 - line, line)
    source = 2 * CELLS_A * (line >> 5) + (line & (CELLS_A - 1))
    pitch = jnp.where(line == G // 2, 1, CELLS_A)
    source = lax.broadcasted_iota(jnp.int32, shape, 1) - source
    parts = thirds(joined[...])
    for half in range(2):
        chosen = jnp.where(source == half * pitch, 1.0, 0.0).astype(BF16)
        value = sum(dot(chosen, part) for part in parts)
        out_ref[:, pl.ds(LANES * half, LANES)] = value * (1.0 / (G * G * G))


def plane_kernel(tiles_ref, spectrum_ref, waves_ref, out_ref):
    lane = lax.broadcasted_iota(jnp.int32, (CELLS_A, LANES), 1)
    slots = [(lane >> 5) == s for s in range(4)]
    wide = lax.broadcasted_iota(jnp.int32, (CELLS_A, G), 1)
    pairs = [((wide & 31) >> 1) == line for line in range(LINES_B)]
    pieces = [
        [tiles_ref[pl.ds(96 * r + v, CELLS_A, stride=3), :] for v in range(3)] for r in range(ROWS)
    ]

    def joined(block):
        parts = []
        for w in range(2):
            value = None
            for s in range(4):
                piece = pieces[4 * w + s][block // 4]
                value = piece if value is None else jnp.where(slots[(block + s) & 3], piece, value)
            parts.append(value)
        return jnp.concatenate(parts, axis=1)

    def waves(start, count, stride=1):
        rows = [waves_ref[half, pl.ds(start, count, stride=stride), :] for half in range(2)]
        return jnp.concatenate(rows, axis=1)

    first = halves(waves(0, G))
    even = (lax.broadcasted_iota(jnp.int32, (CELLS_A, G), 0) & 1) == 0
    outer = []
    for slot in range(ROWS):
        start = CELLS_A * ((row_at(slot, LINES_B) + 1) % ROWS)
        outer.append(jnp.where(even, waves(start, 1), waves(start + 1, 1)))
    outer = halves(jnp.concatenate(outer, axis=0))
    lines = [line for group in GROUPS for line in group]
    flipped = []
    for line in lines:
        rows = waves(line % CELLS_B, COLS, CELLS_B)
        flipped.append(pltpu.roll(rows, COLS - 1, 0) if line >= CELLS_B else rows)
    flipped = jnp.concatenate([*flipped, jnp.zeros((LINES - MAIN, G), F32)], axis=0)
    second = halves(flipped.T[:, :MAIN])
    flipped = halves(flipped[:MAIN])

    def table(m):
        order = [row_at(slot, m) for slot in range(ROWS)]
        return [
            jnp.concatenate([part[CELLS_A * r : CELLS_A * (r + 1)] for r in order], axis=0)
            for part in first
        ]

    rim = joined(LINES_B)
    main = [
        halves(jnp.concatenate([joined(line) for line in group], axis=0)) for group in GROUPS
    ]
    rims = halves(jnp.concatenate([jnp.where(pairs[line], rim, 0.0) for line in lines], axis=0))
    half = jnp.concatenate([dot_table(rows, table(m)) for m, rows in enumerate(main)], axis=0)
    half = halves(half + dot_table(rims, outer))
    image = table_dot(second, half) * spectrum_ref[...]
    half = halves(table_dot(flipped, halves(image)))
    rims = dot_table(half, outer, ((1,), (1,)))
    blocks, at = {}, 0
    for m, group in enumerate(GROUPS):
        size = CELLS_A * len(group)
        rows = [part[at : at + size] for part in half]
        value = dot_table(rows, table(m), ((1,), (1,)))
        for place, line in enumerate(group):
            blocks[line] = value[CELLS_A * place : CELLS_A * (place + 1)]
        at += size
    zero = jnp.zeros((CELLS_A, G), F32)
    rim = zero
    for place, line in enumerate(lines):
        rim = jnp.where(pairs[line], rims[CELLS_A * place : CELLS_A * (place + 1)], rim)
    blocks[LINES_B], blocks[LINES_B + 1] = rim, zero
    for r in range(ROWS):
        lanes = slice(LANES * (r // 4), LANES * (r // 4 + 1))
        for v in range(3):
            value = None
            for block in range(4 * v, 4 * v + 4):
                piece = blocks[block][:, lanes]
                value = piece if value is None else jnp.where(slots[(block + r) & 3], piece, value)
            out_ref[pl.ds(96 * r + v, CELLS_A, stride=3), :] = value


def gather_tile(weights_ref, anchors_ref, place, picked, tile, base, at):
    near_masks, next_masks, groups, bits = masks_of(place)
    weights_at = pl.ds(tile * LANES, LANES)
    odd = jnp.broadcast_to((anchors_ref[2:3, weights_at] & 1) != 0, (8, LANES))
    total = jnp.zeros((8, LANES), F32)
    before = None
    for shift in range(SHIFTS):
        blocks = []
        for line in range(LINES_B):
            start = SPREAD * shift + CELLS_A * line
            rows = [picked[base, pl.ds(start + 8 * v, 8), at] for v in range(4)]
            last = picked[base, pl.ds(SPREAD * shift + MAIN + 8 * (line // 4), 8), at]
            rows.append(pltpu.roll(last, 8 - 2 * (line % 4), 0) if line % 4 else last)
            pair = []
            for skip in range(2):
                chosen = rows[skip]
                for g in range(1, 4):
                    chosen = jnp.where(groups[g], rows[g + skip], chosen)
                pair.append(chosen)
            blocks.append(pair)
        for mask, width, count in zip(bits[::-1], (4, 2, 1), (7, 5, 4)):
            fewer = []
            for line in range(count):
                low = blocks[line]
                if line + width < len(blocks):
                    high = blocks[line + width]
                    low = [jnp.where(mask, h, l) for h, l in zip(high, low)]
                fewer.append(low)
            blocks = fewer
        if shift:
            for j in range(4):
                rows = stencil_rows(weights_ref, j, shift - 1, weights_at)
                weights = two_rows(rows, near_masks, next_masks)
                for weight, high, low in zip(weights, blocks[j], before[j]):
                    total = total + weight * jnp.where(odd, high, low)
        before = blocks
    return jnp.sum(total, axis=0, keepdims=True)


def gather_kernel(
    field_ref, anchors_ref, weights_ref, table_ref, near_ref, out_ref, lines, parts, picked
):
    turned = [field_ref[pl.ds(v, G, stride=3), :].T for v in range(3)]
    turned = halves(jnp.concatenate(turned, axis=0))
    lines[...] = dot_table(turned, (table_ref[0], table_ref[1]))
    field = jnp.concatenate([lines[block_place(b), :] for b in range(LINES_B + 1)], axis=0)
    for shift in range(SHIFTS):
        value = field[:, LANES * (shift % 2) : LANES * (shift % 2 + 1)]
        high, low = halves(pltpu.roll(value, LANES - shift // 2, 1) if shift > 1 else value)
        rows = pl.ds(SPREAD * shift, SPREAD)
        parts[rows, pl.ds(0, LANES)] = high
        parts[rows, pl.ds(LANES, LANES)] = low
    hot = onehot(anchors_ref)
    hot = jnp.concatenate([hot, hot], axis=0)
    for chunk in range(TRI // CHUNK):
        picked[chunk] = dot(parts[...], hot[:, CHUNK * chunk : CHUNK * (chunk + 1)])
        for step in range(CHUNK // LANES):
            tile = chunk * (CHUNK // LANES) + step
            at = pl.ds(tile * LANES, LANES)
            place = local_place(anchors_ref, at)
            value = gather_tile(
                weights_ref, anchors_ref, place, picked, tile, chunk, pl.ds(step * LANES, LANES)
            )
            out_ref[:, at] = value + near_ref[:, at]


def near_kernel(
    count_ref, target_ref, source_ref, before_ref, own_ref, after_ref, tiles_hbm, out_ref,
    charges_ref, total, tiles_ref, sem,
):
    size = LANES
    parts = tiles_hbm.shape[0] // PART
    copies = []
    for part in range(parts):
        at = pl.ds(PART * part, PART)
        copies.append(pltpu.make_async_copy(tiles_hbm.at[at], tiles_ref.at[at], sem.at[part]))
    for copy in copies:
        copy.start()
    total[...] = jnp.zeros_like(total)
    for place, ref in enumerate((before_ref, own_ref, after_ref)):
        charges_ref[pl.ds(24 * place, 24), :] = ref[...]

    def slot(place, carry):
        rows = pl.ds(pl.multiple_of(target_ref[place] * size, size), size)
        code = source_ref[place]
        neighbour = code >> 3
        row = neighbour // 3
        line = 24 * (neighbour - 3 * row) + 8 * row + (code & 7)
        source = charges_ref[pl.ds(line, 1), :]
        total[rows, :] = total[rows, :] + tiles_ref[place] * source
        return carry

    for part, copy in enumerate(copies):
        copy.wait()
        start = PART * part
        lax.fori_loop(start, jnp.clip(count_ref[0], start, start + PART), slot, 0)
    ones = jnp.ones((8, size), BF16)
    result = sum(dot(ones, part, ((1,), (1,))) for part in thirds(total[...]))
    out_ref[...] = result[0:1]


def shifted(value, axis, by):
    size = lax.axis_size(axis)
    return lax.ppermute(value, axis, [(i, (i + by) % size) for i in range(size)])


def near_field(beside, near_count, near_target, near_source, near_tiles):
    slots, size, _ = near_tiles.shape
    before, after = shifted(beside, "col", 1), shifted(beside, "col", -1)
    smem = pl.BlockSpec(memory_space=pltpu.SMEM)
    vmem = pl.BlockSpec(memory_space=pltpu.VMEM)
    return pl.pallas_call(
        near_kernel,
        in_specs=[smem, smem, smem, vmem, vmem, vmem, pl.BlockSpec(memory_space=pltpu.HBM)],
        out_shape=jax.ShapeDtypeStruct((1, TRI), F32),
        scratch_shapes=[
            pltpu.VMEM((72, size), F32),
            pltpu.VMEM((TRI, size), F32),
            pltpu.VMEM((slots, size, size), F32),
            pltpu.SemaphoreType.DMA((slots // PART,)),
        ],
        compiler_params=params(8),
        name="near",
    )(
        near_count,
        near_target,
        near_source,
        before,
        beside,
        after,
        pltpu.with_memory_space_constraint(near_tiles, pltpu.HBM),
    )


def swapped(value, mask):
    return lax.ppermute(value, "row", [(i, i ^ mask) for i in range(ROWS)])


def exchange(values, axes, pieces):
    shaped = values.reshape(pieces, 1, values.size // pieces)
    moved = lax.all_to_all(shaped, axes, split_axis=0, concat_axis=0, tiled=True)
    return moved.reshape(values.shape)


def local(
    charges,
    anchors,
    stencil_weights,
    kernel_spectrum,
    near_count,
    near_target,
    near_source,
    near_tiles,
):
    lines = line_table()
    table = jnp.asarray(lines)
    turned = jnp.asarray(np.concatenate([lines[:, :, 0::2], lines[:, :, 1::2]], axis=2))
    devices = ROWS * COLS
    packed = jax.ShapeDtypeStruct((devices * LINES // LANES, LANES), F32)
    hbm = pl.BlockSpec(memory_space=pltpu.HBM)
    deposited, first, *sent = pl.pallas_call(
        deposit_kernel,
        out_shape=(packed, *[jax.ShapeDtypeStruct((size, LANES), F32) for size in (24, *[SENT] * HALF)]),
        in_specs=[hbm] * 5,
        scratch_shapes=[
            pltpu.VMEM((1, TRI), F32),
            pltpu.VMEM((3, TRI), jnp.int32),
            pltpu.VMEM((64, TRI), F32),
            pltpu.VMEM((2, G, G), BF16),
            pltpu.VMEM((2, CELLS_A * CELLS_B, LANES), F32),
            pltpu.VMEM((64, TRI), F32),
            pltpu.VMEM((4, 2 * SPREAD, TRI), BF16),
            pltpu.VMEM((LINES, G), F32),
            pltpu.SemaphoreType.DMA((6,)),
        ],
        compiler_params=params(20),
        name="deposit",
    )(
        *[
            pltpu.with_memory_space_constraint(value, pltpu.HBM)
            for value in (
                charges.reshape(1, TRI),
                anchors,
                stencil_weights,
                table,
                kernel_spectrum.reshape(CELLS_A * CELLS_B, G),
            )
        ]
    )
    received = exchange(deposited, BOTH, devices)
    first = swapped(first, ROWS - 1)
    joined = pl.pallas_call(
        join_kernel,
        out_shape=[jax.ShapeDtypeStruct((SENT + 8, LANES), F32)] * (HALF - 1),
        compiler_params=params(8),
        name="join",
    )(first, *sent[1:])
    joined = [swapped(value, step + 1) for step, value in enumerate(joined)]
    waves = pl.pallas_call(
        waves_kernel,
        out_shape=jax.ShapeDtypeStruct((2, G, LANES), F32),
        compiler_params=params(8),
        name="waves",
    )(first)
    spectrum, beside = pl.pallas_call(
        spectrum_kernel,
        out_shape=(
            jax.ShapeDtypeStruct((G, G), F32),
            jax.ShapeDtypeStruct((24, LANES), F32),
        ),
        scratch_shapes=[pltpu.VMEM((2 * CELLS_A * HALF + 8, LANES), F32)],
        compiler_params=params(8),
        name="spectrum",
    )(first, sent[0], *joined)
    handed = pl.pallas_call(
        plane_kernel, out_shape=packed, compiler_params=params(12), name="plane"
    )(received, spectrum, waves)
    field = exchange(handed, BOTH, devices)
    beside, _ = lax.optimization_barrier((beside, handed))
    near = near_field(beside, near_count, near_target, near_source, near_tiles)
    result = pl.pallas_call(
        gather_kernel,
        out_shape=jax.ShapeDtypeStruct((1, TRI), F32),
        scratch_shapes=[
            pltpu.VMEM((LINES, G), F32),
            pltpu.VMEM((SHIFTS * SPREAD, G), BF16),
            pltpu.VMEM((TRI // CHUNK, SHIFTS * SPREAD, CHUNK), F32),
        ],
        compiler_params=params(20),
        name="gather",
    )(field, anchors, stencil_weights, turned, near)
    return result.reshape(TRI)


def solution(mesh):
    return jax.shard_map(
        local,
        mesh=mesh,
        in_specs=(
            P(("row", "col")),
            P(None, ("row", "col")),
            P(None, ("row", "col")),
            P("row", "col", None),
            P(("row", "col")),
            P(("row", "col")),
            P(("row", "col")),
            P(("row", "col"), None, None),
        ),
        out_specs=P(("row", "col")),
        check_vma=False,
    )
```

```python
import math

import jax
import jax.numpy as jnp
import ml_dtypes
import numpy as np
from jax import lax
from jax.experimental import pallas as pl
from jax.experimental.pallas import tpu as pltpu
from jax.sharding import PartitionSpec as P

G = 256
ROWS = 8
COLS = 32
CELLS_A = 32
CELLS_B = 8
TRI = 1024
LINES_B = 10
MAIN = LINES_B * CELLS_A
BLOCKS = 12
LINES = BLOCKS * CELLS_A
SPREAD = MAIN + CELLS_A
LANES = 128
TILES = TRI // LANES
HALF = ROWS // 2
SENT = 2 * CELLS_A + 8
CHUNK = 256
PART = 8
SHIFTS = 5
GROUPS = ((0, 4, 8), (1, 5, 9), (2, 6), (3, 7))
F32 = jnp.float32
BF16 = jnp.bfloat16
BOTH = ("row", "col")


def params(mebibytes):
    return pltpu.CompilerParams(vmem_limit_bytes=mebibytes * 1024 * 1024)


def split_table(table):
    high = table.astype(np.float32).astype(ml_dtypes.bfloat16)
    low = (table - high.astype(np.float64)).astype(np.float32).astype(ml_dtypes.bfloat16)
    return np.stack([high, low])


def cas(first, second):
    angle = (np.outer(first, second) % G) * (2.0 * np.pi / G)
    return np.cos(angle) + np.sin(angle)


def row_at(slot, block):
    return 4 * (slot // 4) + (slot - block) % 4


def line_table():
    steps = np.arange(G)
    device = np.arange(ROWS * COLS)
    plane = CELLS_B * (device % COLS) + device // COLS
    return split_table(cas(plane, steps))


def halves(value):
    high = value.astype(BF16)
    low = (value - high.astype(F32)).astype(BF16)
    return high, low


def paired(value):
    high = value.astype(BF16).astype(F32)
    return jnp.concatenate([high, value - high], axis=0).astype(BF16)


def thirds(value):
    parts = []
    for _ in range(3):
        parts.append(value.astype(BF16))
        value = value - parts[-1].astype(F32)
    return parts


def dot(left, right, dims=((1,), (0,))):
    return lax.dot_general(left, right, (dims, ((), ())), preferred_element_type=F32)


def dot_table(rows, table, dims=((1,), (0,))):
    high, low = rows
    size = high.shape[0]
    both = dot(jnp.concatenate([high, low], axis=0), table[0], dims)
    return both[:size] + (both[size:] + dot(high, table[1], dims))


def table_dot(table, value, dims=((1,), (0,))):
    high, low = value
    size = table[0].shape[0]
    both = dot(jnp.concatenate([table[0], table[1]], axis=0), high, dims)
    return both[:size] + (both[size:] + dot(table[0], low, dims))


def block_place(block):
    slot = (lax.axis_index("row") + block) & 3
    return pl.ds(pl.multiple_of(LANES * (block // 4) + CELLS_A * slot, CELLS_A), CELLS_A)


def onehot(anchors_ref):
    cells = lax.broadcasted_iota(jnp.int32, (LANES, TRI), 0)
    matched = cells == anchors_ref[2:3, :] >> 1
    return jnp.where(matched, 1.0, 0.0).astype(BF16)


def local_place(anchors_ref, at):
    first = (anchors_ref[0:1, at] - (lax.axis_index("row") * CELLS_A - 1)) & (G - 1)
    second = (anchors_ref[1:2, at] - (lax.axis_index("col") * CELLS_B - 1)) & (G - 1)
    first = jnp.broadcast_to(first, (8, LANES))
    second = jnp.broadcast_to(second, (8, LANES))
    return lax.broadcasted_iota(jnp.int32, (8, LANES), 0) - (first & 7), first >> 3, second


def masks_of(place):
    relative, group, second = place
    near_masks = [relative == i for i in range(4)]
    next_masks = [relative == i - 8 for i in range(1, 4)]
    groups = [group == g for g in range(4)]
    bits = [(second & bit) != 0 for bit in (1, 2, 4)]
    return near_masks, next_masks, groups, bits


def two_rows(rows, near_masks, next_masks):
    near = jnp.zeros((8, LANES), F32)
    after = jnp.zeros((8, LANES), F32)
    for i in range(4):
        near = jnp.where(near_masks[i], rows[i], near)
    for i in range(1, 4):
        after = jnp.where(next_masks[i - 1], rows[i], after)
    return near, after


def stencil_rows(ref, j, k, at):
    return [
        jnp.broadcast_to(ref[16 * i + 4 * j + k, at][None, :], (8, LANES)) for i in range(4)
    ]


def spread_tile(scaled, place, spread, k, tile):
    at = pl.ds(tile * LANES, LANES)
    zero = jnp.zeros((8, LANES), F32)
    none = jnp.zeros((16, LANES), BF16)
    near_masks, next_masks, groups, bits = masks_of(place)
    _, group, second = place
    group, second = [jnp.concatenate([part, part], axis=0) for part in (group, second)]
    wide_groups = [group == g for g in range(4)]
    wide_bits = [(second & bit) != 0 for bit in (1, 2, 4)]
    blocks, rims = [], []
    for j in range(4):
        rows = two_rows(stencil_rows(scaled, j, k, at), near_masks, next_masks)
        blocks.append([paired(row) for row in rows])
        rim = jnp.where(groups[3], rows[1], zero)
        rim = rim + pltpu.roll(rim, 2, 0)
        rims.append(rim + pltpu.roll(rim, 4, 0))
    for mask, shift, count in zip(wide_bits, (1, 2, 4), (5, 7, 10)):
        wider = []
        for line in range(count):
            if line < shift:
                wider.append([jnp.where(mask, none, low) for low in blocks[line]])
            elif line >= len(blocks):
                wider.append([jnp.where(mask, high, none) for high in blocks[line - shift]])
            else:
                pairs = zip(blocks[line - shift], blocks[line])
                wider.append([jnp.where(mask, high, low) for high, low in pairs])
        blocks = wider
    for line in range(LINES_B):
        near, after = blocks[line]
        for v in range(4):
            piece = jnp.where(wide_groups[v], near, none)
            piece = jnp.where(wide_groups[v - 1], after, piece) if v else piece
            spread[k, pl.ds(2 * (CELLS_A * line + 8 * v), 16), at] = piece
    beyond = (lax.broadcasted_iota(jnp.int32, (8, LANES), 0) >> 1) - place[2]
    for v in range(3):
        piece = zero
        for j in range(4):
            piece = jnp.where(beyond == j - 4 * v, rims[j], piece)
        spread[k, pl.ds(2 * (MAIN + 8 * v), 16), at] = paired(piece)
    spread[k, pl.ds(2 * (MAIN + 24), 16), at] = none


def deposit_kernel(
    charges_hbm, anchors_hbm, weights_hbm, table_hbm, spectrum_hbm, out_ref, *rest
):
    first_ref, sent_refs = rest[0], rest[1 : 1 + HALF]
    charges_ref, anchors_ref, weights_ref, table_ref, spectrum_ref = rest[1 + HALF : 6 + HALF]
    scaled, spread, lines, sem = rest[6 + HALF :]
    pairs = (
        (weights_hbm, weights_ref),
        (anchors_hbm, anchors_ref),
        (charges_hbm, charges_ref),
        (spectrum_hbm.at[:, pl.ds(0, LANES)], spectrum_ref.at[0, pl.ds(0, G)]),
        (spectrum_hbm.at[:, pl.ds(LANES, LANES)], spectrum_ref.at[1, pl.ds(0, G)]),
        (table_hbm, table_ref),
    )
    copies = [pltpu.make_async_copy(a, b, sem.at[n]) for n, (a, b) in enumerate(pairs)]
    for copy in copies:
        copy.start()
    for copy in copies[:3]:
        copy.wait()
    scaled[...] = weights_ref[...] * charges_ref[...]
    places = [local_place(anchors_ref, pl.ds(tile * LANES, LANES)) for tile in range(TILES)]
    cells = lax.broadcasted_iota(jnp.int32, (LANES, G), 1)
    hot = []
    for tile in range(TILES):
        row = anchors_ref[2:3, pl.ds(tile * LANES, LANES)]
        column = jnp.broadcast_to(row, (LANES, LANES)).T
        column = jnp.concatenate([column, column], axis=1)
        hot.append(jnp.where(cells == column, 1.0, 0.0).astype(BF16))
    hot = jnp.concatenate(hot, axis=0)
    total = None
    for k in (1, 2, 3, 0):
        for tile in range(TILES):
            spread_tile(scaled, places[tile], spread, k, tile)
        placed = dot(spread[k], hot).reshape(SPREAD // 8, 2, 8, G)
        placed = (placed[:, 0] + placed[:, 1]).reshape(SPREAD, G)
        placed = pltpu.roll(placed, k, 1) if k else placed
        total = placed if total is None else total + placed
    for block in range(LINES_B + 1):
        lines[block_place(block), :] = total[CELLS_A * block : CELLS_A * (block + 1)]
    lines[block_place(LINES_B + 1), :] = jnp.zeros((CELLS_A, G), F32)
    for copy in copies[3:]:
        copy.wait()
    result = table_dot((table_ref[0], table_ref[1]), halves(lines[...]), ((1,), (1,)))
    for v in range(3):
        out_ref[pl.ds(v, G, stride=3), :] = result[:, LANES * v : LANES * (v + 1)]
    for half in range(2):
        first_ref[pl.ds(CELLS_B * half, CELLS_B), :] = spectrum_ref[half, pl.ds(0, CELLS_B), :]
    for step, sent in enumerate(sent_refs):
        c = lax.axis_index("row") ^ step
        for half in range(2):
            rows = spectrum_ref[half, pl.ds(c, CELLS_A, stride=CELLS_B), :]
            sent[pl.ds(CELLS_A * half, CELLS_A), :] = rows
    for block in range(8):
        charges = charges_ref[:, pl.ds(block * LANES, LANES)]
        first_ref[pl.ds(16 + block, 1), :] = charges
        for sent in sent_refs:
            sent[pl.ds(2 * CELLS_A + block, 1), :] = charges


def join_kernel(first_ref, *refs):
    row = lax.axis_index("row")
    for step in range(1, HALF):
        sent, out = refs[step - 1], refs[step + HALF - 2]
        out[pl.ds(0, SENT), :] = sent[...]
        out[pl.ds(SENT, 8), :] = line_of(first_ref, row ^ step)


def line_of(first_ref, c):
    halves_of = [first_ref[pl.ds(c + CELLS_B * half, 1), :] for half in range(2)]
    return jnp.concatenate([*halves_of, jnp.zeros((6, LANES), F32)], axis=0)


def waves_kernel(_, waves_ref):
    for half in range(2):
        cell = lax.broadcasted_iota(jnp.int32, (G, LANES), 0) - 1
        wave = lax.broadcasted_iota(jnp.int32, (G, LANES), 1) + LANES * half
        waves_ref[half] = cas_of(cell * wave)


def cas_of(turns):
    centred = ((turns + 3 * G // 8) & (G - 1)) - G // 2
    angle = (G // 4 - jnp.abs(centred)).astype(F32) * (2.0 * math.pi / G)
    square = angle * angle
    value = jnp.full_like(square, math.sqrt(2.0) / math.factorial(13))
    for power in (11, 9, 7, 5, 3, 1):
        sign = 1.0 if power % 4 == 1 else -1.0
        value = value * square + sign * math.sqrt(2.0) / math.factorial(power)
    return value * angle


def spectrum_kernel(first_ref, own_ref, *refs):
    received, (out_ref, beside_ref, joined) = refs[: HALF - 1], refs[HALF - 1 :]
    row = lax.axis_index("row")
    place = row & (HALF - 1)
    missing = line_of(first_ref, row)
    for step, ref in enumerate((own_ref, *received)):
        at = pl.ds(pl.multiple_of(2 * CELLS_A * (place ^ step), 2 * CELLS_A), 2 * CELLS_A)
        joined[at, :] = ref[pl.ds(0, 2 * CELLS_A), :]
        if step:
            missing = jnp.where(place ^ step == HALF - 1, ref[pl.ds(SENT, 8), :], missing)
    joined[pl.ds(2 * CELLS_A * HALF, 8), :] = missing
    charges = pl.ds(2 * CELLS_A, 8)
    nearest = received[0][charges, :]
    outside = (place == 0) | (place == HALF - 1)
    other = jnp.where(outside, first_ref[pl.ds(16, 8), :], received[2][charges, :])
    odd = (row & 1) == 1
    beside_ref[pl.ds(0, 8), :] = jnp.where(odd, nearest, other)
    beside_ref[pl.ds(8, 8), :] = own_ref[charges, :]
    beside_ref[pl.ds(16, 8), :] = jnp.where(odd, other, nearest)
    shape = (G, joined.shape[0])
    line = lax.broadcasted_iota(jnp.int32, shape, 0)
    line = jnp.minimum(line, G - line)
    line = jnp.where(row >= HALF, G // 2 - line, line)
    source = 2 * CELLS_A * (line >> 5) + (line & (CELLS_A - 1))
    pitch = jnp.where(line == G // 2, 1, CELLS_A)
    source = lax.broadcasted_iota(jnp.int32, shape, 1) - source
    parts = thirds(joined[...])
    for half in range(2):
        chosen = jnp.where(source == half * pitch, 1.0, 0.0).astype(BF16)
        value = sum(dot(chosen, part) for part in parts)
        out_ref[:, pl.ds(LANES * half, LANES)] = value * (1.0 / (G * G * G))


def plane_kernel(tiles_ref, spectrum_ref, waves_ref, out_ref):
    lane = lax.broadcasted_iota(jnp.int32, (CELLS_A, LANES), 1)
    slots = [(lane >> 5) == s for s in range(4)]
    wide = lax.broadcasted_iota(jnp.int32, (CELLS_A, G), 1)
    pairs = [((wide & 31) >> 1) == line for line in range(LINES_B)]
    pieces = [
        [tiles_ref[pl.ds(96 * r + v, CELLS_A, stride=3), :] for v in range(3)] for r in range(ROWS)
    ]

    def joined(block):
        parts = []
        for w in range(2):
            value = None
            for s in range(4):
                piece = pieces[4 * w + s][block // 4]
                value = piece if value is None else jnp.where(slots[(block + s) & 3], piece, value)
            parts.append(value)
        return jnp.concatenate(parts, axis=1)

    def waves(start, count, stride=1):
        rows = [waves_ref[half, pl.ds(start, count, stride=stride), :] for half in range(2)]
        return jnp.concatenate(rows, axis=1)

    first = halves(waves(0, G))
    even = (lax.broadcasted_iota(jnp.int32, (CELLS_A, G), 0) & 1) == 0
    outer = []
    for slot in range(ROWS):
        start = CELLS_A * ((row_at(slot, LINES_B) + 1) % ROWS)
        outer.append(jnp.where(even, waves(start, 1), waves(start + 1, 1)))
    outer = halves(jnp.concatenate(outer, axis=0))
    lines = [line for group in GROUPS for line in group]
    flipped = []
    for line in lines:
        rows = waves(line % CELLS_B, COLS, CELLS_B)
        flipped.append(pltpu.roll(rows, COLS - 1, 0) if line >= CELLS_B else rows)
    flipped = jnp.concatenate([*flipped, jnp.zeros((LINES - MAIN, G), F32)], axis=0)
    second = halves(flipped.T[:, :MAIN])
    flipped = halves(flipped[:MAIN])

    def table(m):
        order = [row_at(slot, m) for slot in range(ROWS)]
        return [
            jnp.concatenate([part[CELLS_A * r : CELLS_A * (r + 1)] for r in order], axis=0)
            for part in first
        ]

    rim = joined(LINES_B)
    main = [
        halves(jnp.concatenate([joined(line) for line in group], axis=0)) for group in GROUPS
    ]
    rims = halves(jnp.concatenate([jnp.where(pairs[line], rim, 0.0) for line in lines], axis=0))
    half = jnp.concatenate([dot_table(rows, table(m)) for m, rows in enumerate(main)], axis=0)
    half = halves(half + dot_table(rims, outer))
    image = table_dot(second, half) * spectrum_ref[...]
    half = halves(table_dot(flipped, halves(image)))
    rims = dot_table(half, outer, ((1,), (1,)))
    blocks, at = {}, 0
    for m, group in enumerate(GROUPS):
        size = CELLS_A * len(group)
        rows = [part[at : at + size] for part in half]
        value = dot_table(rows, table(m), ((1,), (1,)))
        for place, line in enumerate(group):
            blocks[line] = value[CELLS_A * place : CELLS_A * (place + 1)]
        at += size
    zero = jnp.zeros((CELLS_A, G), F32)
    rim = zero
    for place, line in enumerate(lines):
        rim = jnp.where(pairs[line], rims[CELLS_A * place : CELLS_A * (place + 1)], rim)
    blocks[LINES_B], blocks[LINES_B + 1] = rim, zero
    for r in range(ROWS):
        lanes = slice(LANES * (r // 4), LANES * (r // 4 + 1))
        for v in range(3):
            value = None
            for block in range(4 * v, 4 * v + 4):
                piece = blocks[block][:, lanes]
                value = piece if value is None else jnp.where(slots[(block + r) & 3], piece, value)
            out_ref[pl.ds(96 * r + v, CELLS_A, stride=3), :] = value


def gather_tile(weights_ref, anchors_ref, place, picked, tile, base, at):
    near_masks, next_masks, groups, bits = masks_of(place)
    weights_at = pl.ds(tile * LANES, LANES)
    odd = jnp.broadcast_to((anchors_ref[2:3, weights_at] & 1) != 0, (8, LANES))
    total = jnp.zeros((8, LANES), F32)
    before = None
    for shift in range(SHIFTS):
        blocks = []
        for line in range(LINES_B):
            start = SPREAD * shift + CELLS_A * line
            rows = [picked[base, pl.ds(start + 8 * v, 8), at] for v in range(4)]
            last = picked[base, pl.ds(SPREAD * shift + MAIN + 8 * (line // 4), 8), at]
            rows.append(pltpu.roll(last, 8 - 2 * (line % 4), 0) if line % 4 else last)
            pair = []
            for skip in range(2):
                chosen = rows[skip]
                for g in range(1, 4):
                    chosen = jnp.where(groups[g], rows[g + skip], chosen)
                pair.append(chosen)
            blocks.append(pair)
        for mask, width, count in zip(bits[::-1], (4, 2, 1), (7, 5, 4)):
            fewer = []
            for line in range(count):
                low = blocks[line]
                if line + width < len(blocks):
                    high = blocks[line + width]
                    low = [jnp.where(mask, h, l) for h, l in zip(high, low)]
                fewer.append(low)
            blocks = fewer
        if shift:
            for j in range(4):
                rows = stencil_rows(weights_ref, j, shift - 1, weights_at)
                weights = two_rows(rows, near_masks, next_masks)
                for weight, high, low in zip(weights, blocks[j], before[j]):
                    total = total + weight * jnp.where(odd, high, low)
        before = blocks
    return jnp.sum(total, axis=0, keepdims=True)


def gather_kernel(
    field_ref, anchors_ref, weights_ref, table_ref, near_ref, out_ref, lines, parts, picked
):
    turned = [field_ref[pl.ds(v, G, stride=3), :].T for v in range(3)]
    turned = halves(jnp.concatenate(turned, axis=0))
    lines[...] = dot_table(turned, (table_ref[0], table_ref[1]))
    field = jnp.concatenate([lines[block_place(b), :] for b in range(LINES_B + 1)], axis=0)
    for shift in range(SHIFTS):
        value = field[:, LANES * (shift % 2) : LANES * (shift % 2 + 1)]
        high, low = halves(pltpu.roll(value, LANES - shift // 2, 1) if shift > 1 else value)
        rows = pl.ds(SPREAD * shift, SPREAD)
        parts[rows, pl.ds(0, LANES)] = high
        parts[rows, pl.ds(LANES, LANES)] = low
    hot = onehot(anchors_ref)
    hot = jnp.concatenate([hot, hot], axis=0)
    for chunk in range(TRI // CHUNK):
        picked[chunk] = dot(parts[...], hot[:, CHUNK * chunk : CHUNK * (chunk + 1)])
        for step in range(CHUNK // LANES):
            tile = chunk * (CHUNK // LANES) + step
            at = pl.ds(tile * LANES, LANES)
            place = local_place(anchors_ref, at)
            value = gather_tile(
                weights_ref, anchors_ref, place, picked, tile, chunk, pl.ds(step * LANES, LANES)
            )
            out_ref[:, at] = value + near_ref[:, at]


def near_kernel(
    count_ref, target_ref, source_ref, before_ref, own_ref, after_ref, tiles_hbm, out_ref,
    charges_ref, total, tiles_ref, sem,
):
    size = LANES
    parts = tiles_hbm.shape[0] // PART
    copies = []
    for part in range(parts):
        at = pl.ds(PART * part, PART)
        copies.append(pltpu.make_async_copy(tiles_hbm.at[at], tiles_ref.at[at], sem.at[part]))
    for copy in copies:
        copy.start()
    total[...] = jnp.zeros_like(total)
    for place, ref in enumerate((before_ref, own_ref, after_ref)):
        charges_ref[pl.ds(24 * place, 24), :] = ref[...]

    def slot(place, carry):
        rows = pl.ds(pl.multiple_of(target_ref[place] * size, size), size)
        code = source_ref[place]
        neighbour = code >> 3
        row = neighbour // 3
        line = 24 * (neighbour - 3 * row) + 8 * row + (code & 7)
        source = charges_ref[pl.ds(line, 1), :]
        total[rows, :] = total[rows, :] + tiles_ref[place] * source
        return carry

    for part, copy in enumerate(copies):
        copy.wait()
        start = PART * part
        lax.fori_loop(start, jnp.clip(count_ref[0], start, start + PART), slot, 0)
    ones = jnp.ones((8, size), BF16)
    result = sum(dot(ones, part, ((1,), (1,))) for part in thirds(total[...]))
    out_ref[...] = result[0:1]


def shifted(value, axis, by):
    size = lax.axis_size(axis)
    return lax.ppermute(value, axis, [(i, (i + by) % size) for i in range(size)])


def near_field(beside, near_count, near_target, near_source, near_tiles):
    slots, size, _ = near_tiles.shape
    before, after = shifted(beside, "col", 1), shifted(beside, "col", -1)
    smem = pl.BlockSpec(memory_space=pltpu.SMEM)
    vmem = pl.BlockSpec(memory_space=pltpu.VMEM)
    return pl.pallas_call(
        near_kernel,
        in_specs=[smem, smem, smem, vmem, vmem, vmem, pl.BlockSpec(memory_space=pltpu.HBM)],
        out_shape=jax.ShapeDtypeStruct((1, TRI), F32),
        scratch_shapes=[
            pltpu.VMEM((80, size), F32),
            pltpu.VMEM((TRI, size), F32),
            pltpu.VMEM((slots, size, size), F32),
            pltpu.SemaphoreType.DMA((slots // PART,)),
        ],
        compiler_params=params(8),
        name="near",
    )(
        near_count,
        near_target,
        near_source,
        before,
        beside,
        after,
        pltpu.with_memory_space_constraint(near_tiles, pltpu.HBM),
    )


def swapped(value, mask):
    return lax.ppermute(value, "row", [(i, i ^ mask) for i in range(ROWS)])


def exchange(values, axes, pieces):
    shaped = values.reshape(pieces, 1, values.size // pieces)
    moved = lax.all_to_all(shaped, axes, split_axis=0, concat_axis=0, tiled=True)
    return moved.reshape(values.shape)


def local(
    charges,
    anchors,
    stencil_weights,
    kernel_spectrum,
    near_count,
    near_target,
    near_source,
    near_tiles,
):
    lines = line_table()
    table = jnp.asarray(lines)
    turned = jnp.asarray(np.concatenate([lines[:, :, 0::2], lines[:, :, 1::2]], axis=2))
    devices = ROWS * COLS
    packed = jax.ShapeDtypeStruct((devices * LINES // LANES, LANES), F32)
    hbm = pl.BlockSpec(memory_space=pltpu.HBM)
    deposited, first, *sent = pl.pallas_call(
        deposit_kernel,
        out_shape=(packed, *[jax.ShapeDtypeStruct((size, LANES), F32) for size in (24, *[SENT] * HALF)]),
        in_specs=[hbm] * 5,
        scratch_shapes=[
            pltpu.VMEM((1, TRI), F32),
            pltpu.VMEM((3, TRI), jnp.int32),
            pltpu.VMEM((64, TRI), F32),
            pltpu.VMEM((2, G, G), BF16),
            pltpu.VMEM((2, CELLS_A * CELLS_B + 8, LANES), F32),
            pltpu.VMEM((64, TRI), F32),
            pltpu.VMEM((4, 2 * SPREAD, TRI), BF16),
            pltpu.VMEM((LINES, G), F32),
            pltpu.SemaphoreType.DMA((6,)),
        ],
        compiler_params=params(20),
        name="deposit",
    )(
        *[
            pltpu.with_memory_space_constraint(value, pltpu.HBM)
            for value in (
                charges.reshape(1, TRI),
                anchors,
                stencil_weights,
                table,
                kernel_spectrum.reshape(CELLS_A * CELLS_B, G),
            )
        ]
    )
    received = exchange(deposited, BOTH, devices)
    first = swapped(first, ROWS - 1)
    joined = pl.pallas_call(
        join_kernel,
        out_shape=[jax.ShapeDtypeStruct((SENT + 8, LANES), F32)] * (HALF - 1),
        compiler_params=params(8),
        name="join",
    )(first, *sent[1:])
    joined = [swapped(value, step + 1) for step, value in enumerate(joined)]
    waves = pl.pallas_call(
        waves_kernel,
        out_shape=jax.ShapeDtypeStruct((2, G, LANES), F32),
        compiler_params=params(8),
        name="waves",
    )(first)
    spectrum, beside = pl.pallas_call(
        spectrum_kernel,
        out_shape=(
            jax.ShapeDtypeStruct((G, G), F32),
            jax.ShapeDtypeStruct((24, LANES), F32),
        ),
        scratch_shapes=[pltpu.VMEM((2 * CELLS_A * HALF + 8, LANES), F32)],
        compiler_params=params(8),
        name="spectrum",
    )(first, sent[0], *joined)
    handed = pl.pallas_call(
        plane_kernel, out_shape=packed, compiler_params=params(12), name="plane"
    )(received, spectrum, waves)
    field = exchange(handed, BOTH, devices)
    beside, _ = lax.optimization_barrier((beside, handed))
    near = near_field(beside, near_count, near_target, near_source, near_tiles)
    result = pl.pallas_call(
        gather_kernel,
        out_shape=jax.ShapeDtypeStruct((1, TRI), F32),
        scratch_shapes=[
            pltpu.VMEM((LINES, G), F32),
            pltpu.VMEM((SHIFTS * SPREAD, G), BF16),
            pltpu.VMEM((TRI // CHUNK, SHIFTS * SPREAD, CHUNK), F32),
        ],
        compiler_params=params(20),
        name="gather",
    )(field, anchors, stencil_weights, turned, near)
    return result.reshape(TRI)


def solution(mesh):
    return jax.shard_map(
        local,
        mesh=mesh,
        in_specs=(
            P(("row", "col")),
            P(None, ("row", "col")),
            P(None, ("row", "col")),
            P("row", "col", None),
            P(("row", "col")),
            P(("row", "col")),
            P(("row", "col")),
            P(("row", "col"), None, None),
        ),
        out_specs=P(("row", "col")),
        check_vma=False,
    )
```

```python
import math

import jax
import jax.numpy as jnp
import ml_dtypes
import numpy as np
from jax import lax
from jax.experimental import pallas as pl
from jax.experimental.pallas import tpu as pltpu
from jax.sharding import PartitionSpec as P

G = 256
ROWS = 8
COLS = 32
CELLS_A = 32
CELLS_B = 8
TRI = 1024
LINES_B = 10
MAIN = LINES_B * CELLS_A
BLOCKS = 12
LINES = BLOCKS * CELLS_A
SPREAD = MAIN + CELLS_A
LANES = 128
TILES = TRI // LANES
HALF = ROWS // 2
SENT = 2 * CELLS_A + 8
CHUNK = 256
PART = 8
SHIFTS = 5
GROUPS = ((0, 4, 8), (1, 5, 9), (2, 6), (3, 7))
F32 = jnp.float32
BF16 = jnp.bfloat16
BOTH = ("row", "col")


def params(mebibytes):
    return pltpu.CompilerParams(vmem_limit_bytes=mebibytes * 1024 * 1024)


def split_table(table):
    high = table.astype(np.float32).astype(ml_dtypes.bfloat16)
    low = (table - high.astype(np.float64)).astype(np.float32).astype(ml_dtypes.bfloat16)
    return np.stack([high, low])


def cas(first, second):
    angle = (np.outer(first, second) % G) * (2.0 * np.pi / G)
    return np.cos(angle) + np.sin(angle)


def row_at(slot, block):
    return 4 * (slot // 4) + (slot - block) % 4


def line_table():
    steps = np.arange(G)
    device = np.arange(ROWS * COLS)
    plane = CELLS_B * (device % COLS) + device // COLS
    return split_table(cas(plane, steps))


def halves(value):
    high = value.astype(BF16)
    low = (value - high.astype(F32)).astype(BF16)
    return high, low


def paired(value):
    high = value.astype(BF16).astype(F32)
    return jnp.concatenate([high, value - high], axis=0).astype(BF16)


def thirds(value):
    parts = []
    for _ in range(3):
        parts.append(value.astype(BF16))
        value = value - parts[-1].astype(F32)
    return parts


def dot(left, right, dims=((1,), (0,))):
    return lax.dot_general(left, right, (dims, ((), ())), preferred_element_type=F32)


def dot_table(rows, table, dims=((1,), (0,))):
    high, low = rows
    size = high.shape[0]
    both = dot(jnp.concatenate([high, low], axis=0), table[0], dims)
    return both[:size] + (both[size:] + dot(high, table[1], dims))


def table_dot(table, value, dims=((1,), (0,))):
    high, low = value
    size = table[0].shape[0]
    both = dot(jnp.concatenate([table[0], table[1]], axis=0), high, dims)
    return both[:size] + (both[size:] + dot(table[0], low, dims))


def block_place(block):
    slot = (lax.axis_index("row") + block) & 3
    return pl.ds(pl.multiple_of(LANES * (block // 4) + CELLS_A * slot, CELLS_A), CELLS_A)


def onehot(anchors_ref):
    cells = lax.broadcasted_iota(jnp.int32, (LANES, TRI), 0)
    matched = cells == anchors_ref[2:3, :] >> 1
    return jnp.where(matched, 1.0, 0.0).astype(BF16)


def local_place(anchors_ref, at):
    first = (anchors_ref[0:1, at] - (lax.axis_index("row") * CELLS_A - 1)) & (G - 1)
    second = (anchors_ref[1:2, at] - (lax.axis_index("col") * CELLS_B - 1)) & (G - 1)
    first = jnp.broadcast_to(first, (8, LANES))
    second = jnp.broadcast_to(second, (8, LANES))
    return lax.broadcasted_iota(jnp.int32, (8, LANES), 0) - (first & 7), first >> 3, second


def masks_of(place):
    relative, group, second = place
    near_masks = [relative == i for i in range(4)]
    next_masks = [relative == i - 8 for i in range(1, 4)]
    groups = [group == g for g in range(4)]
    bits = [(second & bit) != 0 for bit in (1, 2, 4)]
    return near_masks, next_masks, groups, bits


def two_rows(rows, near_masks, next_masks):
    near = jnp.zeros((8, LANES), F32)
    after = jnp.zeros((8, LANES), F32)
    for i in range(4):
        near = jnp.where(near_masks[i], rows[i], near)
    for i in range(1, 4):
        after = jnp.where(next_masks[i - 1], rows[i], after)
    return near, after


def stencil_rows(ref, j, k, at):
    return [
        jnp.broadcast_to(ref[16 * i + 4 * j + k, at][None, :], (8, LANES)) for i in range(4)
    ]


def spread_tile(scaled, place, spread, k, tile):
    at = pl.ds(tile * LANES, LANES)
    zero = jnp.zeros((8, LANES), F32)
    none = jnp.zeros((16, LANES), BF16)
    near_masks, next_masks, groups, bits = masks_of(place)
    _, group, second = place
    group, second = [jnp.concatenate([part, part], axis=0) for part in (group, second)]
    wide_groups = [group == g for g in range(4)]
    wide_bits = [(second & bit) != 0 for bit in (1, 2, 4)]
    blocks, rims = [], []
    for j in range(4):
        rows = two_rows(stencil_rows(scaled, j, k, at), near_masks, next_masks)
        blocks.append([paired(row) for row in rows])
        rim = jnp.where(groups[3], rows[1], zero)
        rim = rim + pltpu.roll(rim, 2, 0)
        rims.append(rim + pltpu.roll(rim, 4, 0))
    for mask, shift, count in zip(wide_bits, (1, 2, 4), (5, 7, 10)):
        wider = []
        for line in range(count):
            if line < shift:
                wider.append([jnp.where(mask, none, low) for low in blocks[line]])
            elif line >= len(blocks):
                wider.append([jnp.where(mask, high, none) for high in blocks[line - shift]])
            else:
                pairs = zip(blocks[line - shift], blocks[line])
                wider.append([jnp.where(mask, high, low) for high, low in pairs])
        blocks = wider
    for line in range(LINES_B):
        near, after = blocks[line]
        for v in range(4):
            piece = jnp.where(wide_groups[v], near, none)
            piece = jnp.where(wide_groups[v - 1], after, piece) if v else piece
            spread[k, pl.ds(2 * (CELLS_A * line + 8 * v), 16), at] = piece
    beyond = (lax.broadcasted_iota(jnp.int32, (8, LANES), 0) >> 1) - place[2]
    for v in range(3):
        piece = zero
        for j in range(4):
            piece = jnp.where(beyond == j - 4 * v, rims[j], piece)
        spread[k, pl.ds(2 * (MAIN + 8 * v), 16), at] = paired(piece)
    spread[k, pl.ds(2 * (MAIN + 24), 16), at] = none


def deposit_kernel(
    charges_hbm, anchors_hbm, weights_hbm, table_hbm, spectrum_hbm, out_ref, *rest
):
    first_ref, sent_refs = rest[0], rest[1 : 1 + HALF]
    charges_ref, anchors_ref, weights_ref, table_ref, spectrum_ref = rest[1 + HALF : 6 + HALF]
    scaled, spread, lines, sem = rest[6 + HALF :]
    pairs = (
        (weights_hbm, weights_ref),
        (anchors_hbm, anchors_ref),
        (charges_hbm, charges_ref),
        (spectrum_hbm.at[:, pl.ds(0, LANES)], spectrum_ref.at[0, pl.ds(0, G)]),
        (spectrum_hbm.at[:, pl.ds(LANES, LANES)], spectrum_ref.at[1, pl.ds(0, G)]),
        (table_hbm, table_ref),
    )
    copies = [pltpu.make_async_copy(a, b, sem.at[n]) for n, (a, b) in enumerate(pairs)]
    for copy in copies:
        copy.start()
    for copy in copies[:3]:
        copy.wait()
    scaled[...] = weights_ref[...] * charges_ref[...]
    places = [local_place(anchors_ref, pl.ds(tile * LANES, LANES)) for tile in range(TILES)]
    cells = lax.broadcasted_iota(jnp.int32, (LANES, G), 1)
    hot = []
    for tile in range(TILES):
        row = anchors_ref[2:3, pl.ds(tile * LANES, LANES)]
        column = jnp.broadcast_to(row, (LANES, LANES)).T
        column = jnp.concatenate([column, column], axis=1)
        hot.append(jnp.where(cells == column, 1.0, 0.0).astype(BF16))
    hot = jnp.concatenate(hot, axis=0)
    total = None
    for k in (1, 2, 3, 0):
        for tile in range(TILES):
            spread_tile(scaled, places[tile], spread, k, tile)
        placed = dot(spread[k], hot).reshape(SPREAD // 8, 2, 8, G)
        placed = (placed[:, 0] + placed[:, 1]).reshape(SPREAD, G)
        placed = pltpu.roll(placed, k, 1) if k else placed
        total = placed if total is None else total + placed
    for block in range(LINES_B + 1):
        lines[block_place(block), :] = total[CELLS_A * block : CELLS_A * (block + 1)]
    lines[block_place(LINES_B + 1), :] = jnp.zeros((CELLS_A, G), F32)
    for copy in copies[3:]:
        copy.wait()
    result = table_dot((table_ref[0], table_ref[1]), halves(lines[...]), ((1,), (1,)))
    for v in range(3):
        out_ref[pl.ds(v, G, stride=3), :] = result[:, LANES * v : LANES * (v + 1)]
    for half in range(2):
        first_ref[pl.ds(CELLS_B * half, CELLS_B), :] = spectrum_ref[half, pl.ds(0, CELLS_B), :]
    for step, sent in enumerate(sent_refs):
        c = lax.axis_index("row") ^ step
        for half in range(2):
            rows = spectrum_ref[half, pl.ds(c, CELLS_A, stride=CELLS_B), :]
            sent[pl.ds(CELLS_A * half, CELLS_A), :] = rows
    for block in range(8):
        charges = charges_ref[:, pl.ds(block * LANES, LANES)]
        first_ref[pl.ds(16 + block, 1), :] = charges
        for sent in sent_refs:
            sent[pl.ds(2 * CELLS_A + block, 1), :] = charges


def join_kernel(first_ref, *refs):
    row = lax.axis_index("row")
    for step in range(1, HALF):
        sent, out = refs[step - 1], refs[step + HALF - 2]
        out[pl.ds(0, SENT), :] = sent[...]
        out[pl.ds(SENT, 8), :] = line_of(first_ref, row ^ step)


def line_of(first_ref, c):
    halves_of = [first_ref[pl.ds(c + CELLS_B * half, 1), :] for half in range(2)]
    return jnp.concatenate([*halves_of, jnp.zeros((6, LANES), F32)], axis=0)


def waves_kernel(_, waves_ref):
    for half in range(2):
        cell = lax.broadcasted_iota(jnp.int32, (G, LANES), 0) - 1
        wave = lax.broadcasted_iota(jnp.int32, (G, LANES), 1) + LANES * half
        waves_ref[half] = cas_of(cell * wave)


def cas_of(turns):
    centred = ((turns + 3 * G // 8) & (G - 1)) - G // 2
    angle = (G // 4 - jnp.abs(centred)).astype(F32) * (2.0 * math.pi / G)
    square = angle * angle
    value = jnp.full_like(square, math.sqrt(2.0) / math.factorial(13))
    for power in (11, 9, 7, 5, 3, 1):
        sign = 1.0 if power % 4 == 1 else -1.0
        value = value * square + sign * math.sqrt(2.0) / math.factorial(power)
    return value * angle


def spectrum_kernel(first_ref, own_ref, *refs):
    received, (out_ref, beside_ref, joined) = refs[: HALF - 1], refs[HALF - 1 :]
    row = lax.axis_index("row")
    place = row & (HALF - 1)
    missing = line_of(first_ref, row)
    for step, ref in enumerate((own_ref, *received)):
        at = pl.ds(pl.multiple_of(2 * CELLS_A * (place ^ step), 2 * CELLS_A), 2 * CELLS_A)
        joined[at, :] = ref[pl.ds(0, 2 * CELLS_A), :]
        if step:
            missing = jnp.where(place ^ step == HALF - 1, ref[pl.ds(SENT, 8), :], missing)
    joined[pl.ds(2 * CELLS_A * HALF, 8), :] = missing
    charges = pl.ds(2 * CELLS_A, 8)
    nearest = received[0][charges, :]
    outside = (place == 0) | (place == HALF - 1)
    other = jnp.where(outside, first_ref[pl.ds(16, 8), :], received[2][charges, :])
    odd = (row & 1) == 1
    beside_ref[pl.ds(0, 8), :] = jnp.where(odd, nearest, other)
    beside_ref[pl.ds(8, 8), :] = own_ref[charges, :]
    beside_ref[pl.ds(16, 8), :] = jnp.where(odd, other, nearest)
    shape = (G, joined.shape[0])
    line = lax.broadcasted_iota(jnp.int32, shape, 0)
    line = jnp.minimum(line, G - line)
    line = jnp.where(row >= HALF, G // 2 - line, line)
    source = 2 * CELLS_A * (line >> 5) + (line & (CELLS_A - 1))
    pitch = jnp.where(line == G // 2, 1, CELLS_A)
    source = lax.broadcasted_iota(jnp.int32, shape, 1) - source
    parts = thirds(joined[...])
    for half in range(2):
        chosen = jnp.where(source == half * pitch, 1.0, 0.0).astype(BF16)
        value = sum(dot(chosen, part) for part in parts)
        out_ref[:, pl.ds(LANES * half, LANES)] = value * (1.0 / (G * G * G))


def plane_kernel(tiles_ref, spectrum_ref, waves_ref, out_ref):
    lane = lax.broadcasted_iota(jnp.int32, (CELLS_A, LANES), 1)
    slots = [(lane >> 5) == s for s in range(4)]
    wide = lax.broadcasted_iota(jnp.int32, (CELLS_A, G), 1)
    pairs = [((wide & 31) >> 1) == line for line in range(LINES_B)]
    pieces = [
        [tiles_ref[pl.ds(96 * r + v, CELLS_A, stride=3), :] for v in range(3)] for r in range(ROWS)
    ]

    def joined(block):
        parts = []
        for w in range(2):
            value = None
            for s in range(4):
                piece = pieces[4 * w + s][block // 4]
                value = piece if value is None else jnp.where(slots[(block + s) & 3], piece, value)
            parts.append(value)
        return jnp.concatenate(parts, axis=1)

    def waves(start, count, stride=1):
        rows = [waves_ref[half, pl.ds(start, count, stride=stride), :] for half in range(2)]
        return jnp.concatenate(rows, axis=1)

    first = halves(waves(0, G))
    even = (lax.broadcasted_iota(jnp.int32, (CELLS_A, G), 0) & 1) == 0
    outer = []
    for slot in range(ROWS):
        start = CELLS_A * ((row_at(slot, LINES_B) + 1) % ROWS)
        outer.append(jnp.where(even, waves(start, 1), waves(start + 1, 1)))
    outer = halves(jnp.concatenate(outer, axis=0))
    lines = [line for group in GROUPS for line in group]
    flipped = []
    for line in lines:
        rows = waves(line % CELLS_B, COLS, CELLS_B)
        flipped.append(pltpu.roll(rows, COLS - 1, 0) if line >= CELLS_B else rows)
    flipped = jnp.concatenate([*flipped, jnp.zeros((LINES - MAIN, G), F32)], axis=0)
    second = halves(flipped.T[:, :MAIN])
    flipped = halves(flipped[:MAIN])

    def table(m):
        order = [row_at(slot, m) for slot in range(ROWS)]
        return [
            jnp.concatenate([part[CELLS_A * r : CELLS_A * (r + 1)] for r in order], axis=0)
            for part in first
        ]

    rim = joined(LINES_B)
    main = [
        halves(jnp.concatenate([joined(line) for line in group], axis=0)) for group in GROUPS
    ]
    rims = halves(jnp.concatenate([jnp.where(pairs[line], rim, 0.0) for line in lines], axis=0))
    half = jnp.concatenate([dot_table(rows, table(m)) for m, rows in enumerate(main)], axis=0)
    half = halves(half + dot_table(rims, outer))
    image = table_dot(second, half) * spectrum_ref[...]
    half = halves(table_dot(flipped, halves(image)))
    rims = dot_table(half, outer, ((1,), (1,)))
    blocks, at = {}, 0
    for m, group in enumerate(GROUPS):
        size = CELLS_A * len(group)
        rows = [part[at : at + size] for part in half]
        value = dot_table(rows, table(m), ((1,), (1,)))
        for place, line in enumerate(group):
            blocks[line] = value[CELLS_A * place : CELLS_A * (place + 1)]
        at += size
    zero = jnp.zeros((CELLS_A, G), F32)
    rim = zero
    for place, line in enumerate(lines):
        rim = jnp.where(pairs[line], rims[CELLS_A * place : CELLS_A * (place + 1)], rim)
    blocks[LINES_B], blocks[LINES_B + 1] = rim, zero
    for r in range(ROWS):
        lanes = slice(LANES * (r // 4), LANES * (r // 4 + 1))
        for v in range(3):
            value = None
            for block in range(4 * v, 4 * v + 4):
                piece = blocks[block][:, lanes]
                value = piece if value is None else jnp.where(slots[(block + r) & 3], piece, value)
            out_ref[pl.ds(96 * r + v, CELLS_A, stride=3), :] = value


def gather_tile(weights_ref, anchors_ref, place, picked, tile, base, at):
    near_masks, next_masks, groups, bits = masks_of(place)
    weights_at = pl.ds(tile * LANES, LANES)
    odd = jnp.broadcast_to((anchors_ref[2:3, weights_at] & 1) != 0, (8, LANES))
    total = jnp.zeros((8, LANES), F32)
    before = None
    for shift in range(SHIFTS):
        blocks = []
        for line in range(LINES_B):
            start = SPREAD * shift + CELLS_A * line
            rows = [picked[base, pl.ds(start + 8 * v, 8), at] for v in range(4)]
            last = picked[base, pl.ds(SPREAD * shift + MAIN + 8 * (line // 4), 8), at]
            rows.append(pltpu.roll(last, 8 - 2 * (line % 4), 0) if line % 4 else last)
            pair = []
            for skip in range(2):
                chosen = rows[skip]
                for g in range(1, 4):
                    chosen = jnp.where(groups[g], rows[g + skip], chosen)
                pair.append(chosen)
            blocks.append(pair)
        for mask, width, count in zip(bits[::-1], (4, 2, 1), (7, 5, 4)):
            fewer = []
            for line in range(count):
                low = blocks[line]
                if line + width < len(blocks):
                    high = blocks[line + width]
                    low = [jnp.where(mask, h, l) for h, l in zip(high, low)]
                fewer.append(low)
            blocks = fewer
        if shift:
            for j in range(4):
                rows = stencil_rows(weights_ref, j, shift - 1, weights_at)
                weights = two_rows(rows, near_masks, next_masks)
                for weight, high, low in zip(weights, blocks[j], before[j]):
                    total = total + weight * jnp.where(odd, high, low)
        before = blocks
    return jnp.sum(total, axis=0, keepdims=True)


def gather_kernel(
    field_ref, anchors_ref, weights_ref, table_ref, near_ref, out_ref, lines, parts, picked
):
    turned = [field_ref[pl.ds(v, G, stride=3), :].T for v in range(3)]
    turned = halves(jnp.concatenate(turned, axis=0))
    lines[...] = dot_table(turned, (table_ref[0], table_ref[1]))
    field = jnp.concatenate([lines[block_place(b), :] for b in range(LINES_B + 1)], axis=0)
    for shift in range(SHIFTS):
        value = field[:, LANES * (shift % 2) : LANES * (shift % 2 + 1)]
        high, low = halves(pltpu.roll(value, LANES - shift // 2, 1) if shift > 1 else value)
        rows = pl.ds(SPREAD * shift, SPREAD)
        parts[rows, pl.ds(0, LANES)] = high
        parts[rows, pl.ds(LANES, LANES)] = low
    hot = onehot(anchors_ref)
    hot = jnp.concatenate([hot, hot], axis=0)
    for chunk in range(TRI // CHUNK):
        columns = hot[:, CHUNK * chunk : CHUNK * (chunk + 1)]
        for first, count in ((0, 2), (2, 3)) if chunk == 0 else ((0, SHIFTS),):
            rows = pl.ds(SPREAD * first, SPREAD * count)
            picked[chunk, rows, :] = dot(parts[rows, :], columns)
        for step in range(CHUNK // LANES):
            tile = chunk * (CHUNK // LANES) + step
            at = pl.ds(tile * LANES, LANES)
            place = local_place(anchors_ref, at)
            value = gather_tile(
                weights_ref, anchors_ref, place, picked, tile, chunk, pl.ds(step * LANES, LANES)
            )
            out_ref[:, at] = value + near_ref[:, at]


def near_kernel(
    count_ref, target_ref, source_ref, before_ref, own_ref, after_ref, tiles_hbm, out_ref,
    charges_ref, total, tiles_ref, sem,
):
    size = LANES
    parts = tiles_hbm.shape[0] // PART
    copies = []
    for part in range(parts):
        at = pl.ds(PART * part, PART)
        copies.append(pltpu.make_async_copy(tiles_hbm.at[at], tiles_ref.at[at], sem.at[part]))
    for copy in copies:
        copy.start()
    total[...] = jnp.zeros_like(total)
    for place, ref in enumerate((before_ref, own_ref, after_ref)):
        charges_ref[pl.ds(24 * place, 24), :] = ref[...]

    def slot(place, carry):
        rows = pl.ds(pl.multiple_of(target_ref[place] * size, size), size)
        code = source_ref[place]
        neighbour = code >> 3
        row = neighbour // 3
        line = 24 * (neighbour - 3 * row) + 8 * row + (code & 7)
        source = charges_ref[pl.ds(line, 1), :]
        total[rows, :] = total[rows, :] + tiles_ref[place] * source
        return carry

    for part, copy in enumerate(copies):
        copy.wait()
        start = PART * part
        lax.fori_loop(start, jnp.clip(count_ref[0], start, start + PART), slot, 0)
    ones = jnp.ones((8, size), BF16)
    result = sum(dot(ones, part, ((1,), (1,))) for part in thirds(total[...]))
    out_ref[...] = result[0:1]


def shifted(value, axis, by):
    size = lax.axis_size(axis)
    return lax.ppermute(value, axis, [(i, (i + by) % size) for i in range(size)])


def near_field(beside, near_count, near_target, near_source, near_tiles):
    slots, size, _ = near_tiles.shape
    before, after = shifted(beside, "col", 1), shifted(beside, "col", -1)
    smem = pl.BlockSpec(memory_space=pltpu.SMEM)
    vmem = pl.BlockSpec(memory_space=pltpu.VMEM)
    return pl.pallas_call(
        near_kernel,
        in_specs=[smem, smem, smem, vmem, vmem, vmem, pl.BlockSpec(memory_space=pltpu.HBM)],
        out_shape=jax.ShapeDtypeStruct((1, TRI), F32),
        scratch_shapes=[
            pltpu.VMEM((80, size), F32),
            pltpu.VMEM((TRI, size), F32),
            pltpu.VMEM((slots, size, size), F32),
            pltpu.SemaphoreType.DMA((slots // PART,)),
        ],
        compiler_params=params(8),
        name="near",
    )(
        near_count,
        near_target,
        near_source,
        before,
        beside,
        after,
        pltpu.with_memory_space_constraint(near_tiles, pltpu.HBM),
    )


def swapped(value, mask):
    return lax.ppermute(value, "row", [(i, i ^ mask) for i in range(ROWS)])


def exchange(values, axes, pieces):
    shaped = values.reshape(pieces, 1, values.size // pieces)
    moved = lax.all_to_all(shaped, axes, split_axis=0, concat_axis=0, tiled=True)
    return moved.reshape(values.shape)


def local(
    charges,
    anchors,
    stencil_weights,
    kernel_spectrum,
    near_count,
    near_target,
    near_source,
    near_tiles,
):
    lines = line_table()
    table = jnp.asarray(lines)
    turned = jnp.asarray(np.concatenate([lines[:, :, 0::2], lines[:, :, 1::2]], axis=2))
    devices = ROWS * COLS
    packed = jax.ShapeDtypeStruct((devices * LINES // LANES, LANES), F32)
    hbm = pl.BlockSpec(memory_space=pltpu.HBM)
    deposited, first, *sent = pl.pallas_call(
        deposit_kernel,
        out_shape=(packed, *[jax.ShapeDtypeStruct((size, LANES), F32) for size in (24, *[SENT] * HALF)]),
        in_specs=[hbm] * 5,
        scratch_shapes=[
            pltpu.VMEM((1, TRI), F32),
            pltpu.VMEM((3, TRI), jnp.int32),
            pltpu.VMEM((64, TRI), F32),
            pltpu.VMEM((2, G, G), BF16),
            pltpu.VMEM((2, CELLS_A * CELLS_B + 8, LANES), F32),
            pltpu.VMEM((64, TRI), F32),
            pltpu.VMEM((4, 2 * SPREAD, TRI), BF16),
            pltpu.VMEM((LINES, G), F32),
            pltpu.SemaphoreType.DMA((6,)),
        ],
        compiler_params=params(20),
        name="deposit",
    )(
        *[
            pltpu.with_memory_space_constraint(value, pltpu.HBM)
            for value in (
                charges.reshape(1, TRI),
                anchors,
                stencil_weights,
                table,
                kernel_spectrum.reshape(CELLS_A * CELLS_B, G),
            )
        ]
    )
    received = exchange(deposited, BOTH, devices)
    first = swapped(first, ROWS - 1)
    joined = pl.pallas_call(
        join_kernel,
        out_shape=[jax.ShapeDtypeStruct((SENT + 8, LANES), F32)] * (HALF - 1),
        compiler_params=params(8),
        name="join",
    )(first, *sent[1:])
    joined = [swapped(value, step + 1) for step, value in enumerate(joined)]
    waves = pl.pallas_call(
        waves_kernel,
        out_shape=jax.ShapeDtypeStruct((2, G, LANES), F32),
        compiler_params=params(8),
        name="waves",
    )(first)
    spectrum, beside = pl.pallas_call(
        spectrum_kernel,
        out_shape=(
            jax.ShapeDtypeStruct((G, G), F32),
            jax.ShapeDtypeStruct((24, LANES), F32),
        ),
        scratch_shapes=[pltpu.VMEM((2 * CELLS_A * HALF + 8, LANES), F32)],
        compiler_params=params(8),
        name="spectrum",
    )(first, sent[0], *joined)
    handed = pl.pallas_call(
        plane_kernel, out_shape=packed, compiler_params=params(12), name="plane"
    )(received, spectrum, waves)
    field = exchange(handed, BOTH, devices)
    beside, _ = lax.optimization_barrier((beside, handed))
    near = near_field(beside, near_count, near_target, near_source, near_tiles)
    result = pl.pallas_call(
        gather_kernel,
        out_shape=jax.ShapeDtypeStruct((1, TRI), F32),
        scratch_shapes=[
            pltpu.VMEM((LINES, G), F32),
            pltpu.VMEM((SHIFTS * SPREAD, G), BF16),
            pltpu.VMEM((TRI // CHUNK, SHIFTS * SPREAD, CHUNK), F32),
        ],
        compiler_params=params(20),
        name="gather",
    )(field, anchors, stencil_weights, turned, near)
    return result.reshape(TRI)


def solution(mesh):
    return jax.shard_map(
        local,
        mesh=mesh,
        in_specs=(
            P(("row", "col")),
            P(None, ("row", "col")),
            P(None, ("row", "col")),
            P("row", "col", None),
            P(("row", "col")),
            P(("row", "col")),
            P(("row", "col")),
            P(("row", "col"), None, None),
        ),
        out_specs=P(("row", "col")),
        check_vma=False,
    )
```
